32 devices in a mesh: gx: 4 (over x, core), gy: 8 (over z, y).
Axes of the slice: x: 2, y: 2, z: 4, core: 2. Of those that a mesh axis runs over, the one named last changes fastest.
Arguments:
- samples: float32 [4096, 2, 128], P(('gx', 'gy')), may hold values from -6 to 6
- kernel: float32 [4096, 3, 4, 128], P(('gx', 'gy')), may hold values from 0.1 to 1
- offsets: int32 [4096, 3, 128], P(('gx', 'gy')), may hold values from 0 to 4
- owners: int32 [4096, 1], P(('gx', 'gy')), may hold values from 0 to 31; in each aligned block of 128 rows (0 to 127, 128 to 255, ...) at most 8 rows name the same one
- tile_ids: int32 [4096], P(('gx', 'gy')), may hold values from 0 to 3455
- deapod_first: float32 [192], replicated, may hold values from 1 to 3
- deapod_second: float32 [192], P('gx'), may hold values from 1 to 3
- deapod_third: float32 [192], P('gy'), may hold values from 1 to 3
Outputs:
- image: float32 [2, 192, 192, 192], P(None, 'gy', 'gx')
The draws below stay inside these ranges and needn't reach their ends.
Inputs may be any that keep to these rules, and one draw needn't show every extreme that they name: `owners`: among the 128 blocks of one device no owner is named more than 8 times, and in some device one owner is named exactly 8 times. `tile_ids`: tiles are numbered row, column, depth over the owner's 12 x 6 x 48 tiles. `offsets`: each sample's kernel lies inside its block's tile.
All inputs are finite; a program needn't handle non-finite values.
Results may differ from the reference program's by a relative error of at most 0.0003.
Values sent between devices are 32-bit elements; how exact they have to be, the bound alone decides.
No kernel may reach another device: no remote copies, remote signals or barrier semaphores. Data moves between devices by JAX's collectives and lax.ppermute only.
A program may use at most 256 MiB of HBM per device.

```python
import math
import jax
import jax.numpy as jnp
import numpy as np
from jax import lax

NX = 384
NY = 384
NZ = 384
TILE = 8
KW = 4
SPB = 128
B_DEV = 128
CAP = 8
BLOCKS = 4096
TILES_DEV = 3456
IX = 192
IY = 192
IZ = 192
N_GX = 4
N_GY = 8
DEVICES = 32


def with_ends(drawn, rng, least, largest):
    index_at = [jax.random.randint(jax.random.fold_in(rng, axis), (), 0, length) for axis, length in enumerate(drawn.shape)]
    longest = drawn.shape.index(max(drawn.shape))
    beside = index_at[:longest] + [(index_at[longest] + 1) % drawn.shape[longest]] + index_at[longest + 1:]
    return drawn.at[tuple(index_at)].set(least).at[tuple(beside)].set(largest)


def block_levels(own_key, extent, cuts, smallest, top_value):
    factor_of = 1.0
    for dim, blocks in cuts:
        draws = jax.random.uniform(jax.random.fold_in(jax.random.fold_in(own_key, 6), dim), (blocks,), jnp.float32, smallest / len(cuts), top_value / len(cuts))
        factor_of = factor_of * jnp.repeat(jnp.exp(draws), extent[dim] // blocks).reshape((-1,) + (1,) * (len(extent) - 1 - dim))
    return factor_of


def routed_block(key, own, number, rows, count, top, most, lean):
    order = jax.random.permutation(key, count)
    crowded, common = portions_of(count, rows * top, most, lean, True), portions_of(count, rows * top, most, lean, False)
    places = jnp.arange(count)

    def named(tallies, offset_by):
        used = int((tallies > 0).sum())
        fixed = max(1, used // 4)
        moved = fixed + (places - fixed + offset_by * (used - fixed)) % max(1, count - fixed)
        return jnp.zeros((count,), jnp.int32).at[order[jnp.where(places < fixed, places, moved)]].set(jnp.asarray(tallies, jnp.int32))

    tallies = jnp.where(number % 4 == 0, named(crowded, number // 4), named(common, number - number // 4 - 1))
    mixed = jax.random.permutation(jax.random.fold_in(own, 3), count)
    source_of, sink = mixed[0:count // 2 * 2:2], mixed[1:count // 2 * 2:2]
    margin = jnp.minimum(tallies[source_of] - 1, most - tallies[sink]) // 2
    margin = jnp.where((source_of == order[0]) | (sink == order[0]) | (tallies[sink] == 0), 0, jnp.maximum(margin, 0))
    moved = jax.random.randint(jax.random.fold_in(own, 4), (count // 2,), 0, 1 << 20) % (margin + 1)
    tallies = tallies.at[source_of].add(-moved).at[sink].add(moved)
    members = jnp.searchsorted(jnp.cumsum(tallies), jnp.arange(rows * top), side="right").astype(jnp.int32)
    listing = members.reshape(top, rows).T
    listing = listing[jax.random.permutation(jax.random.fold_in(own, 1), rows)]
    offset_by = jax.random.randint(jax.random.fold_in(own, 2), (rows, 1), 0, top)
    return jnp.take_along_axis(listing, (jnp.arange(top)[None, :] + offset_by) % top, axis=1)


def portions_of(amount, total, limit, lean, full):
    weights = [(1 << 20) // math.isqrt(grade ** lean) + 1 for grade in range(1, amount + 1)]
    largest = limit if full else min(limit, max(-(-total // amount), total * weights[0] // sum(weights)))
    least = 1 if total - largest >= amount - 1 else 0
    holding, rest = [largest] + [least] * (amount - 1), total - largest - least * (amount - 1)
    while rest > 0:
        free = [i for i in range(1, amount) if holding[i] < largest] or [i for i in range(1, amount) if holding[i] < limit]
        whole, left = sum([weights[i] for i in free]), rest
        for i in free:
            addition = min(limit - holding[i], max(1, left * weights[i] // whole), rest)
            holding[i] = holding[i] + addition
            rest = rest - addition
    return np.array(holding)


def normal_values(stream_key, shape, scale, reach, split=(), held_as=jnp.bfloat16):
    entries = jax.random.normal(stream_key, shape, jnp.float32) * scale
    if len(split) > 0:
        entries = block_levels(stream_key, shape, split, -0.22, 0.18) * entries
    return jnp.clip(entries, min=-reach, max=reach).astype(held_as)


def setup_inputs(seed: int = 0) -> dict:
    key_of = jax.random.split(jax.random.key(seed), 9)
    samples = normal_values(key_of[0], (BLOCKS, 2, SPB), 1.0, 6.0, ((0, 32),), jnp.float32)
    kernel = jnp.clip(jnp.exp(math.log(1.0) - 2.3025851 * jax.random.uniform(key_of[1], (BLOCKS, 3, KW, SPB), jnp.float32) ** block_levels(key_of[1], (BLOCKS, 3, KW, SPB), ((0, 32),), -0.2, 0.2)), 0.1, 1.0)
    offsets = with_ends(jax.random.randint(key_of[2], (BLOCKS, 3, SPB), 0, TILE - KW + 1), jax.random.fold_in(key_of[2], 1), 0, TILE - KW).astype(jnp.int32)
    owners_keys = jax.random.split(jax.random.fold_in(key_of[3], 1), BLOCKS // B_DEV)
    owners_turns = jax.random.permutation(jax.random.fold_in(key_of[3], 3), BLOCKS // B_DEV)
    owners = jax.vmap(lambda own, number: routed_block(jax.random.fold_in(key_of[3], 2), own, number, B_DEV, DEVICES, 1, CAP, 2))(owners_keys, owners_turns).reshape((BLOCKS, 1))
    tile_ids = with_ends(jax.random.randint(key_of[4], (BLOCKS,), 0, TILES_DEV), jax.random.fold_in(key_of[4], 1), 0, TILES_DEV - 1).astype(jnp.int32)
    deapod_first = jnp.clip(jnp.exp(jax.random.uniform(key_of[5], (IX,), jnp.float32, math.log(1.0), math.log(3.0))), 1.0, 3.0)
    deapod_second = jnp.clip(jnp.exp(math.log(3.0) - 1.0986123 * jax.random.uniform(key_of[6], (IY,), jnp.float32) ** block_levels(key_of[6], (IY,), ((0, 4),), -0.2, 0.2)), 1.0, 3.0)
    deapod_third = jnp.clip(jnp.exp(math.log(3.0) - 1.0986123 * jax.random.uniform(key_of[7], (IZ,), jnp.float32) ** block_levels(key_of[7], (IZ,), ((0, 8),), -0.2, 0.2)), 1.0, 3.0)
    return {"samples": samples, "kernel": kernel, "offsets": offsets, "owners": owners, "tile_ids": tile_ids, "deapod_first": deapod_first, "deapod_second": deapod_second, "deapod_third": deapod_third}


def fourier_table(length, outputs):
    freq = jnp.arange(length, dtype=jnp.int32) - length // 2
    image_pos = jnp.arange(outputs, dtype=jnp.int32) - outputs // 2
    phase_steps = jnp.mod(freq[:, None] * image_pos[None, :], length)
    phases = phase_steps.astype(jnp.float32) * (2.0 * math.pi / length)
    norming = 1.0 / math.sqrt(length)
    return (jnp.cos(phases) * norming, jnp.sin(phases) * norming)

def complex_apply(real_part, imag_part, cos_table, sin_table, pattern):
    highest = lax.Precision.HIGHEST
    real_cos = jnp.einsum(pattern, real_part, cos_table, precision=highest)
    real_sin = jnp.einsum(pattern, real_part, sin_table, precision=highest)
    imag_cos = jnp.einsum(pattern, imag_part, cos_table, precision=highest)
    imag_sin = jnp.einsum(pattern, imag_part, sin_table, precision=highest)
    return jnp.stack((real_cos - imag_sin, real_sin + imag_cos))

def spread(values, kernel, starts, tile_width):
    kernel_taps = jnp.arange(kernel.shape[2], dtype=jnp.float32)
    cell_axis = jnp.arange(tile_width, dtype=jnp.float32)
    matches = (cell_axis[None, None, :, None, None] == starts[:, :, None, None, :] + kernel_taps[None, None, None, :, None]).astype(jnp.float32)
    placed = lax.optimization_barrier(jnp.sum(matches * kernel[:, :, None, :, :], axis=3))
    plane_weight = placed[:, 0][:, :, None, :] * placed[:, 1][:, None, :, :]
    depth_weight = values[:, :, None, :] * placed[:, 2][:, None, :, :]
    return jnp.einsum('nijs,ncls->ncijl', plane_weight, depth_weight, precision=lax.Precision.HIGHEST)

def reference(samples, kernel, offsets, owners, tile_ids, deapod_first, deapod_second, deapod_third):
    device_count = N_GX * N_GY
    per_device = samples.shape[0] // device_count
    block_width = samples.shape[2]
    kernel_taps = kernel.shape[2]

    def spread_group(operands):
        return spread(operands[0], operands[1], operands[2], TILE)
    pieces = lax.map(spread_group, (samples.reshape(device_count, per_device, 2, block_width), kernel.reshape(device_count, per_device, 3, kernel_taps, block_width), offsets.astype(jnp.float32).reshape(device_count, per_device, 3, block_width)))
    pieces = pieces.reshape(-1, 2, TILE, TILE, TILE)
    tile_rows = NX // (TILE * N_GX)
    tile_cols = NY // (TILE * N_GY)
    tile_depth = NZ // TILE
    target = owners[:, 0]
    global_row = target // N_GY * tile_rows + tile_ids // (tile_cols * tile_depth)
    global_col = target % N_GY * tile_cols + tile_ids // tile_depth % tile_cols
    slab_slot = global_col * tile_depth + tile_ids % tile_depth
    slab_tiles = NY // TILE * tile_depth
    cos_z, sin_z = fourier_table(NZ, NZ // 2)
    cos_y, sin_y = fourier_table(NY, NY // 2)
    cos_x, sin_x = fourier_table(NX, NX // 2)

    def add_row(accumulated, tile_row):
        chosen = jnp.where(global_row == tile_row, slab_slot, slab_tiles)
        slab = jnp.zeros((slab_tiles, 2, TILE, TILE, TILE), jnp.float32).at[chosen].add(pieces, mode='drop')
        slab = slab.reshape(NY // TILE, tile_depth, 2, TILE, TILE, TILE).transpose(2, 3, 0, 4, 1, 5).reshape(2, TILE, NY, NZ)
        along_z = complex_apply(slab[0], slab[1], cos_z, sin_z, 'xyk,km->xym')
        along_y = complex_apply(along_z[0], along_z[1], cos_y, sin_y, 'xym,yq->xqm')
        rows_cos = lax.dynamic_slice_in_dim(cos_x, tile_row * TILE, TILE, 0)
        rows_sin = lax.dynamic_slice_in_dim(sin_x, tile_row * TILE, TILE, 0)
        along_x = complex_apply(along_y[0], along_y[1], rows_cos, rows_sin, 'xqm,xp->mqp')
        return (accumulated + along_x, None)
    start = jnp.zeros((2, NZ // 2, NY // 2, NX // 2), jnp.float32)
    accumulated, _ = lax.scan(add_row, start, jnp.arange(NX // TILE, dtype=jnp.int32))
    return accumulated * deapod_third[None, :, None, None] * deapod_second[None, None, :, None] * deapod_first[None, None, None, :]
```

```python
import functools
import math

import jax
import jax.numpy as jnp
import ml_dtypes
import numpy as np
from jax import lax
from jax.experimental import pallas as pl
from jax.experimental.pallas import tpu as pltpu
from jax.sharding import PartitionSpec as P

NX = 384
NY = 384
NZ = 384
TILE = 8
LANES = 128
PLANES = 32
PHASES = 128
BF16 = jnp.bfloat16
F32 = jnp.float32
VMEM_LIMIT = 60 * 1024 * 1024


def halves(array):
    high = array.astype(ml_dtypes.bfloat16)
    low = (array - high.astype(np.float64)).astype(ml_dtypes.bfloat16)
    return high, low


def split(value):
    high = value.astype(BF16)
    return high, (value - high.astype(F32)).astype(BF16)


def waves(freq, position, length):
    steps = np.mod(freq[:, None] * position[None, :], length)
    phase = 2.0 * math.pi * steps / length
    return np.cos(phase), np.sin(phase)


def depth_tables(planes):
    matrices, phases = [], []
    lane_part = np.arange(LANES) // 64
    lane_odd = np.arange(LANES) // 32 % 2
    lane_plane = np.arange(LANES) % 32
    used = (lane_plane < planes).astype(np.float64)
    for index in range(NZ // 2 // planes):
        position = index * planes + lane_plane - NZ // 4
        cos, sin = waves(np.arange(TILE) - NZ // 2, position, NZ)
        cos, sin = cos * used / math.sqrt(NZ), sin * used / math.sqrt(NZ)
        real = np.where(lane_part == 0, cos, sin)
        imag = np.where(lane_part == 0, -sin, cos)
        plain = np.concatenate((real, imag))
        turned = np.concatenate((-np.where(lane_part == 0, sin, -cos), -np.where(lane_part == 0, cos, sin)))
        high, low = halves(np.concatenate((plain, turned), axis=1))
        matrices.append(np.concatenate((high, high, low), axis=0))
        cos, sin = waves(np.arange(NZ // TILE), position, NZ // TILE)
        sign = np.where(lane_odd == 1, -1.0, 1.0)[None, :]
        phases.append(np.stack((np.concatenate((cos, cos * sign)), np.concatenate((sin, sin * sign)))))
    return np.stack(matrices), np.stack(phases).astype(np.float32)


def column_tables(chunks):
    half = NY // 2
    out = []
    for chunk in range(chunks):
        rows = half // chunks
        parts = []
        for parity in range(2):
            position = chunk * rows + 2 * np.arange(rows // 2) + parity - NY // 4
            cos, sin = waves(position, np.arange(half) - half, NY)
            high, low = halves(np.concatenate((cos, sin)) / math.sqrt(NY))
            parts.append(np.concatenate((high, high, low), axis=1))
        out.append(np.stack(parts))
    return np.stack(out)


def row_tables():
    half = NX // 2
    quarter = NX // 4
    out = []
    for parity in range(2):
        position = 2 * np.arange(quarter) + parity - NX // 4
        cos, sin = waves(np.arange(half) - half, position, NX)
        table = np.zeros((half, 2 * LANES))
        lanes = (np.arange(quarter) + parity * quarter) % LANES
        table[:, lanes] = cos / math.sqrt(NX)
        table[:, LANES + lanes] = sin / math.sqrt(NX)
        out.append(np.stack(halves(table)))
    return np.stack(out)


def order_tables():
    first = np.zeros((LANES, NX // 2))
    second = np.zeros((LANES, NX // 2))
    quarter = NX // 4
    for m1 in range(NX // 2):
        place = m1 // 2 + m1 % 2 * quarter
        if place < LANES:
            first[place, m1] = 1.0
        else:
            second[place - LANES, m1] = 1.0
    return np.concatenate((first, first, second, second)).astype(ml_dtypes.bfloat16)


def spread_kernel(samples_ref, kernel_ref, offsets_ref, codes_ref, out_ref):
    blocks = samples_ref.shape[0]
    taps = kernel_ref.shape[2]
    cell = lax.broadcasted_iota(jnp.int32, (TILE, LANES), 0)
    left = lax.broadcasted_iota(jnp.int32, (2 * TILE, LANES), 1) < LANES // 2

    def weights(block):
        placed = []
        for dim in range(3):
            shifted = cell - offsets_ref[block, pl.ds(dim, 1), :]
            value = jnp.zeros((TILE, LANES), F32)
            for tap in range(taps):
                value = jnp.where(shifted == tap, kernel_ref[block, dim, pl.ds(tap, 1), :], value)
            placed.append(value)
        plane = jnp.concatenate([placed[0][i : i + 1] * placed[1] for i in range(TILE)], axis=0)
        depth = jnp.concatenate([samples_ref[block, pl.ds(c, 1), :] * placed[2] for c in range(2)], axis=0)
        return depth, plane

    def pair_body(pair, carry):
        depth_a, plane_a = weights(2 * pair)
        depth_b, plane_b = weights(2 * pair + 1)
        depth_high, depth_low = split(jnp.concatenate((depth_a, depth_b), axis=0))
        plane_high, plane_low = split(jnp.concatenate((plane_a, plane_b), axis=0))
        piece = lax.dot_general(
            jnp.concatenate((depth_high, depth_low, depth_high), axis=1),
            jnp.concatenate((plane_high, plane_high, plane_low), axis=1),
            (((1,), (1,)), ((), ())),
            preferred_element_type=F32,
        )
        out_ref[pair] = jnp.where(left, piece[: 2 * TILE], piece[2 * TILE :])
        return carry

    lax.fori_loop(0, blocks // 2, pair_body, 0, unroll=2)
    out_ref[blocks // 2] = jnp.broadcast_to(codes_ref[...], (2 * TILE, LANES))


def transform_kernel(
    group, planes_padded, place_ref, codes_ref, tiles_ref, depth_ref, phases_ref, column_ref, row_ref, keep_ref, send_ref, acc_ref
):
    half = NX // 2
    stride = NY
    sources = tiles_ref.shape[0]
    pairs = tiles_ref.shape[1] - 1
    kept = column_ref.shape[1]
    per_device = kept // group
    slots = per_device // 2

    def clear(step, carry):
        acc_ref[pl.ds(pl.multiple_of(step * stride, stride), stride), :] = jnp.zeros((stride, LANES), F32)
        return carry

    lax.fori_loop(0, half, clear, 0)

    def add_source(source, carry):
        def add_pair(pair, inner):
            high, low = split(tiles_ref[source, pair])
            spectrum = lax.dot_general(
                jnp.concatenate((high, low, high), axis=0),
                depth_ref[...],
                (((0,), (0,)), ((), ())),
                preferred_element_type=F32,
            )
            for side in range(2):
                code = codes_ref[source * 2 * pairs + 2 * pair + side]
                base = lax.shift_right_logical(code, 7)
                phase = jnp.bitwise_and(code, PHASES - 1)
                cos = phases_ref[0, pl.ds(phase, 1), :]
                sin = phases_ref[1, pl.ds(phase, 1), :]
                for i in range(TILE):
                    row = side * TILE * TILE + i * TILE
                    value = spectrum[row : row + TILE, :LANES] * cos + spectrum[row : row + TILE, LANES:] * sin
                    at = pl.ds(pl.multiple_of(base * TILE + i * stride, TILE), TILE)
                    acc_ref[at, :] = acc_ref[at, :] + value
            return inner

        lax.fori_loop(0, pairs, add_pair, 0, unroll=2)
        return carry

    lax.fori_loop(0, sources, add_source, 0)

    turn = jnp.where(lax.broadcasted_iota(jnp.int32, (kept // 2, LANES), 1) < LANES // 2, -1.0, 1.0)

    def columns(step, carry):
        folded = ([], [])
        for side in range(2):
            start = pl.multiple_of((2 * step + side) * stride, stride)
            lower = acc_ref[pl.ds(start, NY // 2), :]
            upper = acc_ref[pl.ds(start + NY // 2, NY // 2), :]
            folded[0].append(lower + upper)
            folded[1].append(lower - upper)
        for parity in range(2):
            high, low = split(jnp.concatenate(folded[parity], axis=1))
            product = jnp.dot(
                column_ref[parity], jnp.concatenate((high, low, high), axis=0), preferred_element_type=F32
            )
            for side in range(2):
                start = pl.multiple_of((2 * step + side) * stride, stride)
                lanes = slice(side * LANES, (side + 1) * LANES)
                acc_ref[pl.ds(start + parity * (kept // 2), kept // 2), :] = (
                    product[: kept // 2, lanes] + pltpu.roll(product[kept // 2 :, lanes], LANES // 2, 1) * turn
                )
        return carry

    lax.fori_loop(0, half // 2, columns, 0)

    member = jnp.bitwise_and(place_ref[0], group - 1)
    lane = lax.broadcasted_iota(jnp.int32, (PLANES, LANES), 1)

    for relative in range(group):
        target = send_ref if relative % 2 else keep_ref
        first = jnp.bitwise_xor(member, relative) * per_device

        def rows(slot, carry):
            turned = []
            for side in range(2):
                m2 = first + slot + side * slots
                row = jnp.bitwise_and(m2, 1) * (kept // 2) + lax.shift_right_logical(m2, 1)
                turned.append(acc_ref[pl.ds(row, half, stride=stride), :].T)
            parts = []
            for parity in range(2):
                at = parity * PLANES
                stacked = [
                    value[part * 64 + at : part * 64 + at + PLANES] for value in turned for part in range(2)
                ]
                high, low = split(jnp.concatenate(stacked, axis=0))
                both = jnp.dot(
                    jnp.concatenate((high, low), axis=0), row_ref[parity, 0], preferred_element_type=F32
                )
                product = (
                    both[: 4 * PLANES]
                    + both[4 * PLANES :]
                    + jnp.dot(high, row_ref[parity, 1], preferred_element_type=F32)
                )
                sides = []
                for side in range(2):
                    real = product[2 * side * PLANES : (2 * side + 1) * PLANES]
                    imag = product[(2 * side + 1) * PLANES : (2 * side + 2) * PLANES]
                    sides.append(
                        (real[:, :LANES] - imag[:, LANES:], real[:, LANES:] + imag[:, :LANES])
                    )
                parts.append(sides)
            for part in range(2):
                even = [parts[0][side][part] for side in range(2)]
                odd = [parts[1][side][part] for side in range(2)]
                values = [jnp.where(lane < NX // 4, even[side], odd[side]) for side in range(2)]
                values.append(jnp.where(lane < LANES // 2, odd[0], pltpu.roll(odd[1], LANES // 2, 1)))
                for number, value in enumerate(values):
                    target[relative // 2, slot, number, pl.ds(part * planes_padded, planes_padded), :] = value[
                        :planes_padded
                    ]
            return carry

        lax.fori_loop(0, slots, rows, 0)


def finish_kernel(slots, planes, planes_padded, parts, refs):
    part_refs = refs[:parts]
    order_ref, first_ref, second_ref, third_ref, out_ref = refs[parts:]
    first = first_ref[...]
    second = second_ref[...]

    def plane_body(plane, carry):
        for part in range(2):
            values = []
            for number in range(3):
                at = pl.ds(number * 2 * planes_padded + part * planes_padded + plane, slots, stride=6 * planes_padded)
                total = part_refs[0][at, :]
                for ref in part_refs[1:]:
                    total = total + ref[at, :]
                values.append(total)
            main = jnp.concatenate(values[:2], axis=0)
            rest = jnp.concatenate((values[2], pltpu.roll(values[2], LANES // 2, 1)), axis=0)
            ordered = jnp.dot(
                jnp.concatenate(split(main) + split(rest), axis=1), order_ref[...], preferred_element_type=F32
            )
            out_ref[part, plane] = ordered * (second * third_ref[plane]) * first
        return carry

    lax.fori_loop(0, planes, plane_body, 0)


def on_device(samples, kernel, offsets, owners, tile_ids, deapod_first, deapod_second, deapod_third):
    grid_rows = lax.axis_size("gx")
    grid_cols = lax.axis_size("gy")
    blocks = samples.shape[0]
    block_width = samples.shape[2]
    assert block_width == LANES and blocks <= LANES
    tile_rows = NX // (TILE * grid_rows)
    tile_cols = NY // (TILE * grid_cols)
    tile_depth = NZ // TILE
    planes = deapod_third.shape[0]
    per_device = deapod_second.shape[0]
    slots = per_device // 2
    planes_padded = -(-planes // 8) * 8
    vmem = pl.BlockSpec(memory_space=pltpu.VMEM)
    smem = pl.BlockSpec(memory_space=pltpu.SMEM)
    params = pltpu.CompilerParams(vmem_limit_bytes=VMEM_LIMIT)

    owner = owners[:, 0]
    row = owner // grid_cols * tile_rows + tile_ids // (tile_cols * tile_depth)
    col = owner % grid_cols * tile_cols + tile_ids // tile_depth % tile_cols
    folds = NX // TILE // 2
    base = row % folds * (TILE * NY // TILE) + col
    phase = tile_ids % tile_depth + row // folds * tile_depth
    codes = (base * PHASES + phase).astype(F32)
    codes = jnp.pad(codes, (0, LANES - blocks))[None, :]

    tiles = pl.pallas_call(
        spread_kernel,
        out_shape=jax.ShapeDtypeStruct((blocks // 2 + 1, 2 * TILE, LANES), F32),
        in_specs=[vmem] * 4,
        out_specs=vmem,
        compiler_params=params,
        name="spread",
    )(samples, kernel, offsets, codes)

    gathered = lax.all_gather(tiles, "gy", axis=0, tiled=False)
    tile_codes = gathered[:, blocks // 2, 0, :blocks].astype(jnp.int32).reshape(-1)

    gx = lax.axis_index("gx").astype(jnp.int32)
    gy = lax.axis_index("gy")
    group = grid_rows
    matrices, phases = depth_tables(planes)
    matrix = lax.dynamic_index_in_dim(jnp.asarray(matrices), gy, 0, keepdims=False)
    phase_rows = lax.dynamic_index_in_dim(jnp.asarray(phases), gy, 0, keepdims=False)
    column = jnp.asarray(column_tables(grid_rows // group)[0])
    shape = jax.ShapeDtypeStruct((group // 2, slots, 3, 2 * planes_padded, LANES), F32)
    keep, send = pl.pallas_call(
        functools.partial(transform_kernel, group, planes_padded),
        out_shape=(shape, shape),
        in_specs=[smem, smem] + [vmem] * 5,
        out_specs=(vmem, vmem),
        scratch_shapes=[pltpu.VMEM((NX // 2 * NY, LANES), F32)],
        compiler_params=params,
        name="transform",
    )(gx.reshape(1), tile_codes, gathered, matrix, phase_rows, column, jnp.asarray(row_tables()))

    parts = [[keep[index] for index in range(group // 2)]]
    sent = [send[index] for index in range(group // 2)]
    bit = 1
    while True:
        swap = [(index, index ^ bit) for index in range(grid_rows)]
        arrived = [lax.ppermute(value, "gx", swap) for value in sent]
        parts.append(arrived)
        bit *= 2
        if bit == group:
            break
        width = len(parts[0])
        sent = [sum(layer[index] for layer in parts) for index in range(1, width, 2)]
        parts = [[layer[index] for index in range(0, width, 2)] for layer in parts]
    finals = [layer[0].reshape(slots * 6 * planes_padded, LANES) for layer in parts]

    def finish(*refs):
        finish_kernel(slots, planes, planes_padded, len(finals), refs)

    return pl.pallas_call(
        finish,
        out_shape=jax.ShapeDtypeStruct((2, planes, per_device, NX // 2), F32),
        in_specs=[vmem] * (len(finals) + 3) + [smem],
        out_specs=vmem,
        compiler_params=params,
        name="finish",
    )(*finals, jnp.asarray(order_tables()), deapod_first[None, :], deapod_second[:, None], deapod_third)


def solution(mesh):
    in_specs = (
        P(("gx", "gy"), None, None),
        P(("gx", "gy"), None, None, None),
        P(("gx", "gy"), None, None),
        P(("gx", "gy"), None),
        P(("gx", "gy")),
        P(),
        P("gx"),
        P("gy"),
    )
    out_specs = P(None, "gy", "gx", None)
    return jax.shard_map(
        on_device, mesh=mesh, in_specs=in_specs, out_specs=out_specs, check_vma=False
    )
```

```python
import functools
import math

import jax
import jax.numpy as jnp
import ml_dtypes
import numpy as np
from jax import lax
from jax.experimental import pallas as pl
from jax.experimental.pallas import tpu as pltpu
from jax.sharding import PartitionSpec as P

NX = 384
NY = 384
NZ = 384
TILE = 8
LANES = 128
PLANES = 32
PHASES = 128
BF16 = jnp.bfloat16
F32 = jnp.float32
VMEM_LIMIT = 60 * 1024 * 1024


def halves(array):
    high = array.astype(ml_dtypes.bfloat16)
    low = (array - high.astype(np.float64)).astype(ml_dtypes.bfloat16)
    return high, low


def split(value):
    high = value.astype(BF16)
    return high, (value - high.astype(F32)).astype(BF16)


def waves(freq, position, length):
    steps = np.mod(freq[:, None] * position[None, :], length)
    phase = 2.0 * math.pi * steps / length
    return np.cos(phase), np.sin(phase)


def depth_tables(planes):
    matrices, phases = [], []
    lane_part = np.arange(LANES) // 64
    lane_odd = np.arange(LANES) // 32 % 2
    lane_plane = np.arange(LANES) % 32
    used = (lane_plane < planes).astype(np.float64)
    for index in range(NZ // 2 // planes):
        position = index * planes + lane_plane - NZ // 4
        cos, sin = waves(np.arange(TILE) - NZ // 2, position, NZ)
        cos, sin = cos * used / math.sqrt(NZ), sin * used / math.sqrt(NZ)
        real = np.where(lane_part == 0, cos, sin)
        imag = np.where(lane_part == 0, -sin, cos)
        plain = np.concatenate((real, imag))
        turned = np.concatenate((-np.where(lane_part == 0, sin, -cos), -np.where(lane_part == 0, cos, sin)))
        high, low = halves(np.concatenate((plain, turned), axis=1))
        matrices.append(np.concatenate((high, high, low), axis=0))
        cos, sin = waves(np.arange(NZ // TILE), position, NZ // TILE)
        sign = np.where(lane_odd == 1, -1.0, 1.0)[None, :]
        phases.append(np.stack((np.concatenate((cos, cos * sign)), np.concatenate((sin, sin * sign)))))
    return np.stack(matrices), np.stack(phases).astype(np.float32)


def padded_rows(per_device):
    return -(-(per_device // 2) // TILE) * TILE


def column_tables(devices, per_device):
    half = NY // 2
    rows = padded_rows(per_device)
    place = np.arange(rows)
    slot = place // 8 * 4 + place % 4
    local = 2 * slot + place % 8 // 4 * (per_device // 2)
    used = (slot < per_device // 4).astype(np.float64)[:, None]
    out = []
    for parity in range(2):
        cos_parts, sin_parts = [], []
        for device in range(devices):
            cos, sin = waves(device * per_device + local + parity - NY // 4, np.arange(half) - half, NY)
            cos_parts.append(cos * used)
            sin_parts.append(sin * used)
        out.append(np.concatenate(halves(np.concatenate(cos_parts + sin_parts) / math.sqrt(NY))))
    return np.stack(out)


def row_tables():
    half = NX // 2
    quarter = NX // 4
    out = []
    for parity in range(2):
        position = 2 * np.arange(quarter) + parity - NX // 4
        cos, sin = waves(np.arange(half) - half, position, NX)
        table = np.zeros((half, 2 * LANES))
        lanes = (np.arange(quarter) + parity * quarter) % LANES
        table[:, lanes] = cos / math.sqrt(NX)
        table[:, LANES + lanes] = sin / math.sqrt(NX)
        out.append(np.stack(halves(table)))
    return np.stack(out)


def order_tables():
    first = np.zeros((LANES, NX // 2))
    second = np.zeros((LANES, NX // 2))
    quarter = NX // 4
    for m1 in range(NX // 2):
        place = m1 // 2 + m1 % 2 * quarter
        if place < LANES:
            first[place, m1] = 1.0
        else:
            second[place - LANES, m1] = 1.0
    return np.concatenate((first, first, second, second)).astype(ml_dtypes.bfloat16)


def spread_kernel(samples_ref, kernel_ref, offsets_ref, codes_ref, out_ref):
    blocks = samples_ref.shape[0]
    taps = kernel_ref.shape[2]
    cell = lax.broadcasted_iota(jnp.int32, (TILE, LANES), 0)
    left = lax.broadcasted_iota(jnp.int32, (2 * TILE, LANES), 1) < LANES // 2

    def weights(block):
        placed = []
        for dim in range(3):
            shifted = cell - offsets_ref[block, pl.ds(dim, 1), :]
            value = jnp.zeros((TILE, LANES), F32)
            for tap in range(taps):
                value = jnp.where(shifted == tap, kernel_ref[block, dim, pl.ds(tap, 1), :], value)
            placed.append(value)
        plane = jnp.concatenate([placed[0][i : i + 1] * placed[1] for i in range(TILE)], axis=0)
        depth = jnp.concatenate([samples_ref[block, pl.ds(c, 1), :] * placed[2] for c in range(2)], axis=0)
        return depth, plane

    def pair_body(pair, carry):
        depth_a, plane_a = weights(2 * pair)
        depth_b, plane_b = weights(2 * pair + 1)
        depth_high, depth_low = split(jnp.concatenate((depth_a, depth_b), axis=0))
        plane_high, plane_low = split(jnp.concatenate((plane_a, plane_b), axis=0))
        piece = lax.dot_general(
            jnp.concatenate((depth_high, depth_low, depth_high), axis=1),
            jnp.concatenate((plane_high, plane_high, plane_low), axis=1),
            (((1,), (1,)), ((), ())),
            preferred_element_type=F32,
        )
        out_ref[pair] = jnp.where(left, piece[: 2 * TILE], piece[2 * TILE :])
        return carry

    lax.fori_loop(0, blocks // 2, pair_body, 0, unroll=2)
    out_ref[blocks // 2] = jnp.broadcast_to(codes_ref[...], (2 * TILE, LANES))


def tiles_kernel(codes_ref, tiles_ref, depth_ref, phases_ref, column_ref, out_ref, acc_ref, even_ref, odd_ref):
    half = NX // 2
    stride = NY
    sources = tiles_ref.shape[0]
    pairs = tiles_ref.shape[1] - 1
    batch = 8
    assert pairs % (2 * batch) == 0
    batches = pairs // batch
    rows = column_ref.shape[1] // 4
    width = out_ref.shape[0]

    def spectrum(source, number, to_ref):
        tiles = jnp.concatenate([tiles_ref[source, number * batch + index] for index in range(batch)], axis=1)
        high, low = split(tiles)
        to_ref[...] = lax.dot_general(
            jnp.concatenate((high, low, high), axis=0),
            depth_ref[...],
            (((0,), (0,)), ((), ())),
            preferred_element_type=F32,
        )

    def accumulate(source, number, from_ref):
        for tile in range(2 * batch):
            code = codes_ref[(source * batches + number) * 2 * batch + tile]
            base = lax.shift_right_logical(code, 7)
            phase = jnp.bitwise_and(code, PHASES - 1)
            cos = phases_ref[0, pl.ds(phase, 1), :]
            sin = phases_ref[1, pl.ds(phase, 1), :]
            for i in range(TILE):
                row = tile * TILE * TILE + i * TILE
                value = from_ref[row : row + TILE, :LANES] * cos + from_ref[row : row + TILE, LANES:] * sin
                at = pl.ds(pl.multiple_of(base * TILE + i * stride, TILE), TILE)
                acc_ref[at, :] = acc_ref[at, :] + value

    @pl.when(pl.program_id(0) == 0)
    def _():
        def clear(step, carry):
            acc_ref[pl.ds(pl.multiple_of(step * stride, stride), stride), :] = jnp.zeros((stride, LANES), F32)
            return carry

        lax.fori_loop(0, half, clear, 0)
        spectrum(0, 0, even_ref)

        def add_pair(step, carry):
            first = 2 * step
            source, number = first // batches, first % batches
            spectrum(source, number + 1, odd_ref)
            accumulate(source, number, even_ref)
            later = jnp.minimum(first + 2, sources * batches - 2)
            spectrum(later // batches, later % batches, even_ref)
            accumulate(source, number + 1, odd_ref)
            return carry

        lax.fori_loop(0, sources * batches // 2, add_pair, 0)

    turn = jnp.where(lax.broadcasted_iota(jnp.int32, (rows, LANES), 1) < LANES // 2, -1.0, 1.0)
    origin = pl.program_id(0) * width

    def columns(step, carry):
        folded = ([], [])
        for side in range(2):
            start = pl.multiple_of((origin + 2 * step + side) * stride, stride)
            lower = acc_ref[pl.ds(start, NY // 2), :]
            upper = acc_ref[pl.ds(start + NY // 2, NY // 2), :]
            folded[0].append(lower + upper)
            folded[1].append(lower - upper)
        for parity in range(2):
            high, low = split(jnp.concatenate(folded[parity], axis=1))
            both = jnp.dot(column_ref[parity], high, preferred_element_type=F32)
            rest = jnp.dot(column_ref[parity, : 2 * rows], low, preferred_element_type=F32)
            product = both[: 2 * rows] + both[2 * rows :] + rest
            for side in range(2):
                lanes = slice(side * LANES, (side + 1) * LANES)
                out_ref[2 * step + side, parity * rows : (parity + 1) * rows, :] = (
                    product[:rows, lanes] + pltpu.roll(product[rows:, lanes], LANES // 2, 1) * turn
                )
        return carry

    lax.fori_loop(0, width // 2, columns, 0, unroll=2)


def rows_kernel(planes_padded, place_ref, in_ref, row_ref, out_ref):
    half = NX // 2
    parity = pl.program_id(1)
    lane = lax.broadcasted_iota(jnp.int32, (PLANES, LANES), 1)
    flat = in_ref.reshape(half * TILE, LANES)
    turned = [flat[pl.ds(row, half, stride=TILE), :].T for row in range(TILE)]
    parts = []
    for odd in range(2):
        at = odd * PLANES
        stacked = [value[part * 64 + at : part * 64 + at + PLANES] for value in turned for part in range(2)]
        high, low = split(jnp.concatenate(stacked, axis=0))
        count = high.shape[0]
        both = jnp.dot(jnp.concatenate((high, low), axis=0), row_ref[odd, 0], preferred_element_type=F32)
        product = both[:count] + both[count:] + jnp.dot(high, row_ref[odd, 1], preferred_element_type=F32)
        sides = []
        for row in range(TILE):
            real = product[2 * row * PLANES : (2 * row + 1) * PLANES]
            imag = product[(2 * row + 1) * PLANES : (2 * row + 2) * PLANES]
            sides.append((real[:, :LANES] - imag[:, LANES:], real[:, LANES:] + imag[:, :LANES]))
        parts.append(sides)
    for slot in range(TILE // 2):
        for part in range(2):
            even = [parts[0][slot + side * TILE // 2][part] for side in range(2)]
            odd = [parts[1][slot + side * TILE // 2][part] for side in range(2)]
            values = [jnp.where(lane < NX // 4, even[side], odd[side]) for side in range(2)]
            values.append(jnp.where(lane < LANES // 2, odd[0], pltpu.roll(odd[1], LANES // 2, 1)))
            for number, value in enumerate(values):
                out_ref[2 * slot + parity, number, part * planes_padded : (part + 1) * planes_padded, :] = value[
                    :planes_padded
                ]


def finish_kernel(slots, parts, refs):
    part_refs = refs[:parts]
    order_ref, first_ref, second_ref, third_ref, out_ref = refs[parts:]
    first = first_ref[...]
    second = second_ref[...]
    flats = [ref.reshape(ref.shape[0] * 6 * TILE, LANES) for ref in part_refs]
    for part in range(2):
        mains, rests = [], []
        for plane in range(TILE):
            values = []
            for number in range(3):
                at = pl.ds((number * 2 + part) * TILE + plane, slots, stride=6 * TILE)
                total = flats[0][at, :]
                for flat in flats[1:]:
                    total = total + flat[at, :]
                values.append(total)
            mains += values[:2]
            rests += [values[2], pltpu.roll(values[2], LANES // 2, 1)]
        main = split(jnp.concatenate(mains, axis=0))
        rest = split(jnp.concatenate(rests, axis=0))
        ordered = jnp.dot(jnp.concatenate(main + rest, axis=1), order_ref[...], preferred_element_type=F32)
        for plane in range(TILE):
            third = third_ref[pl.program_id(0) * TILE + plane]
            out_ref[part, plane] = ordered[plane * 2 * slots : (plane + 1) * 2 * slots] * (second * third) * first


def on_device(samples, kernel, offsets, owners, tile_ids, deapod_first, deapod_second, deapod_third):
    grid_rows = lax.axis_size("gx")
    grid_cols = lax.axis_size("gy")
    blocks = samples.shape[0]
    block_width = samples.shape[2]
    assert block_width == LANES and blocks <= LANES
    tile_rows = NX // (TILE * grid_rows)
    tile_cols = NY // (TILE * grid_cols)
    tile_depth = NZ // TILE
    planes = deapod_third.shape[0]
    per_device = deapod_second.shape[0]
    rows = padded_rows(per_device)
    planes_padded = -(-planes // 8) * 8
    vmem = pl.BlockSpec(memory_space=pltpu.VMEM)
    params = pltpu.CompilerParams(vmem_limit_bytes=VMEM_LIMIT)

    owner = owners[:, 0]
    row = owner // grid_cols * tile_rows + tile_ids // (tile_cols * tile_depth)
    col = owner % grid_cols * tile_cols + tile_ids // tile_depth % tile_cols
    folds = NX // TILE // 2
    base = row % folds * NY + col
    phase = tile_ids % tile_depth + row // folds * tile_depth
    codes = (base * PHASES + phase).astype(F32)
    codes = jnp.pad(codes, (0, LANES - blocks))[None, :]

    tiles = pl.pallas_call(
        spread_kernel,
        out_shape=jax.ShapeDtypeStruct((blocks // 2 + 1, 2 * TILE, LANES), F32),
        in_specs=[vmem] * 4,
        out_specs=vmem,
        compiler_params=params,
        name="spread",
    )(samples, kernel, offsets, codes)

    gathered = lax.all_gather(tiles, "gy", axis=0, tiled=False)
    tile_codes = gathered[:, blocks // 2, 0, :blocks].astype(jnp.int32).reshape(-1)

    place = lax.axis_index("gx").astype(jnp.int32).reshape(1)
    gy = lax.axis_index("gy")
    matrices, phases = depth_tables(planes)
    matrix = lax.dynamic_index_in_dim(jnp.asarray(matrices), gy, 0, keepdims=False)
    phase_rows = lax.dynamic_index_in_dim(jnp.asarray(phases), gy, 0, keepdims=False)
    column = jnp.asarray(column_tables(grid_rows, per_device))

    def whole(shape):
        return pl.BlockSpec(shape, lambda step: (0,) * len(shape), pipeline_mode=pl.Buffered(1))

    half = NX // 2
    width = 16
    kept = 2 * grid_rows * rows
    spectra = pltpu.VMEM((16 * TILE * TILE, 2 * LANES), F32)
    columns = pl.pallas_call(
        tiles_kernel,
        grid=(half // width,),
        out_shape=jax.ShapeDtypeStruct((half, kept, LANES), F32),
        in_specs=[pl.BlockSpec(memory_space=pltpu.SMEM)]
        + [whole(array.shape) for array in (gathered, matrix, phase_rows, column)],
        out_specs=pl.BlockSpec((width, kept, LANES), lambda step: (step, 0, 0)),
        scratch_shapes=[pltpu.VMEM((half * NY, LANES), F32), spectra, spectra],
        compiler_params=params,
        name="tiles",
    )(tile_codes, gathered, matrix, phase_rows, column)

    row_table = jnp.asarray(row_tables())
    slots = rows
    part_shape = (slots, 3, 2 * planes_padded, LANES)

    def rows_for(relative):
        def block(step, parity, place_ref):
            device = jnp.bitwise_xor(place_ref[0], relative)
            return (0, (parity * grid_rows + device) * (rows // TILE) + step, 0)

        return pl.pallas_call(
            functools.partial(rows_kernel, planes_padded),
            grid_spec=pltpu.PrefetchScalarGridSpec(
                num_scalar_prefetch=1,
                grid=(rows // TILE, 2),
                in_specs=[
                    pl.BlockSpec((half, TILE, LANES), block),
                    pl.BlockSpec(row_table.shape, lambda step, parity, place_ref: (0, 0, 0, 0)),
                ],
                out_specs=pl.BlockSpec((TILE,) + part_shape[1:], lambda step, parity, place_ref: (step, 0, 0, 0)),
            ),
            out_shape=jax.ShapeDtypeStruct(part_shape, F32),
            compiler_params=params,
            cost_estimate=pl.CostEstimate(
                flops=2 * 3 * slots * 2 * LANES * half * 2 * LANES,
                bytes_accessed=4 * (half * 2 * slots * LANES + math.prod(part_shape)),
                transcendentals=0,
            ),
            name="rows",
        )(place, columns, row_table)

    def sums(relatives, bit):
        if bit == 0:
            return [rows_for(relatives)]
        swap = [(index, index ^ bit) for index in range(grid_rows)]
        sent = sum(sums(relatives | bit, bit // 2))
        arrived = lax.ppermute(sent, "gx", swap)
        return sums(relatives, bit // 2) + [arrived]

    finals = sums(0, grid_rows // 2)
    finals = [layer.reshape(slots, 3, 2, planes_padded, LANES) for layer in finals]

    def finish(*refs):
        finish_kernel(per_device // 2, len(finals), refs)

    def shared(shape):
        return pl.BlockSpec(shape, lambda step: (0,) * len(shape))

    return pl.pallas_call(
        finish,
        grid=(planes_padded // TILE,),
        out_shape=jax.ShapeDtypeStruct((2, planes, per_device, NX // 2), F32),
        in_specs=[pl.BlockSpec((slots, 3, 2, TILE, LANES), lambda step: (0, 0, 0, step, 0))] * len(finals)
        + [shared((4 * LANES, NX // 2)), shared((1, NX // 2)), shared((per_device, 1)), pl.BlockSpec(memory_space=pltpu.SMEM)],
        out_specs=pl.BlockSpec((2, TILE, per_device, NX // 2), lambda step: (0, step, 0, 0)),
        compiler_params=params,
        name="finish",
    )(
        *finals,
        jnp.asarray(order_tables()),
        deapod_first[None, :],
        deapod_second[:, None],
        jnp.pad(deapod_third, (0, planes_padded - planes)),
    )


def solution(mesh):
    in_specs = (
        P(("gx", "gy"), None, None),
        P(("gx", "gy"), None, None, None),
        P(("gx", "gy"), None, None),
        P(("gx", "gy"), None),
        P(("gx", "gy")),
        P(),
        P("gx"),
        P("gy"),
    )
    out_specs = P(None, "gy", "gx", None)
    return jax.shard_map(
        on_device, mesh=mesh, in_specs=in_specs, out_specs=out_specs, check_vma=False
    )
```

```python
import functools
import math

import jax
import jax.numpy as jnp
import ml_dtypes
import numpy as np
from jax import lax
from jax.experimental import pallas as pl
from jax.experimental.pallas import tpu as pltpu
from jax.sharding import PartitionSpec as P

NX = 384
NY = 384
NZ = 384
TILE = 8
LANES = 128
PLANES = 32
Z_CHIPS = 4
PHASES = 128
BF16 = jnp.bfloat16
F32 = jnp.float32
VMEM_LIMIT = 60 * 1024 * 1024


def halves(array):
    high = array.astype(ml_dtypes.bfloat16)
    low = (array - high.astype(np.float64)).astype(ml_dtypes.bfloat16)
    return high, low


def split(value):
    high = value.astype(BF16)
    return high, (value - high.astype(F32)).astype(BF16)


def waves(freq, position, length):
    steps = np.mod(freq[:, None] * position[None, :], length)
    phase = 2.0 * math.pi * steps / length
    return np.cos(phase), np.sin(phase)


def depth_tables(planes):
    matrices, phases = [], []
    lane_part = np.arange(LANES) // 64
    lane_odd = np.arange(LANES) // 32 % 2
    lane_plane = np.arange(LANES) % 32
    used = (lane_plane < planes).astype(np.float64)
    for index in range(NZ // 2 // planes):
        position = index * planes + lane_plane - NZ // 4
        cos, sin = waves(np.arange(TILE) - NZ // 2, position, NZ)
        cos, sin = cos * used / math.sqrt(NZ), sin * used / math.sqrt(NZ)
        real = np.where(lane_part == 0, cos, sin)
        imag = np.where(lane_part == 0, -sin, cos)
        plain = np.concatenate((real, imag))
        turned = np.concatenate((-np.where(lane_part == 0, sin, -cos), -np.where(lane_part == 0, cos, sin)))
        high, low = halves(np.concatenate((plain, turned), axis=1))
        matrices.append(np.concatenate((high, high, low), axis=0))
        cos, sin = waves(np.arange(NZ // TILE), position, NZ // TILE)
        sign = np.where(lane_odd == 1, -1.0, 1.0)[None, :]
        phases.append(np.stack((np.concatenate((cos, cos * sign)), np.concatenate((sin, sin * sign)))))
    return np.stack(matrices), np.stack(phases).astype(np.float32)


def padded_rows(per_device):
    return -(-(per_device // 2) // TILE) * TILE


def column_tables(devices, per_device):
    half = NY // 2
    rows = padded_rows(per_device)
    place = np.arange(rows)
    slot = place // 8 * 4 + place % 4
    local = 2 * slot + place % 8 // 4 * (per_device // 2)
    used = (slot < per_device // 4).astype(np.float64)[:, None]
    out = []
    for parity in range(2):
        cos_parts, sin_parts = [], []
        for device in range(devices):
            cos, sin = waves(device * per_device + local + parity - NY // 4, np.arange(half) - half, NY)
            cos_parts.append(cos * used)
            sin_parts.append(sin * used)
        out.append(np.concatenate(halves(np.concatenate(cos_parts + sin_parts) / math.sqrt(NY))))
    return np.stack(out)


def row_tables():
    half = NX // 2
    quarter = NX // 4
    out = []
    for parity in range(2):
        position = 2 * np.arange(quarter) + parity - NX // 4
        cos, sin = waves(np.arange(half) - half, position, NX)
        table = np.zeros((half, 2 * LANES))
        lanes = (np.arange(quarter) + parity * quarter) % LANES
        table[:, lanes] = cos / math.sqrt(NX)
        table[:, LANES + lanes] = sin / math.sqrt(NX)
        out.append(np.stack(halves(table)))
    return np.stack(out)


def order_tables():
    first = np.zeros((LANES, NX // 2))
    second = np.zeros((LANES, NX // 2))
    quarter = NX // 4
    for m1 in range(NX // 2):
        place = m1 // 2 + m1 % 2 * quarter
        if place < LANES:
            first[place, m1] = 1.0
        else:
            second[place - LANES, m1] = 1.0
    return np.concatenate((first, first, second, second)).astype(ml_dtypes.bfloat16)


def spread_kernel(samples_ref, kernel_ref, offsets_ref, out_ref):
    blocks = samples_ref.shape[0]
    taps = kernel_ref.shape[2]
    cell = lax.broadcasted_iota(jnp.int32, (TILE, LANES), 0)
    left = lax.broadcasted_iota(jnp.int32, (2 * TILE, LANES), 1) < LANES // 2

    def weights(block):
        placed = []
        for dim in range(3):
            shifted = cell - offsets_ref[dim, pl.ds(block, 1), :]
            value = jnp.zeros((TILE, LANES), F32)
            for tap in range(taps):
                value = jnp.where(shifted == tap, kernel_ref[block, dim, pl.ds(tap, 1), :], value)
            placed.append(value)
        plane = jnp.concatenate([placed[0][i : i + 1] * placed[1] for i in range(TILE)], axis=0)
        depth = jnp.concatenate([samples_ref[block, pl.ds(c, 1), :] * placed[2] for c in range(2)], axis=0)
        return depth, plane

    def pair_body(pair, carry):
        depth_a, plane_a = weights(2 * pair)
        depth_b, plane_b = weights(2 * pair + 1)
        depth_high, depth_low = split(jnp.concatenate((depth_a, depth_b), axis=0))
        plane_high, plane_low = split(jnp.concatenate((plane_a, plane_b), axis=0))
        piece = lax.dot_general(
            jnp.concatenate((depth_high, depth_low, depth_high), axis=1),
            jnp.concatenate((plane_high, plane_high, plane_low), axis=1),
            (((1,), (1,)), ((), ())),
            preferred_element_type=F32,
        )
        out_ref[pair] = jnp.where(left, piece[: 2 * TILE], piece[2 * TILE :])
        return carry

    lax.fori_loop(0, blocks // 2, pair_body, 0, unroll=4)


def tiles_kernel(sources, *refs):
    source_refs = refs[1 : 1 + sources]
    codes_ref, depth_ref, phases_ref, column_ref, out_ref = refs[:1] + refs[1 + sources : 5 + sources]
    tiles_ref, acc_ref, even_ref, odd_ref, arrived = refs[5 + sources :]
    half = NX // 2
    stride = NY
    pairs = tiles_ref.shape[1]
    batch = 8
    assert pairs % (2 * batch) == 0
    batches = pairs // batch
    rows = column_ref.shape[1] // 4
    width = out_ref.shape[0]

    def spectrum(source, number, to_ref):
        tiles = jnp.concatenate([tiles_ref[source, number * batch + index] for index in range(batch)], axis=1)
        high, low = split(tiles)
        to_ref[...] = lax.dot_general(
            jnp.concatenate((high, low, high), axis=0),
            depth_ref[...],
            (((0,), (0,)), ((), ())),
            preferred_element_type=F32,
        )

    def accumulate(source, number, from_ref):
        for tile in range(2 * batch):
            code = codes_ref[(source * batches + number) * 2 * batch + tile]
            base = lax.shift_right_logical(code, 7)
            phase = jnp.bitwise_and(code, PHASES - 1)
            cos = phases_ref[0, pl.ds(phase, 1), :]
            sin = phases_ref[1, pl.ds(phase, 1), :]
            for i in range(TILE):
                row = tile * TILE * TILE + i * TILE
                value = from_ref[row : row + TILE, :LANES] * cos + from_ref[row : row + TILE, LANES:] * sin
                at = pl.ds(pl.multiple_of(base * TILE + i * stride, TILE), TILE)
                acc_ref[at, :] = acc_ref[at, :] + value

    @pl.when(pl.program_id(0) == 0)
    def _():
        copies = [
            pltpu.make_async_copy(source_ref, tiles_ref.at[index], arrived.at[index])
            for index, source_ref in enumerate(source_refs)
        ]
        for copy in copies:
            copy.start()

        def clear(step, carry):
            acc_ref[pl.ds(pl.multiple_of(step * stride, stride), stride), :] = jnp.zeros((stride, LANES), F32)
            return carry

        lax.fori_loop(0, half, clear, 0)
        for copy in copies:
            copy.wait()
        spectrum(0, 0, even_ref)

        def add_pair(step, carry):
            first = 2 * step
            source, number = first // batches, first % batches
            spectrum(source, number + 1, odd_ref)
            accumulate(source, number, even_ref)
            later = jnp.minimum(first + 2, sources * batches - 2)
            spectrum(later // batches, later % batches, even_ref)
            accumulate(source, number + 1, odd_ref)
            return carry

        lax.fori_loop(0, sources * batches // 2, add_pair, 0)

    turn = jnp.where(lax.broadcasted_iota(jnp.int32, (rows, LANES), 1) < LANES // 2, -1.0, 1.0)
    origin = pl.program_id(0) * width

    def columns(step, carry):
        folded = ([], [])
        for side in range(2):
            start = pl.multiple_of((origin + 2 * step + side) * stride, stride)
            lower = acc_ref[pl.ds(start, NY // 2), :]
            upper = acc_ref[pl.ds(start + NY // 2, NY // 2), :]
            folded[0].append(lower + upper)
            folded[1].append(lower - upper)
        for parity in range(2):
            high, low = split(jnp.concatenate(folded[parity], axis=1))
            both = jnp.dot(column_ref[parity], high, preferred_element_type=F32)
            rest = jnp.dot(column_ref[parity, : 2 * rows], low, preferred_element_type=F32)
            product = both[: 2 * rows] + both[2 * rows :] + rest
            for side in range(2):
                lanes = slice(side * LANES, (side + 1) * LANES)
                out_ref[2 * step + side, parity * rows : (parity + 1) * rows, :] = (
                    product[:rows, lanes] + pltpu.roll(product[rows:, lanes], LANES // 2, 1) * turn
                )
        return carry

    lax.fori_loop(0, width // 2, columns, 0, unroll=2)


def rows_kernel(planes_padded, addends, place_ref, in_ref, row_ref, *refs):
    out_ref = refs[-1]
    half = NX // 2
    parity = pl.program_id(1)
    lane = lax.broadcasted_iota(jnp.int32, (PLANES, LANES), 1)
    flat = in_ref.reshape(half * TILE, LANES)
    turned = [flat[pl.ds(row, half, stride=TILE), :].T for row in range(TILE)]
    parts = []
    for odd in range(2):
        at = odd * PLANES
        stacked = [value[part * 64 + at : part * 64 + at + PLANES] for value in turned for part in range(2)]
        high, low = split(jnp.concatenate(stacked, axis=0))
        count = high.shape[0]
        both = jnp.dot(jnp.concatenate((high, low), axis=0), row_ref[odd, 0], preferred_element_type=F32)
        product = both[:count] + both[count:] + jnp.dot(high, row_ref[odd, 1], preferred_element_type=F32)
        sides = []
        for row in range(TILE):
            real = product[2 * row * PLANES : (2 * row + 1) * PLANES]
            imag = product[(2 * row + 1) * PLANES : (2 * row + 2) * PLANES]
            sides.append((real[:, :LANES] - imag[:, LANES:], real[:, LANES:] + imag[:, :LANES]))
        parts.append(sides)
    for slot in range(TILE // 2):
        for part in range(2):
            even = [parts[0][slot + side * TILE // 2][part] for side in range(2)]
            odd = [parts[1][slot + side * TILE // 2][part] for side in range(2)]
            values = [jnp.where(lane < NX // 4, even[side], odd[side]) for side in range(2)]
            values.append(jnp.where(lane < LANES // 2, odd[0], pltpu.roll(odd[1], LANES // 2, 1)))
            for number, value in enumerate(values):
                at = (2 * slot + parity, number, pl.ds(part * planes_padded, planes_padded))
                total = value[:planes_padded]
                for ref in refs[:addends]:
                    total = total + ref[at]
                out_ref[at] = total


def finish_kernel(planes_padded, parts, refs):
    part_refs = refs[:parts]
    order_ref, first_ref, second_ref, third_ref = refs[parts : parts + 4]
    out_ref = refs[-1]
    planes = out_ref.shape[1]
    stride = 6 * planes_padded
    flats = [ref.reshape(TILE * stride, LANES) for ref in part_refs]
    order = order_ref[...]
    for part in range(2):
        for group in range(0, planes, TILE):
            members = range(group, min(group + TILE, planes))
            mains, rests = [], []
            for plane in members:
                values = []
                for number in range(3):
                    at = pl.ds((number * 2 + part) * planes_padded + plane, TILE, stride=stride)
                    total = flats[0][at, :]
                    for flat in flats[1:]:
                        total = total + flat[at, :]
                    values.append(total)
                mains += values[:2]
                rests += [values[2], pltpu.roll(values[2], LANES // 2, 1)]
            main = split(jnp.concatenate(mains, axis=0))
            rest = split(jnp.concatenate(rests, axis=0))
            ordered = jnp.dot(jnp.concatenate(main + rest, axis=1), order, preferred_element_type=F32)
            for index, plane in enumerate(members):
                for side in range(2):
                    row = (2 * index + side) * TILE
                    scale = second_ref[side] * third_ref[plane] * first_ref[...]
                    out_ref[part, plane, side] = ordered[row : row + TILE] * scale


def on_device(samples, kernel, offsets, owners, tile_ids, deapod_first, deapod_second, deapod_third):
    grid_rows = lax.axis_size("gx")
    grid_cols = lax.axis_size("gy")
    blocks = samples.shape[0]
    block_width = samples.shape[2]
    assert block_width == LANES and blocks <= LANES
    tile_rows = NX // (TILE * grid_rows)
    tile_cols = NY // (TILE * grid_cols)
    tile_depth = NZ // TILE
    planes = deapod_third.shape[0]
    per_device = deapod_second.shape[0]
    rows = padded_rows(per_device)
    planes_padded = -(-planes // 8) * 8
    vmem = pl.BlockSpec(memory_space=pltpu.VMEM)
    params = pltpu.CompilerParams(vmem_limit_bytes=VMEM_LIMIT)

    owner = owners[:, 0]
    row = owner // grid_cols * tile_rows + tile_ids // (tile_cols * tile_depth)
    col = owner % grid_cols * tile_cols + tile_ids // tile_depth % tile_cols
    folds = NX // TILE // 2
    base = row % folds * NY + col
    phase = tile_ids % tile_depth + row // folds * tile_depth
    codes = base * PHASES + phase

    tiles = pl.pallas_call(
        spread_kernel,
        out_shape=jax.ShapeDtypeStruct((blocks // 2, 2 * TILE, LANES), F32),
        in_specs=[vmem] * 3,
        out_specs=vmem,
        compiler_params=params,
        name="spread",
    )(samples, kernel, offsets.transpose(1, 0, 2))

    along = grid_cols // Z_CHIPS

    def shift(value, deep, wide):
        moves = [
            (z * along + y, (z + deep) % Z_CHIPS * along + (y + wide) % along)
            for z in range(Z_CHIPS)
            for y in range(along)
        ]
        return lax.ppermute(value, "gy", moves)

    def collect(value):
        stack = [value] + [shift(value, deep, 0) for deep in (1, 3, 2)]
        return stack + [shift(held, 0, wide) for wide in range(1, along) for held in stack]

    tile_codes = jnp.concatenate(collect(codes))
    gathered = collect(tiles)

    place = lax.axis_index("gx").astype(jnp.int32).reshape(1)
    gy = lax.axis_index("gy")
    matrices, phases = depth_tables(planes)
    matrix = lax.dynamic_index_in_dim(jnp.asarray(matrices), gy, 0, keepdims=False)
    phase_rows = lax.dynamic_index_in_dim(jnp.asarray(phases), gy, 0, keepdims=False)
    column = jnp.asarray(column_tables(grid_rows, per_device))

    def whole(shape):
        return pl.BlockSpec(shape, lambda step: (0,) * len(shape), pipeline_mode=pl.Buffered(1))

    half = NX // 2
    width = 16
    kept = 2 * grid_rows * rows
    spectra = pltpu.VMEM((16 * TILE * TILE, 2 * LANES), F32)
    columns = pl.pallas_call(
        functools.partial(tiles_kernel, len(gathered)),
        grid=(half // width,),
        out_shape=jax.ShapeDtypeStruct((half, kept, LANES), F32),
        in_specs=[pl.BlockSpec(memory_space=pltpu.SMEM)]
        + [pl.BlockSpec(memory_space=pl.ANY)] * len(gathered)
        + [whole(array.shape) for array in (matrix, phase_rows, column)],
        out_specs=pl.BlockSpec((width, kept, LANES), lambda step: (step, 0, 0)),
        scratch_shapes=[
            pltpu.VMEM((len(gathered),) + tiles.shape, F32),
            pltpu.VMEM((half * NY, LANES), F32),
            spectra,
            spectra,
            pltpu.SemaphoreType.DMA((len(gathered),)),
        ],
        compiler_params=params,
        name="tiles",
    )(tile_codes, *gathered, matrix, phase_rows, column)

    row_table = jnp.asarray(row_tables())
    chunks = rows // TILE
    part_shape = (3, 2 * planes_padded, LANES)

    def rows_for(relative, first, count, addends, after):
        def block(step, parity, place_ref):
            device = jnp.bitwise_xor(place_ref[0], relative)
            return (0, (parity * grid_rows + device) * chunks + first + step, 0)

        part = pl.BlockSpec((TILE,) + part_shape, lambda step, parity, place_ref: (step, 0, 0, 0))
        slots = count * TILE

        def body(*refs):
            rows_kernel(planes_padded, len(addends), *refs[: 3 + len(addends)], refs[-1])

        return pl.pallas_call(
            body,
            grid_spec=pltpu.PrefetchScalarGridSpec(
                num_scalar_prefetch=1,
                grid=(count, 2),
                in_specs=[
                    pl.BlockSpec((half, TILE, LANES), block),
                    pl.BlockSpec(row_table.shape, lambda step, parity, place_ref: (0, 0, 0, 0)),
                ]
                + [part] * len(addends)
                + [pl.BlockSpec(memory_space=pl.ANY)] * len(after),
                out_specs=part,
            ),
            out_shape=jax.ShapeDtypeStruct((slots,) + part_shape, F32),
            compiler_params=params,
            cost_estimate=pl.CostEstimate(
                flops=2 * 3 * slots * 2 * LANES * half * 2 * LANES,
                bytes_accessed=4 * (half * 2 * slots * LANES + slots * math.prod(part_shape)),
                transcendentals=0,
            ),
            name="rows",
        )(place, columns, row_table, *addends, *after)

    def swap(value, bit):
        return lax.ppermute(value, "gx", [(index, index ^ bit) for index in range(grid_rows)])

    def total(relative, top, first, count, after):
        arrived = []
        bit = 1
        while bit <= top:
            arrived.append(swap(total(relative | bit, bit // 2, first, count, after), bit))
            bit *= 2
        return rows_for(relative, first, count, arrived, after)

    top = grid_rows // 2
    crossing = [total(top, top // 2, chunk, 1, []) for chunk in range(chunks)]
    kept_part = total(0, top // 2, 0, chunks, [crossing[-1]])
    crossed = [swap(value, top) for value in crossing]

    image = None
    shape = (2, planes, 2, per_device // 2, NX // 2)
    for chunk in range(chunks):

        def at_chunk(_, chunk=chunk):
            return (chunk, 0, 0, 0)

        def finish(*refs):
            finish_kernel(planes_padded, 2, refs)

        earlier = [] if image is None else [image]
        image = pl.pallas_call(
            finish,
            grid=(1,),
            out_shape=jax.ShapeDtypeStruct(shape, F32),
            in_specs=[
                pl.BlockSpec((TILE,) + part_shape, at_chunk),
                pl.BlockSpec((TILE,) + part_shape, lambda step: (0, 0, 0, 0)),
                pl.BlockSpec((4 * LANES, NX // 2), lambda step: (0, 0)),
                pl.BlockSpec((1, NX // 2), lambda step: (0, 0)),
                pl.BlockSpec((2, TILE, 1), lambda step, chunk=chunk: (0, chunk, 0)),
                pl.BlockSpec(memory_space=pltpu.SMEM),
            ]
            + [pl.BlockSpec(memory_space=pl.ANY)] * len(earlier),
            out_specs=pl.BlockSpec((2, planes, 2, TILE, NX // 2), lambda step, chunk=chunk: (0, 0, 0, chunk, 0)),
            input_output_aliases={6: 0} if earlier else {},
            compiler_params=params,
            name="finish",
        )(
            kept_part,
            crossed[chunk],
            jnp.asarray(order_tables()),
            deapod_first[None, :],
            deapod_second.reshape(2, per_device // 2, 1),
            deapod_third,
            *earlier,
        )
    return image.reshape(2, planes, per_device, NX // 2)


def solution(mesh):
    in_specs = (
        P(("gx", "gy"), None, None),
        P(("gx", "gy"), None, None, None),
        P(("gx", "gy"), None, None),
        P(("gx", "gy"), None),
        P(("gx", "gy")),
        P(),
        P("gx"),
        P("gy"),
    )
    out_specs = P(None, "gy", "gx", None)
    return jax.shard_map(
        on_device, mesh=mesh, in_specs=in_specs, out_specs=out_specs, check_vma=False
    )
```

```python
import functools
import math

import jax
import jax.numpy as jnp
import ml_dtypes
import numpy as np
from jax import lax
from jax.experimental import pallas as pl
from jax.experimental.pallas import tpu as pltpu
from jax.sharding import PartitionSpec as P

NX = 384
NY = 384
NZ = 384
TILE = 8
LANES = 128
PLANES = 32
Z_CHIPS = 4
PHASES = 128
BF16 = jnp.bfloat16
F32 = jnp.float32
VMEM_LIMIT = 60 * 1024 * 1024


def halves(array):
    high = array.astype(ml_dtypes.bfloat16)
    low = (array - high.astype(np.float64)).astype(ml_dtypes.bfloat16)
    return high, low


def split(value):
    high = value.astype(BF16)
    return high, (value - high.astype(F32)).astype(BF16)


def waves(freq, position, length):
    steps = np.mod(freq[:, None] * position[None, :], length)
    phase = 2.0 * math.pi * steps / length
    return np.cos(phase), np.sin(phase)


def depth_tables(planes):
    matrices, phases = [], []
    lane_part = np.arange(LANES) // 64
    lane_odd = np.arange(LANES) // 32 % 2
    lane_plane = np.arange(LANES) % 32
    used = (lane_plane < planes).astype(np.float64)
    for index in range(NZ // 2 // planes):
        position = index * planes + lane_plane - NZ // 4
        cos, sin = waves(np.arange(TILE) - NZ // 2, position, NZ)
        cos, sin = cos * used / math.sqrt(NZ), sin * used / math.sqrt(NZ)
        real = np.where(lane_part == 0, cos, sin)
        imag = np.where(lane_part == 0, -sin, cos)
        plain = np.concatenate((real, imag))
        turned = np.concatenate((-np.where(lane_part == 0, sin, -cos), -np.where(lane_part == 0, cos, sin)))
        matrices.append(np.stack((plain, turned)))
        cos, sin = waves(np.arange(NZ // TILE), position, NZ // TILE)
        sign = np.where(lane_odd == 1, -1.0, 1.0)[None, :]
        phases.append(np.stack((np.concatenate((cos, cos * sign)), np.concatenate((sin, sin * sign)))))
    return np.stack(matrices).astype(np.float32), np.stack(phases).astype(np.float32)


def padded_rows(per_device):
    return -(-(per_device // 2) // TILE) * TILE


def column_tables(devices, per_device):
    half = NY // 2
    rows = padded_rows(per_device)
    place = np.arange(rows)
    slot = place // 8 * 4 + place % 4
    local = 2 * slot + place % 8 // 4 * (per_device // 2)
    used = (slot < per_device // 4).astype(np.float64)[:, None]
    out = []
    for parity in range(2):
        cos_parts, sin_parts = [], []
        for device in range(devices):
            cos, sin = waves(device * per_device + local + parity - NY // 4, np.arange(half) - half, NY)
            cos_parts.append(cos * used)
            sin_parts.append(sin * used)
        out.append(np.concatenate(halves(np.concatenate(cos_parts + sin_parts) / math.sqrt(NY))))
    return np.stack(out)


def row_tables():
    half = NX // 2
    quarter = NX // 4
    out = []
    for parity in range(2):
        position = 2 * np.arange(quarter) + parity - NX // 4
        cos, sin = waves(np.arange(half) - half, position, NX)
        table = np.zeros((half, 2 * LANES))
        lanes = (np.arange(quarter) + parity * quarter) % LANES
        table[:, lanes] = cos / math.sqrt(NX)
        table[:, LANES + lanes] = sin / math.sqrt(NX)
        out.append(np.stack(halves(table)))
    return np.stack(out)


def order_tables():
    first = np.zeros((LANES, NX // 2))
    second = np.zeros((LANES, NX // 2))
    quarter = NX // 4
    for m1 in range(NX // 2):
        place = m1 // 2 + m1 % 2 * quarter
        if place < LANES:
            first[place, m1] = 1.0
        else:
            second[place - LANES, m1] = 1.0
    return np.concatenate((first, first, second, second)).astype(ml_dtypes.bfloat16)


def divide(value, divisor, limit):
    for shift in range(8, 24):
        factor = (1 << shift) // divisor + 1
        tried = np.arange(limit, dtype=np.int64)
        if factor * limit < 1 << 31 and np.array_equal(tried * factor >> shift, tried // divisor):
            return lax.shift_right_logical(value * factor, shift)
    raise ValueError(divisor)


def spread_kernel(tile_rows, tile_cols, grid_cols, devices, samples_ref, kernel_ref, offsets_ref, owners_ref, ids_ref, out_ref):
    owner, tile_id = owners_ref[...], ids_ref[...]
    tile_depth = NZ // TILE
    tiles_device = tile_rows * tile_cols * tile_depth
    owner_row = divide(owner, grid_cols, devices)
    tile_row = divide(tile_id, tile_cols * tile_depth, tiles_device)
    tile_col = divide(tile_id, tile_depth, tiles_device)
    row = owner_row * tile_rows + tile_row
    col = (owner - owner_row * grid_cols) * tile_cols + tile_col - tile_row * tile_cols
    folds = NX // TILE // 2
    upper = (row >= folds).astype(jnp.int32)
    base = (row - upper * folds) * NY + col
    phase = tile_id - tile_col * tile_depth + upper * tile_depth
    codes = (base * PHASES + phase).astype(F32)

    blocks = samples_ref.shape[0]
    taps = kernel_ref.shape[2]
    cell = lax.broadcasted_iota(jnp.int32, (TILE, LANES), 0)
    left = lax.broadcasted_iota(jnp.int32, (2 * TILE, LANES), 1) < LANES // 2

    def weights(block):
        placed = []
        for dim in range(3):
            shifted = cell - offsets_ref[dim, pl.ds(block, 1), :]
            value = jnp.zeros((TILE, LANES), F32)
            for tap in range(taps):
                value = jnp.where(shifted == tap, kernel_ref[block, dim, pl.ds(tap, 1), :], value)
            placed.append(value)
        plane = jnp.concatenate([placed[0][i : i + 1] * placed[1] for i in range(TILE)], axis=0)
        depth = jnp.concatenate([samples_ref[block, pl.ds(c, 1), :] * placed[2] for c in range(2)], axis=0)
        return depth, plane

    def pair_body(pair, carry):
        depth_a, plane_a = weights(2 * pair)
        depth_b, plane_b = weights(2 * pair + 1)
        depth_high, depth_low = split(jnp.concatenate((depth_a, depth_b), axis=0))
        plane_high, plane_low = split(jnp.concatenate((plane_a, plane_b), axis=0))
        piece = lax.dot_general(
            jnp.concatenate((depth_high, depth_low, depth_high), axis=1),
            jnp.concatenate((plane_high, plane_high, plane_low), axis=1),
            (((1,), (1,)), ((), ())),
            preferred_element_type=F32,
        )
        out_ref[pair] = jnp.where(left, piece[: 2 * TILE], piece[2 * TILE :])
        return carry

    lax.fori_loop(0, blocks // 2, pair_body, 0, unroll=4)
    out_ref[blocks // 2] = jnp.broadcast_to(codes, (2 * TILE, LANES))


def weights_kernel(matrix_ref, phases_ref, out_ref):
    plain, turned = matrix_ref[0], matrix_ref[1]

    def body(row, carry):
        high, low = split(plain * phases_ref[0, pl.ds(row, 1), :] + turned * phases_ref[1, pl.ds(row, 1), :])
        out_ref[row] = jnp.concatenate((high, high, low), axis=0)
        return carry

    lax.fori_loop(0, out_ref.shape[0], body, 0, unroll=4)


def tiles_kernel(sources, *refs):
    source_refs = refs[:sources]
    weights_ref, column_ref, out_ref, tiles_ref, codes_ref, acc_ref, arrived = refs[sources:]
    half = NX // 2
    stride = NY
    pairs = tiles_ref.shape[1]
    batch = 8
    rows = column_ref.shape[1] // 4
    width = out_ref.shape[0]

    @pl.when(pl.program_id(0) == 0)
    def _():
        copies = []
        for index, ref in enumerate(source_refs):
            copies.append(pltpu.make_async_copy(ref.at[pl.ds(0, pairs)], tiles_ref.at[index], arrived.at[0, index]))
            copies.append(pltpu.make_async_copy(ref.at[pairs, pl.ds(0, TILE)], codes_ref.at[index], arrived.at[1, index]))
        for copy in copies:
            copy.start()

        def clear(step, carry):
            acc_ref[pl.ds(pl.multiple_of(step * stride, stride), stride), :] = jnp.zeros((stride, LANES), F32)
            return carry

        lax.fori_loop(0, half, clear, 0)
        for copy in copies:
            copy.wait()

        def add_batch(step, carry):
            source = step // (pairs // batch)
            first = step % (pairs // batch) * batch
            for index in range(batch):
                high, low = split(tiles_ref[source, first + index])
                stacked = jnp.concatenate((high, low, high), axis=0).T
                for side in range(2):
                    code = codes_ref[source, 0, 2 * (first + index) + side].astype(jnp.int32)
                    base = lax.shift_right_logical(code, 7)
                    phase = jnp.bitwise_and(code, PHASES - 1)
                    value = jnp.dot(
                        stacked[side * TILE * TILE : (side + 1) * TILE * TILE],
                        weights_ref[phase],
                        preferred_element_type=F32,
                    )
                    for i in range(TILE):
                        at = pl.ds(pl.multiple_of(base * TILE + i * stride, TILE), TILE)
                        acc_ref[at, :] = acc_ref[at, :] + value[i * TILE : (i + 1) * TILE]
            return carry

        lax.fori_loop(0, sources * pairs // batch, add_batch, 0)

    turn = jnp.where(lax.broadcasted_iota(jnp.int32, (rows, LANES), 1) < LANES // 2, -1.0, 1.0)
    origin = pl.program_id(0) * width

    def columns(step, carry):
        folded = ([], [])
        for side in range(2):
            start = pl.multiple_of((origin + 2 * step + side) * stride, stride)
            lower = acc_ref[pl.ds(start, NY // 2), :]
            upper = acc_ref[pl.ds(start + NY // 2, NY // 2), :]
            folded[0].append(lower + upper)
            folded[1].append(lower - upper)
        for parity in range(2):
            high, low = split(jnp.concatenate(folded[parity], axis=1))
            both = jnp.dot(column_ref[parity], high, preferred_element_type=F32)
            rest = jnp.dot(column_ref[parity, : 2 * rows], low, preferred_element_type=F32)
            product = both[: 2 * rows] + both[2 * rows :] + rest
            for side in range(2):
                lanes = slice(side * LANES, (side + 1) * LANES)
                out_ref[2 * step + side, parity * rows : (parity + 1) * rows, :] = (
                    product[:rows, lanes] + pltpu.roll(product[rows:, lanes], LANES // 2, 1) * turn
                )
        return carry

    lax.fori_loop(0, width // 2, columns, 0, unroll=2)


def rows_kernel(planes_padded, addends, place_ref, in_ref, row_ref, *refs):
    out_ref = refs[-1]
    half = NX // 2
    parity = pl.program_id(1)
    lane = lax.broadcasted_iota(jnp.int32, (PLANES, LANES), 1)
    flat = in_ref.reshape(half * TILE, LANES)
    turned = [flat[pl.ds(row, half, stride=TILE), :].T for row in range(TILE)]
    parts = []
    for odd in range(2):
        at = odd * PLANES
        stacked = [value[part * 64 + at : part * 64 + at + PLANES] for value in turned for part in range(2)]
        high, low = split(jnp.concatenate(stacked, axis=0))
        count = high.shape[0]
        both = jnp.dot(jnp.concatenate((high, low), axis=0), row_ref[odd, 0], preferred_element_type=F32)
        product = both[:count] + both[count:] + jnp.dot(high, row_ref[odd, 1], preferred_element_type=F32)
        sides = []
        for row in range(TILE):
            real = product[2 * row * PLANES : (2 * row + 1) * PLANES]
            imag = product[(2 * row + 1) * PLANES : (2 * row + 2) * PLANES]
            sides.append((real[:, :LANES] - imag[:, LANES:], real[:, LANES:] + imag[:, :LANES]))
        parts.append(sides)
    for slot in range(TILE // 2):
        for part in range(2):
            even = [parts[0][slot + side * TILE // 2][part] for side in range(2)]
            odd = [parts[1][slot + side * TILE // 2][part] for side in range(2)]
            values = [jnp.where(lane < NX // 4, even[side], odd[side]) for side in range(2)]
            values.append(jnp.where(lane < LANES // 2, odd[0], pltpu.roll(odd[1], LANES // 2, 1)))
            for number, value in enumerate(values):
                at = (2 * slot + parity, number, pl.ds(part * planes_padded, planes_padded))
                total = value[:planes_padded]
                for ref in refs[:addends]:
                    total = total + ref[at]
                out_ref[at] = total


def finish_kernel(planes_padded, parts, refs):
    part_refs = refs[:parts]
    order_ref, first_ref, second_ref, third_ref = refs[parts : parts + 4]
    out_ref = refs[-1]
    planes = out_ref.shape[1]
    stride = 6 * planes_padded
    flats = [ref.reshape(TILE * stride, LANES) for ref in part_refs]
    order = order_ref[...]
    for part in range(2):
        for group in range(0, planes, TILE):
            members = range(group, min(group + TILE, planes))
            mains, rests = [], []
            for plane in members:
                values = []
                for number in range(3):
                    at = pl.ds((number * 2 + part) * planes_padded + plane, TILE, stride=stride)
                    total = flats[0][at, :]
                    for flat in flats[1:]:
                        total = total + flat[at, :]
                    values.append(total)
                mains += values[:2]
                rests += [values[2], pltpu.roll(values[2], LANES // 2, 1)]
            main = split(jnp.concatenate(mains, axis=0))
            rest = split(jnp.concatenate(rests, axis=0))
            ordered = jnp.dot(jnp.concatenate(main + rest, axis=1), order, preferred_element_type=F32)
            for index, plane in enumerate(members):
                for side in range(2):
                    row = (2 * index + side) * TILE
                    scale = second_ref[side] * third_ref[plane] * first_ref[...]
                    out_ref[part, plane, side] = ordered[row : row + TILE] * scale


def on_device(samples, kernel, offsets, owners, tile_ids, deapod_first, deapod_second, deapod_third):
    grid_rows = lax.axis_size("gx")
    grid_cols = lax.axis_size("gy")
    blocks = samples.shape[0]
    block_width = samples.shape[2]
    assert block_width == LANES and blocks == LANES
    tile_rows = NX // (TILE * grid_rows)
    tile_cols = NY // (TILE * grid_cols)
    planes = deapod_third.shape[0]
    per_device = deapod_second.shape[0]
    rows = padded_rows(per_device)
    planes_padded = -(-planes // 8) * 8
    vmem = pl.BlockSpec(memory_space=pltpu.VMEM)
    params = pltpu.CompilerParams(vmem_limit_bytes=VMEM_LIMIT)

    tiles = pl.pallas_call(
        functools.partial(spread_kernel, tile_rows, tile_cols, grid_cols, grid_rows * grid_cols),
        out_shape=jax.ShapeDtypeStruct((blocks // 2 + 1, 2 * TILE, LANES), F32),
        in_specs=[vmem] * 5,
        out_specs=vmem,
        compiler_params=params,
        name="spread",
    )(samples, kernel, offsets.transpose(1, 0, 2), owners.reshape(1, blocks), tile_ids.reshape(1, blocks))

    along = grid_cols // Z_CHIPS

    def shift(value, deep, wide):
        moves = [
            (z * along + y, (z + deep) % Z_CHIPS * along + (y + wide) % along)
            for z in range(Z_CHIPS)
            for y in range(along)
        ]
        return lax.ppermute(value, "gy", moves)

    gathered = [tiles] + [shift(tiles, deep, 0) for deep in (1, 3, 2)]
    crossed_y = []
    for held in list(gathered):
        for wide in range(1, along):
            if len(crossed_y) > 1:
                held, _ = lax.optimization_barrier((held, crossed_y[-2]))
            crossed_y.append(shift(held, 0, wide))
    gathered += crossed_y

    place = lax.axis_index("gx").astype(jnp.int32).reshape(1)
    gy = lax.axis_index("gy")
    matrices, phases = depth_tables(planes)
    matrix = lax.dynamic_index_in_dim(jnp.asarray(matrices), gy, 0, keepdims=False)
    phase_rows = lax.dynamic_index_in_dim(jnp.asarray(phases), gy, 0, keepdims=False)
    column = jnp.asarray(column_tables(grid_rows, per_device))
    weights = pl.pallas_call(
        weights_kernel,
        out_shape=jax.ShapeDtypeStruct((phases.shape[2], 6 * TILE, LANES), BF16),
        in_specs=[vmem] * 2,
        out_specs=vmem,
        compiler_params=params,
        name="weights",
    )(matrix, phase_rows)

    def whole(shape):
        return pl.BlockSpec(shape, lambda step: (0,) * len(shape), pipeline_mode=pl.Buffered(1))

    half = NX // 2
    width = 16
    kept = 2 * grid_rows * rows
    columns = pl.pallas_call(
        functools.partial(tiles_kernel, len(gathered)),
        grid=(half // width,),
        out_shape=jax.ShapeDtypeStruct((half, kept, LANES), F32),
        in_specs=[pl.BlockSpec(memory_space=pl.ANY)] * len(gathered)
        + [whole(array.shape) for array in (weights, column)],
        out_specs=pl.BlockSpec((width, kept, LANES), lambda step: (step, 0, 0)),
        scratch_shapes=[
            pltpu.VMEM((len(gathered), blocks // 2) + tiles.shape[1:], F32),
            pltpu.SMEM((len(gathered), TILE, LANES), F32),
            pltpu.VMEM((half * NY, LANES), F32),
            pltpu.SemaphoreType.DMA((2, len(gathered))),
        ],
        compiler_params=params,
        name="tiles",
    )(*gathered, weights, column)

    row_table = jnp.asarray(row_tables())
    chunks = rows // TILE
    part_shape = (3, 2 * planes_padded, LANES)

    def rows_for(relative, first, count, addends, after):
        def block(step, parity, place_ref):
            device = jnp.bitwise_xor(place_ref[0], relative)
            return (0, (parity * grid_rows + device) * chunks + first + step, 0)

        part = pl.BlockSpec((TILE,) + part_shape, lambda step, parity, place_ref: (step, 0, 0, 0))
        slots = count * TILE

        def body(*refs):
            rows_kernel(planes_padded, len(addends), *refs[: 3 + len(addends)], refs[-1])

        return pl.pallas_call(
            body,
            grid_spec=pltpu.PrefetchScalarGridSpec(
                num_scalar_prefetch=1,
                grid=(count, 2),
                in_specs=[
                    pl.BlockSpec((half, TILE, LANES), block),
                    pl.BlockSpec(row_table.shape, lambda step, parity, place_ref: (0, 0, 0, 0)),
                ]
                + [part] * len(addends)
                + [pl.BlockSpec(memory_space=pl.ANY)] * len(after),
                out_specs=part,
            ),
            out_shape=jax.ShapeDtypeStruct((slots,) + part_shape, F32),
            compiler_params=params,
            cost_estimate=pl.CostEstimate(flops=1, bytes_accessed=1, transcendentals=0),
            name="rows",
        )(place, columns, row_table, *addends, *after)

    def swap(value, bit):
        return lax.ppermute(value, "gx", [(index, index ^ bit) for index in range(grid_rows)])

    def total(relative, top, first, count, after):
        arrived = []
        bit = 1
        while bit <= top:
            arrived.append(swap(total(relative | bit, bit // 2, first, count, after), bit))
            bit *= 2
        return rows_for(relative, first, count, arrived, after)

    top = grid_rows // 2
    others, last = [], []
    for chunk in range(chunks):
        others.append(total(top | 1, 0, chunk, 1, last) if top == 2 else None)
        last = others[-1:] if top == 2 else []
    crossed, ready = [], []
    for chunk in range(chunks):
        after = others[chunk + 1 : chunk + 2] + ready[-1:]
        if top == 2:
            whole_part = rows_for(top, chunk, 1, [swap(others[chunk], 1)], after)
        else:
            whole_part = total(top, top // 2, chunk, 1, [])
        ready.append(whole_part)
        crossed.append(swap(whole_part, top))
    near = [swap(total(bit, bit // 2, 0, chunks, ready[-1:]), bit) for bit in (1 << n for n in range(top.bit_length() - 1))]
    kept_parts = [rows_for(0, 0, chunks, [], ready[-1:])] + near

    image = None
    shape = (2, planes, 2, per_device // 2, NX // 2)
    for chunk in range(chunks):

        def at_chunk(_, chunk=chunk):
            return (chunk, 0, 0, 0)

        def finish(*refs):
            finish_kernel(planes_padded, len(kept_parts) + 1, refs)

        earlier = [] if image is None else [image]
        image = pl.pallas_call(
            finish,
            grid=(1,),
            out_shape=jax.ShapeDtypeStruct(shape, F32),
            in_specs=[pl.BlockSpec((TILE,) + part_shape, at_chunk)] * len(kept_parts)
            + [
                pl.BlockSpec((TILE,) + part_shape, lambda step: (0, 0, 0, 0)),
                pl.BlockSpec((4 * LANES, NX // 2), lambda step: (0, 0)),
                pl.BlockSpec((1, NX // 2), lambda step: (0, 0)),
                pl.BlockSpec((2, TILE, 1), lambda step, chunk=chunk: (0, chunk, 0)),
                pl.BlockSpec(memory_space=pltpu.SMEM),
            ]
            + [pl.BlockSpec(memory_space=pl.ANY)] * len(earlier),
            out_specs=pl.BlockSpec((2, planes, 2, TILE, NX // 2), lambda step, chunk=chunk: (0, 0, 0, chunk, 0)),
            input_output_aliases={len(kept_parts) + 5: 0} if earlier else {},
            compiler_params=params,
            name="finish",
        )(
            *kept_parts,
            crossed[chunk],
            jnp.asarray(order_tables()),
            deapod_first[None, :],
            deapod_second.reshape(2, per_device // 2, 1),
            deapod_third,
            *earlier,
        )
    return image.reshape(2, planes, per_device, NX // 2)


def solution(mesh):
    in_specs = (
        P(("gx", "gy"), None, None),
        P(("gx", "gy"), None, None, None),
        P(("gx", "gy"), None, None),
        P(("gx", "gy"), None),
        P(("gx", "gy")),
        P(),
        P("gx"),
        P("gy"),
    )
    out_specs = P(None, "gy", "gx", None)
    return jax.shard_map(
        on_device, mesh=mesh, in_specs=in_specs, out_specs=out_specs, check_vma=False
    )
```

```python
import functools
import math

import jax
import jax.numpy as jnp
import ml_dtypes
import numpy as np
from jax import lax
from jax.experimental import pallas as pl
from jax.experimental.pallas import tpu as pltpu
from jax.sharding import PartitionSpec as P

NX = 384
NY = 384
NZ = 384
TILE = 8
LANES = 128
PLANES = 32
Z_CHIPS = 4
PHASES = 128
BF16 = jnp.bfloat16
F32 = jnp.float32
VMEM_LIMIT = 60 * 1024 * 1024


def halves(array):
    high = array.astype(ml_dtypes.bfloat16)
    low = (array - high.astype(np.float64)).astype(ml_dtypes.bfloat16)
    return high, low


def split(value):
    high = value.astype(BF16)
    return high, (value - high.astype(F32)).astype(BF16)


def waves(freq, position, length):
    steps = np.mod(freq[:, None] * position[None, :], length)
    phase = 2.0 * math.pi * steps / length
    return np.cos(phase), np.sin(phase)


def depth_tables(planes):
    matrices, phases = [], []
    lane_part = np.arange(LANES) // 64
    lane_odd = np.arange(LANES) // 32 % 2
    lane_plane = np.arange(LANES) % 32
    used = (lane_plane < planes).astype(np.float64)
    for index in range(NZ // 2 // planes):
        position = index * planes + lane_plane - NZ // 4
        cos, sin = waves(np.arange(TILE) - NZ // 2, position, NZ)
        cos, sin = cos * used / math.sqrt(NZ), sin * used / math.sqrt(NZ)
        real = np.where(lane_part == 0, cos, sin)
        imag = np.where(lane_part == 0, -sin, cos)
        high, low = halves(np.concatenate((real, imag)))
        matrices.append(np.concatenate((high, high, low)))
        cos, sin = waves(np.arange(NZ // TILE), position, NZ // TILE)
        sign = np.where(lane_odd == 1, -1.0, 1.0)[None, :]
        sin = sin * np.where(lane_part == 0, -1.0, 1.0)[None, :]
        phases.append(np.stack((np.concatenate((cos, cos * sign)), np.concatenate((sin, sin * sign)))))
    return np.stack(matrices), np.stack(phases).astype(np.float32)


def padded_rows(per_device):
    return -(-(per_device // 2) // TILE) * TILE


def column_tables(devices, per_device):
    half = NY // 2
    rows = padded_rows(per_device)
    place = np.arange(rows)
    slot = place // 8 * 4 + place % 4
    local = 2 * slot + place % 8 // 4 * (per_device // 2)
    used = (slot < per_device // 4).astype(np.float64)[:, None]
    out = []
    for parity in range(2):
        cos_parts, sin_parts = [], []
        for device in range(devices):
            cos, sin = waves(device * per_device + local + parity - NY // 4, np.arange(half) - half, NY)
            cos_parts.append(cos * used)
            sin_parts.append(sin * used)
        out.append(np.concatenate(halves(np.concatenate(cos_parts + sin_parts) / math.sqrt(NY))))
    return np.stack(out)


def row_tables():
    half = NX // 2
    quarter = NX // 4
    out = []
    for parity in range(2):
        position = 2 * np.arange(quarter) + parity - NX // 4
        cos, sin = waves(np.arange(half) - half, position, NX)
        table = np.zeros((half, 2 * LANES))
        lanes = (np.arange(quarter) + parity * quarter) % LANES
        table[:, lanes] = cos / math.sqrt(NX)
        table[:, LANES + lanes] = sin / math.sqrt(NX)
        out.append(np.stack(halves(table)))
    return np.stack(out)


def order_tables():
    first = np.zeros((LANES, NX // 2))
    second = np.zeros((LANES, NX // 2))
    quarter = NX // 4
    for m1 in range(NX // 2):
        place = m1 // 2 + m1 % 2 * quarter
        if place < LANES:
            first[place, m1] = 1.0
        else:
            second[place - LANES, m1] = 1.0
    return np.concatenate((first, first, second, second)).astype(ml_dtypes.bfloat16)


def divide(value, divisor, limit):
    for shift in range(8, 24):
        factor = (1 << shift) // divisor + 1
        tried = np.arange(limit, dtype=np.int64)
        if factor * limit < 1 << 31 and np.array_equal(tried * factor >> shift, tried // divisor):
            return lax.shift_right_logical(value * factor, shift)
    raise ValueError(divisor)


def spread_kernel(tile_rows, tile_cols, grid_cols, devices, samples_ref, kernel_ref, offsets_ref, owners_ref, ids_ref, out_ref):
    owner, tile_id = owners_ref[...], ids_ref[...]
    tile_depth = NZ // TILE
    tiles_device = tile_rows * tile_cols * tile_depth
    owner_row = divide(owner, grid_cols, devices)
    tile_row = divide(tile_id, tile_cols * tile_depth, tiles_device)
    tile_col = divide(tile_id, tile_depth, tiles_device)
    row = owner_row * tile_rows + tile_row
    col = (owner - owner_row * grid_cols) * tile_cols + tile_col - tile_row * tile_cols
    folds = NX // TILE // 2
    upper = (row >= folds).astype(jnp.int32)
    base = (row - upper * folds) * NY + col
    phase = tile_id - tile_col * tile_depth + upper * tile_depth
    codes = (base * PHASES + phase).astype(F32)

    blocks = samples_ref.shape[0]
    taps = kernel_ref.shape[2]
    cell = lax.broadcasted_iota(jnp.int32, (TILE, LANES), 0)
    left = lax.broadcasted_iota(jnp.int32, (2 * TILE, LANES), 1) < LANES // 2

    def weights(block):
        placed = []
        for dim in range(3):
            shifted = cell - offsets_ref[dim, pl.ds(block, 1), :]
            value = jnp.zeros((TILE, LANES), F32)
            for tap in range(taps):
                value = jnp.where(shifted == tap, kernel_ref[block, dim, pl.ds(tap, 1), :], value)
            placed.append(value)
        plane = jnp.concatenate([placed[0][i : i + 1] * placed[1] for i in range(TILE)], axis=0)
        depth = jnp.concatenate([samples_ref[block, pl.ds(c, 1), :] * placed[2] for c in range(2)], axis=0)
        return depth, plane

    def pair_body(pair, carry):
        depth_a, plane_a = weights(2 * pair)
        depth_b, plane_b = weights(2 * pair + 1)
        depth_high, depth_low = split(jnp.concatenate((depth_a, depth_b), axis=0))
        plane_high, plane_low = split(jnp.concatenate((plane_a, plane_b), axis=0))
        piece = lax.dot_general(
            jnp.concatenate((depth_high, depth_low, depth_high), axis=1),
            jnp.concatenate((plane_high, plane_high, plane_low), axis=1),
            (((1,), (1,)), ((), ())),
            preferred_element_type=F32,
        )
        out_ref[pair] = jnp.where(left, piece[: 2 * TILE], piece[2 * TILE :])
        return carry

    lax.fori_loop(0, blocks // 2, pair_body, 0, unroll=4)
    out_ref[blocks // 2] = jnp.broadcast_to(codes, (2 * TILE, LANES))


def tiles_kernel(arrays, *refs):
    deep_ref = refs[0]
    source_refs = refs[1 : 1 + arrays]
    depth_ref, phases_ref, column_ref, out_ref, tiles_ref, codes_ref, acc_ref, even_ref, odd_ref, arrived = refs[1 + arrays :]
    sources = tiles_ref.shape[0]
    half = NX // 2
    stride = NY
    pairs = tiles_ref.shape[1]
    batch = 8
    rows = column_ref.shape[1] // 4
    width = out_ref.shape[0]

    @pl.when(pl.program_id(0) == 0)
    def _():
        def copies(array, slot):
            ref = source_refs[array]
            return (
                pltpu.make_async_copy(ref.at[pl.ds(0, pairs)], tiles_ref.at[slot], arrived.at[0, slot]),
                pltpu.make_async_copy(ref.at[pairs, pl.ds(0, TILE)], codes_ref.at[slot], arrived.at[1, slot]),
            )

        def start(array, slot):
            for copy in copies(array, slot):
                copy.start()

        chips = Z_CHIPS
        for slot in range(sources):
            array = slot // chips * (2 * chips - 1) + max(2 * (slot % chips) - 1, 0)
            if slot % chips == 0:
                start(array, slot)
            else:
                upper = deep_ref[0] >= slot % chips
                pl.when(upper)(functools.partial(start, array, slot))
                pl.when(jnp.logical_not(upper))(functools.partial(start, array + 1, slot))

        def clear(step, carry):
            acc_ref[pl.ds(pl.multiple_of(step * stride, stride), stride), :] = jnp.zeros((stride, LANES), F32)
            return carry

        lax.fori_loop(0, half, clear, 0)
        for slot in range(sources):
            for copy in copies(0, slot):
                copy.wait()

        batches = pairs // batch
        assert batches % 2 == 0

        def spectrum(source, number, to_ref):
            first = number * batch
            tiles = jnp.concatenate([tiles_ref[source, first + index] for index in range(batch)], axis=1)
            high, low = split(tiles)
            to_ref[...] = lax.dot_general(
                jnp.concatenate((high, low, high), axis=0),
                depth_ref[...],
                (((0,), (0,)), ((), ())),
                preferred_element_type=F32,
            )

        def accumulate(source, number, from_ref):
            for tile in range(2 * batch):
                code = codes_ref[source, 0, number * 2 * batch + tile].astype(jnp.int32)
                base = lax.shift_right_logical(code, 7)
                phase = jnp.bitwise_and(code, PHASES - 1)
                cos = phases_ref[0, pl.ds(phase, 1), :]
                sin = phases_ref[1, pl.ds(phase, 1), :]
                for i in range(TILE):
                    row = tile * TILE * TILE + i * TILE
                    value = from_ref[row : row + TILE, :]
                    value = value * cos + pltpu.roll(value, LANES // 2, 1) * sin
                    at = pl.ds(pl.multiple_of(base * TILE + i * stride, TILE), TILE)
                    acc_ref[at, :] = acc_ref[at, :] + value

        spectrum(0, 0, even_ref)

        def add_pair(step, carry):
            source = step // (batches // 2)
            number = step % (batches // 2) * 2
            spectrum(source, number + 1, odd_ref)
            accumulate(source, number, even_ref)
            later = jnp.minimum(step + 1, sources * batches // 2 - 1)
            spectrum(later // (batches // 2), later % (batches // 2) * 2, even_ref)
            accumulate(source, number + 1, odd_ref)
            return carry

        lax.fori_loop(0, sources * batches // 2, add_pair, 0)

    turn = jnp.where(lax.broadcasted_iota(jnp.int32, (rows, LANES), 1) < LANES // 2, -1.0, 1.0)
    origin = pl.program_id(0) * width

    def columns(step, carry):
        folded = ([], [])
        for side in range(2):
            start = pl.multiple_of((origin + 2 * step + side) * stride, stride)
            lower = acc_ref[pl.ds(start, NY // 2), :]
            upper = acc_ref[pl.ds(start + NY // 2, NY // 2), :]
            folded[0].append(lower + upper)
            folded[1].append(lower - upper)
        for parity in range(2):
            high, low = split(jnp.concatenate(folded[parity], axis=1))
            both = jnp.dot(column_ref[parity], high, preferred_element_type=F32)
            rest = jnp.dot(column_ref[parity, : 2 * rows], low, preferred_element_type=F32)
            product = both[: 2 * rows] + both[2 * rows :] + rest
            for side in range(2):
                lanes = slice(side * LANES, (side + 1) * LANES)
                out_ref[2 * step + side, parity * rows : (parity + 1) * rows, :] = (
                    product[:rows, lanes] + pltpu.roll(product[rows:, lanes], LANES // 2, 1) * turn
                )
        return carry

    lax.fori_loop(0, width // 2, columns, 0, unroll=2)


def rows_kernel(planes_padded, addends, place_ref, in_ref, row_ref, *refs):
    out_ref = refs[-1]
    half = NX // 2
    parity = pl.program_id(1)
    lane = lax.broadcasted_iota(jnp.int32, (PLANES, LANES), 1)
    flat = in_ref.reshape(half * TILE, LANES)
    turned = [flat[pl.ds(row, half, stride=TILE), :].T for row in range(TILE)]
    parts = []
    for odd in range(2):
        at = odd * PLANES
        stacked = [value[part * 64 + at : part * 64 + at + PLANES] for value in turned for part in range(2)]
        high, low = split(jnp.concatenate(stacked, axis=0))
        count = high.shape[0]
        both = jnp.dot(jnp.concatenate((high, low), axis=0), row_ref[odd, 0], preferred_element_type=F32)
        product = both[:count] + both[count:] + jnp.dot(high, row_ref[odd, 1], preferred_element_type=F32)
        sides = []
        for row in range(TILE):
            real = product[2 * row * PLANES : (2 * row + 1) * PLANES]
            imag = product[(2 * row + 1) * PLANES : (2 * row + 2) * PLANES]
            sides.append((real[:, :LANES] - imag[:, LANES:], real[:, LANES:] + imag[:, :LANES]))
        parts.append(sides)
    for slot in range(TILE // 2):
        for part in range(2):
            even = [parts[0][slot + side * TILE // 2][part] for side in range(2)]
            odd = [parts[1][slot + side * TILE // 2][part] for side in range(2)]
            values = [jnp.where(lane < NX // 4, even[side], odd[side]) for side in range(2)]
            values.append(jnp.where(lane < LANES // 2, odd[0], pltpu.roll(odd[1], LANES // 2, 1)))
            for number, value in enumerate(values):
                at = (2 * slot + parity, number, pl.ds(part * planes_padded, planes_padded))
                total = value[:planes_padded]
                for ref in refs[:addends]:
                    total = total + ref[at]
                out_ref[at] = total


def finish_kernel(planes_padded, parts, refs):
    part_refs = refs[:parts]
    order_ref, first_ref, second_ref, third_ref = refs[parts : parts + 4]
    out_ref = refs[-1]
    planes = out_ref.shape[1]
    stride = 6 * planes_padded
    flats = [ref.reshape(TILE * stride, LANES) for ref in part_refs]
    order = order_ref[...]
    for part in range(2):
        for group in range(0, planes, TILE):
            members = range(group, min(group + TILE, planes))
            mains, rests = [], []
            for plane in members:
                values = []
                for number in range(3):
                    at = pl.ds((number * 2 + part) * planes_padded + plane, TILE, stride=stride)
                    total = flats[0][at, :]
                    for flat in flats[1:]:
                        total = total + flat[at, :]
                    values.append(total)
                mains += values[:2]
                rests += [values[2], pltpu.roll(values[2], LANES // 2, 1)]
            main = split(jnp.concatenate(mains, axis=0))
            rest = split(jnp.concatenate(rests, axis=0))
            ordered = jnp.dot(jnp.concatenate(main + rest, axis=1), order, preferred_element_type=F32)
            for index, plane in enumerate(members):
                for side in range(2):
                    row = (2 * index + side) * TILE
                    scale = second_ref[side] * third_ref[plane] * first_ref[...]
                    out_ref[part, plane, side] = ordered[row : row + TILE] * scale


def on_device(samples, kernel, offsets, owners, tile_ids, deapod_first, deapod_second, deapod_third):
    grid_rows = lax.axis_size("gx")
    grid_cols = lax.axis_size("gy")
    blocks = samples.shape[0]
    block_width = samples.shape[2]
    assert block_width == LANES and blocks == LANES
    tile_rows = NX // (TILE * grid_rows)
    tile_cols = NY // (TILE * grid_cols)
    planes = deapod_third.shape[0]
    per_device = deapod_second.shape[0]
    rows = padded_rows(per_device)
    planes_padded = -(-planes // 8) * 8
    vmem = pl.BlockSpec(memory_space=pltpu.VMEM)
    params = pltpu.CompilerParams(vmem_limit_bytes=VMEM_LIMIT)

    tiles = pl.pallas_call(
        functools.partial(spread_kernel, tile_rows, tile_cols, grid_cols, grid_rows * grid_cols),
        out_shape=jax.ShapeDtypeStruct((blocks // 2 + 1, 2 * TILE, LANES), F32),
        in_specs=[vmem] * 5,
        out_specs=vmem,
        compiler_params=params,
        name="spread",
    )(samples, kernel, offsets.transpose(1, 0, 2), owners.reshape(1, blocks), tile_ids.reshape(1, blocks))

    along = grid_cols // Z_CHIPS
    deep_at = lax.div(lax.axis_index("gy").astype(jnp.int32), jnp.int32(along))

    def shift(value, senders, deep, wide):
        moves = [
            (z * along + y, (z + deep) * along + (y + wide) % along) for z in senders for y in range(along)
        ]
        return lax.ppermute(value, "gy", moves)

    held = {0: tiles}
    for steps in range(1, Z_CHIPS):
        held[steps] = shift(held[steps - 1], range(steps - 1, Z_CHIPS - 1), 1, 0)
        held[-steps] = shift(held[1 - steps], range(1, Z_CHIPS + 1 - steps), -1, 0)
    holders = {0: range(Z_CHIPS)}
    for steps in range(1, Z_CHIPS):
        holders[steps] = range(steps, Z_CHIPS)
        holders[-steps] = range(Z_CHIPS - steps)
    crossed_y = {}
    chain = []
    for steps in sorted(held, key=abs):
        for wide in range(1, along):
            value = held[steps]
            if len(chain) > 1:
                value, _ = lax.optimization_barrier((value, chain[-2]))
            crossed_y[steps, wide] = shift(value, holders[steps], 0, wide)
            chain.append(crossed_y[steps, wide])
    gathered = [tiles]
    for wide in range(along):
        def pick(steps):
            return crossed_y[steps, wide] if wide else held[steps]

        if wide:
            gathered.append(pick(0))
        for steps in range(1, Z_CHIPS):
            gathered += [pick(steps), pick(steps - Z_CHIPS)]
    place = lax.axis_index("gx").astype(jnp.int32).reshape(1)
    deep_place = deep_at.reshape(1)
    gy = lax.axis_index("gy")
    matrices, phases = depth_tables(planes)
    matrix = lax.dynamic_index_in_dim(jnp.asarray(matrices), gy, 0, keepdims=False)
    phase_rows = lax.dynamic_index_in_dim(jnp.asarray(phases), gy, 0, keepdims=False)
    column = jnp.asarray(column_tables(grid_rows, per_device))
    def whole(shape):
        return pl.BlockSpec(shape, lambda step: (0,) * len(shape), pipeline_mode=pl.Buffered(1))

    half = NX // 2
    width = 16
    kept = 2 * grid_rows * rows
    spectra = pltpu.VMEM((16 * TILE * TILE, LANES), F32)
    columns = pl.pallas_call(
        functools.partial(tiles_kernel, len(gathered)),
        grid=(half // width,),
        out_shape=jax.ShapeDtypeStruct((half, kept, LANES), F32),
        in_specs=[pl.BlockSpec(memory_space=pltpu.SMEM)]
        + [pl.BlockSpec(memory_space=pl.ANY)] * len(gathered)
        + [whole(array.shape) for array in (matrix, phase_rows, column)],
        out_specs=pl.BlockSpec((width, kept, LANES), lambda step: (step, 0, 0)),
        scratch_shapes=[
            pltpu.VMEM((grid_cols, blocks // 2) + tiles.shape[1:], F32),
            pltpu.SMEM((grid_cols, TILE, LANES), F32),
            pltpu.VMEM((half * NY, LANES), F32),
            spectra,
            spectra,
            pltpu.SemaphoreType.DMA((2, grid_cols)),
        ],
        compiler_params=params,
        name="tiles",
    )(deep_place, *gathered, matrix, phase_rows, column)

    row_table = jnp.asarray(row_tables())
    chunks = rows // TILE
    part_shape = (3, 2 * planes_padded, LANES)

    def rows_for(relative, first, count, addends, after):
        def block(step, parity, place_ref):
            device = jnp.bitwise_xor(place_ref[0], relative)
            return (0, (parity * grid_rows + device) * chunks + first + step, 0)

        part = pl.BlockSpec((TILE,) + part_shape, lambda step, parity, place_ref: (step, 0, 0, 0))
        addend = pl.BlockSpec((TILE,) + part_shape, lambda step, parity, place_ref: (first + step, 0, 0, 0))
        slots = count * TILE

        def body(*refs):
            rows_kernel(planes_padded, len(addends), *refs[: 3 + len(addends)], refs[-1])

        return pl.pallas_call(
            body,
            grid_spec=pltpu.PrefetchScalarGridSpec(
                num_scalar_prefetch=1,
                grid=(count, 2),
                in_specs=[
                    pl.BlockSpec((half, TILE, LANES), block),
                    pl.BlockSpec(row_table.shape, lambda step, parity, place_ref: (0, 0, 0, 0)),
                ]
                + [addend] * len(addends)
                + [pl.BlockSpec(memory_space=pl.ANY)] * len(after),
                out_specs=part,
            ),
            out_shape=jax.ShapeDtypeStruct((slots,) + part_shape, F32),
            compiler_params=params,
            cost_estimate=pl.CostEstimate(flops=1, bytes_accessed=1, transcendentals=0),
            name="rows",
        )(place, columns, row_table, *addends, *after)

    def swap(value, bit):
        return lax.ppermute(value, "gx", [(index, index ^ bit) for index in range(grid_rows)])

    last = []

    def arrivals(relative, top):
        arrived = []
        bit = 1
        while bit <= top:
            part = rows_for(relative | bit, 0, chunks, arrivals(relative | bit, bit // 2), last)
            last[:] = [part]
            arrived.append(swap(part, bit))
            bit *= 2
        return arrived

    top = grid_rows // 2
    far = arrivals(top, top // 2)
    near = arrivals(0, top // 2)
    crossed = []
    for chunk in range(chunks):
        part = rows_for(top, chunk, 1, far, last)
        last[:] = [part]
        crossed.append(swap(part, top))
    kept_parts = [rows_for(0, 0, chunks, [], last)] + near

    image = None
    shape = (2, planes, 2, per_device // 2, NX // 2)
    for chunk in range(chunks):

        def at_chunk(_, chunk=chunk):
            return (chunk, 0, 0, 0)

        def finish(*refs):
            finish_kernel(planes_padded, len(kept_parts) + 1, refs)

        earlier = [] if image is None else [image]
        image = pl.pallas_call(
            finish,
            grid=(1,),
            out_shape=jax.ShapeDtypeStruct(shape, F32),
            in_specs=[pl.BlockSpec((TILE,) + part_shape, at_chunk)] * len(kept_parts)
            + [
                pl.BlockSpec((TILE,) + part_shape, lambda step: (0, 0, 0, 0)),
                pl.BlockSpec((4 * LANES, NX // 2), lambda step: (0, 0)),
                pl.BlockSpec((1, NX // 2), lambda step: (0, 0)),
                pl.BlockSpec((2, TILE, 1), lambda step, chunk=chunk: (0, chunk, 0)),
                pl.BlockSpec(memory_space=pltpu.SMEM),
            ]
            + [pl.BlockSpec(memory_space=pl.ANY)] * len(earlier),
            out_specs=pl.BlockSpec((2, planes, 2, TILE, NX // 2), lambda step, chunk=chunk: (0, 0, 0, chunk, 0)),
            input_output_aliases={len(kept_parts) + 5: 0} if earlier else {},
            compiler_params=params,
            name="finish",
        )(
            *kept_parts,
            crossed[chunk],
            jnp.asarray(order_tables()),
            deapod_first[None, :],
            deapod_second.reshape(2, per_device // 2, 1),
            deapod_third,
            *earlier,
        )
    return image.reshape(2, planes, per_device, NX // 2)


def solution(mesh):
    in_specs = (
        P(("gx", "gy"), None, None),
        P(("gx", "gy"), None, None, None),
        P(("gx", "gy"), None, None),
        P(("gx", "gy"), None),
        P(("gx", "gy")),
        P(),
        P("gx"),
        P("gy"),
    )
    out_specs = P(None, "gy", "gx", None)
    return jax.shard_map(
        on_device, mesh=mesh, in_specs=in_specs, out_specs=out_specs, check_vma=False
    )
```

```python
import functools
import math

import jax
import jax.numpy as jnp
import ml_dtypes
import numpy as np
from jax import lax
from jax.experimental import pallas as pl
from jax.experimental.pallas import tpu as pltpu
from jax.sharding import PartitionSpec as P

NX = 384
NY = 384
NZ = 384
TILE = 8
LANES = 128
PLANES = 32
CHUNK = 24
Z_CHIPS = 4
PHASES = 128
BF16 = jnp.bfloat16
F32 = jnp.float32
VMEM_LIMIT = 60 * 1024 * 1024


def halves(array):
    high = array.astype(ml_dtypes.bfloat16)
    low = (array - high.astype(np.float64)).astype(ml_dtypes.bfloat16)
    return high, low


def split(value):
    high = value.astype(BF16)
    return high, (value - high.astype(F32)).astype(BF16)


def waves(freq, position, length):
    steps = np.mod(freq[:, None] * position[None, :], length)
    phase = 2.0 * math.pi * steps / length
    return np.cos(phase), np.sin(phase)


def depth_tables(planes):
    matrices, phases = [], []
    lane_part = np.arange(LANES) // 64
    lane_odd = np.arange(LANES) // 32 % 2
    lane_plane = np.arange(LANES) % 32
    used = (lane_plane < planes).astype(np.float64)
    for index in range(NZ // 2 // planes):
        position = index * planes + lane_plane - NZ // 4
        cos, sin = waves(np.arange(TILE) - NZ // 2, position, NZ)
        cos, sin = cos * used / math.sqrt(NZ), sin * used / math.sqrt(NZ)
        real = np.where(lane_part == 0, cos, sin)
        imag = np.where(lane_part == 0, -sin, cos)
        high, low = halves(np.concatenate((real, imag)))
        matrices.append(np.concatenate((high, high, low)))
        cos, sin = waves(np.arange(NZ // TILE), position, NZ // TILE)
        sign = np.where(lane_odd == 1, -1.0, 1.0)[None, :]
        sin = sin * np.where(lane_part == 0, -1.0, 1.0)[None, :]
        phases.append(np.stack((np.concatenate((cos, cos * sign)), np.concatenate((sin, sin * sign)))))
    return np.stack(matrices), np.stack(phases).astype(np.float32)


def column_tables():
    third = NY // 3
    out = []
    for residue in range(3):
        cos, sin = waves(3 * np.arange(NY // 6) + residue - NY // 4, np.arange(third) - NY // 2, NY)
        high, low = halves(np.concatenate((cos, sin)) / math.sqrt(NY))
        out.append(np.block([[high, high], [low, np.zeros_like(low)]]))
    return np.stack(out)


def row_tables():
    half = NX // 2
    quarter = NX // 4
    out = []
    for parity in range(2):
        position = 2 * np.arange(quarter) + parity - NX // 4
        cos, sin = waves(np.arange(half) - half, position, NX)
        table = np.zeros((half, 2 * LANES))
        lanes = (np.arange(quarter) + parity * quarter) % LANES
        table[:, lanes] = cos / math.sqrt(NX)
        table[:, LANES + lanes] = sin / math.sqrt(NX)
        out.append(np.stack(halves(table)))
    return np.stack(out)


def order_tables():
    first = np.zeros((LANES, NX // 2))
    second = np.zeros((LANES, NX // 2))
    quarter = NX // 4
    for m1 in range(NX // 2):
        place = m1 // 2 + m1 % 2 * quarter
        if place < LANES:
            first[place, m1] = 1.0
        else:
            second[place - LANES, m1] = 1.0
    return np.concatenate((first, first, second, second)).astype(ml_dtypes.bfloat16)


def divide(value, divisor, limit):
    for shift in range(8, 24):
        factor = (1 << shift) // divisor + 1
        tried = np.arange(limit, dtype=np.int64)
        if factor * limit < 1 << 31 and np.array_equal(tried * factor >> shift, tried // divisor):
            return lax.shift_right_logical(value * factor, shift)
    raise ValueError(divisor)


def spread_kernel(tile_rows, tile_cols, grid_cols, devices, samples_ref, kernel_ref, offsets_ref, owners_ref, ids_ref, out_ref):
    owner, tile_id = owners_ref[...], ids_ref[...]
    tile_depth = NZ // TILE
    tiles_device = tile_rows * tile_cols * tile_depth
    owner_row = divide(owner, grid_cols, devices)
    tile_row = divide(tile_id, tile_cols * tile_depth, tiles_device)
    tile_col = divide(tile_id, tile_depth, tiles_device)
    row = owner_row * tile_rows + tile_row
    col = (owner - owner_row * grid_cols) * tile_cols + tile_col - tile_row * tile_cols
    folds = NX // TILE // 2
    upper = (row >= folds).astype(jnp.int32)
    base = (row - upper * folds) * NY + col
    phase = tile_id - tile_col * tile_depth + upper * tile_depth
    codes = (base * PHASES + phase).astype(F32)

    blocks = samples_ref.shape[0]
    taps = kernel_ref.shape[2]
    cell = lax.broadcasted_iota(jnp.int32, (TILE, LANES), 0)
    left = lax.broadcasted_iota(jnp.int32, (2 * TILE, LANES), 1) < LANES // 2

    def weights(block):
        placed = []
        for dim in range(3):
            shifted = cell - offsets_ref[dim, pl.ds(block, 1), :]
            value = jnp.zeros((TILE, LANES), F32)
            for tap in range(taps):
                value = jnp.where(shifted == tap, kernel_ref[block, dim, pl.ds(tap, 1), :], value)
            placed.append(value)
        plane = jnp.concatenate([placed[0][i : i + 1] * placed[1] for i in range(TILE)], axis=0)
        depth = jnp.concatenate([samples_ref[block, pl.ds(c, 1), :] * placed[2] for c in range(2)], axis=0)
        return depth, plane

    def pair_body(pair, carry):
        depth_a, plane_a = weights(2 * pair)
        depth_b, plane_b = weights(2 * pair + 1)
        depth_high, depth_low = split(jnp.concatenate((depth_a, depth_b), axis=0))
        plane_high, plane_low = split(jnp.concatenate((plane_a, plane_b), axis=0))
        piece = lax.dot_general(
            jnp.concatenate((depth_high, depth_low, depth_high), axis=1),
            jnp.concatenate((plane_high, plane_high, plane_low), axis=1),
            (((1,), (1,)), ((), ())),
            preferred_element_type=F32,
        )
        out_ref[pair] = jnp.where(left, piece[: 2 * TILE], piece[2 * TILE :])
        return carry

    lax.fori_loop(0, blocks // 2, pair_body, 0, unroll=4)
    out_ref[blocks // 2] = jnp.broadcast_to(codes, (2 * TILE, LANES))


def tiles_kernel(arrays, *refs):
    deep_ref = refs[0]
    source_refs = refs[1 : 1 + arrays]
    depth_ref, phases_ref, column_ref, out_ref, tiles_ref, codes_ref, acc_ref, even_ref, odd_ref, arrived = refs[1 + arrays :]
    sources = tiles_ref.shape[0]
    half = NX // 2
    stride = NY
    pairs = tiles_ref.shape[1]
    batch = 8
    rows = column_ref.shape[1] // 4
    width = out_ref.shape[0]

    @pl.when(pl.program_id(0) == 0)
    def _():
        def copies(array, slot):
            ref = source_refs[array]
            return (
                pltpu.make_async_copy(ref.at[pl.ds(0, pairs)], tiles_ref.at[slot], arrived.at[0, slot]),
                pltpu.make_async_copy(ref.at[pairs, pl.ds(0, TILE)], codes_ref.at[slot], arrived.at[1, slot]),
            )

        def start(array, slot):
            for copy in copies(array, slot):
                copy.start()

        chips = Z_CHIPS
        for slot in range(sources):
            array = slot // chips * (2 * chips - 1) + max(2 * (slot % chips) - 1, 0)
            if slot % chips == 0:
                start(array, slot)
            else:
                upper = deep_ref[0] >= slot % chips
                pl.when(upper)(functools.partial(start, array, slot))
                pl.when(jnp.logical_not(upper))(functools.partial(start, array + 1, slot))

        def clear(step, carry):
            acc_ref[pl.ds(pl.multiple_of(step * stride, stride), stride), :] = jnp.zeros((stride, LANES), F32)
            return carry

        lax.fori_loop(0, half, clear, 0)
        for slot in range(sources):
            for copy in copies(0, slot):
                copy.wait()

        batches = pairs // batch
        assert batches % 2 == 0

        def spectrum(source, number, to_ref):
            first = number * batch
            tiles = jnp.concatenate([tiles_ref[source, first + index] for index in range(batch)], axis=1)
            high, low = split(tiles)
            to_ref[...] = lax.dot_general(
                jnp.concatenate((high, low, high), axis=0),
                depth_ref[...],
                (((0,), (0,)), ((), ())),
                preferred_element_type=F32,
            )

        def accumulate(source, number, from_ref):
            for tile in range(2 * batch):
                code = codes_ref[source, 0, number * 2 * batch + tile].astype(jnp.int32)
                base = lax.shift_right_logical(code, 7)
                phase = jnp.bitwise_and(code, PHASES - 1)
                cos = phases_ref[0, pl.ds(phase, 1), :]
                sin = phases_ref[1, pl.ds(phase, 1), :]
                for i in range(TILE):
                    row = tile * TILE * TILE + i * TILE
                    value = from_ref[row : row + TILE, :]
                    value = value * cos + pltpu.roll(value, LANES // 2, 1) * sin
                    at = pl.ds(pl.multiple_of(base * TILE + i * stride, TILE), TILE)
                    acc_ref[at, :] = acc_ref[at, :] + value

        spectrum(0, 0, even_ref)

        def add_pair(step, carry):
            source = step // (batches // 2)
            number = step % (batches // 2) * 2
            spectrum(source, number + 1, odd_ref)
            accumulate(source, number, even_ref)
            later = jnp.minimum(step + 1, sources * batches // 2 - 1)
            spectrum(later // (batches // 2), later % (batches // 2) * 2, even_ref)
            accumulate(source, number + 1, odd_ref)
            return carry

        lax.fori_loop(0, sources * batches // 2, add_pair, 0)

    turn = jnp.where(lax.broadcasted_iota(jnp.int32, (1, LANES), 1) < LANES // 2, -1.0, 1.0)
    origin = pl.program_id(0) * width
    third = NY // 3

    def columns(step, carry):
        folded = ([], [], [])
        for side in range(2):
            start = pl.multiple_of((origin + 2 * step + side) * stride, stride)
            first, second, last = (acc_ref[pl.ds(start + third * part, third), :] for part in range(3))
            both = second + last
            across = pltpu.roll(second - last, LANES // 2, 1) * (turn * math.sqrt(0.75))
            middle = first - 0.5 * both
            folded[0].append(first + both)
            folded[1].append(middle + across)
            folded[2].append(middle - across)
        for residue in range(3):
            high_low = split(jnp.concatenate(folded[residue], axis=1))
            product = jnp.dot(column_ref[residue], jnp.concatenate(high_low, axis=0), preferred_element_type=F32)
            product = product[: 2 * rows] + product[2 * rows :]
            for side in range(2):
                lanes = slice(side * LANES, (side + 1) * LANES)
                out_ref[2 * step + side, residue * rows : (residue + 1) * rows, :] = (
                    product[:rows, lanes] + pltpu.roll(product[rows:, lanes], LANES // 2, 1) * turn
                )
        return carry

    lax.fori_loop(0, width // 2, columns, 0, unroll=2)


def rows_kernel(planes_padded, addends, place_ref, in_ref, row_ref, *refs):
    out_ref = refs[-1]
    half = NX // 2
    residue = pl.program_id(1)
    lane = lax.broadcasted_iota(jnp.int32, (PLANES, LANES), 1)
    flat = in_ref.reshape(half * TILE, LANES)
    turned = [flat[pl.ds(row, half, stride=TILE), :].T for row in range(TILE)]
    parts = []
    for odd in range(2):
        at = odd * PLANES
        stacked = [value[part * 64 + at : part * 64 + at + PLANES] for value in turned for part in range(2)]
        high, low = split(jnp.concatenate(stacked, axis=0))
        count = high.shape[0]
        both = jnp.dot(jnp.concatenate((high, low), axis=0), row_ref[odd, 0], preferred_element_type=F32)
        product = both[:count] + both[count:] + jnp.dot(high, row_ref[odd, 1], preferred_element_type=F32)
        sides = []
        for row in range(TILE):
            real = product[2 * row * PLANES : (2 * row + 1) * PLANES]
            imag = product[(2 * row + 1) * PLANES : (2 * row + 2) * PLANES]
            sides.append((real[:, :LANES] - imag[:, LANES:], real[:, LANES:] + imag[:, :LANES]))
        parts.append(sides)
    for slot in range(TILE // 2):
        for part in range(2):
            even = [parts[0][slot + side * TILE // 2][part] for side in range(2)]
            odd = [parts[1][slot + side * TILE // 2][part] for side in range(2)]
            values = [jnp.where(lane < NX // 4, even[side], odd[side]) for side in range(2)]
            values.append(jnp.where(lane < LANES // 2, odd[0], pltpu.roll(odd[1], LANES // 2, 1)))
            for number, value in enumerate(values):
                at = (3 * slot + residue, number, pl.ds(part * planes_padded, planes_padded))
                total = value[:planes_padded]
                for ref in refs[:addends]:
                    total = total + ref[at]
                out_ref[at] = total


def finish_kernel(planes_padded, parts, refs):
    part_refs = refs[:parts]
    order_ref, first_ref, second_ref, third_ref = refs[parts : parts + 4]
    out_ref = refs[-1]
    planes = out_ref.shape[1]
    slots = part_refs[0].shape[0]
    stride = 6 * planes_padded
    flats = [ref.reshape(slots * stride, LANES) for ref in part_refs]
    order = order_ref[...]
    scale = second_ref[...] * first_ref[...]
    for part in range(2):
        for group in range(0, planes, TILE):
            members = range(group, min(group + TILE, planes))
            mains, rests = [], []
            for plane in members:
                values = []
                for number in range(3):
                    at = pl.ds((number * 2 + part) * planes_padded + plane, slots, stride=stride)
                    total = flats[0][at, :]
                    for flat in flats[1:]:
                        total = total + flat[at, :]
                    values.append(total)
                mains.append(jnp.concatenate(values[:2], axis=0))
                rests.append(jnp.concatenate((values[2], pltpu.roll(values[2], LANES // 2, 1)), axis=0))
            main = split(jnp.concatenate(mains, axis=0))
            rest = split(jnp.concatenate(rests, axis=0))
            ordered = jnp.dot(jnp.concatenate(main + rest, axis=1), order, preferred_element_type=F32)
            for index, plane in enumerate(members):
                out_ref[part, plane] = ordered[index * 2 * slots : (index + 1) * 2 * slots] * (scale * third_ref[plane])


def on_device(samples, kernel, offsets, owners, tile_ids, deapod_first, deapod_second, deapod_third):
    grid_rows = lax.axis_size("gx")
    grid_cols = lax.axis_size("gy")
    blocks = samples.shape[0]
    block_width = samples.shape[2]
    assert block_width == LANES and blocks == LANES
    tile_rows = NX // (TILE * grid_rows)
    tile_cols = NY // (TILE * grid_cols)
    planes = deapod_third.shape[0]
    per_device = deapod_second.shape[0]
    assert per_device % CHUNK == 0
    chunks = per_device // CHUNK
    slots = CHUNK // 2
    planes_padded = -(-planes // 8) * 8
    vmem = pl.BlockSpec(memory_space=pltpu.VMEM)
    params = pltpu.CompilerParams(vmem_limit_bytes=VMEM_LIMIT)

    tiles = pl.pallas_call(
        functools.partial(spread_kernel, tile_rows, tile_cols, grid_cols, grid_rows * grid_cols),
        out_shape=jax.ShapeDtypeStruct((blocks // 2 + 1, 2 * TILE, LANES), F32),
        in_specs=[vmem] * 5,
        out_specs=vmem,
        compiler_params=params,
        name="spread",
    )(samples, kernel, offsets.transpose(1, 0, 2), owners.reshape(1, blocks), tile_ids.reshape(1, blocks))

    along = grid_cols // Z_CHIPS
    deep_at = lax.div(lax.axis_index("gy").astype(jnp.int32), jnp.int32(along))

    def shift(value, senders, deep, wide):
        moves = [
            (z * along + y, (z + deep) * along + (y + wide) % along) for z in senders for y in range(along)
        ]
        return lax.ppermute(value, "gy", moves)

    held = {0: tiles}
    for steps in range(1, Z_CHIPS):
        held[steps] = shift(held[steps - 1], range(steps - 1, Z_CHIPS - 1), 1, 0)
        held[-steps] = shift(held[1 - steps], range(1, Z_CHIPS + 1 - steps), -1, 0)
    holders = {0: range(Z_CHIPS)}
    for steps in range(1, Z_CHIPS):
        holders[steps] = range(steps, Z_CHIPS)
        holders[-steps] = range(Z_CHIPS - steps)
    crossed_y = {}
    chain = []
    for steps in sorted(held, key=abs):
        for wide in range(1, along):
            value = held[steps]
            if len(chain) > 1:
                value, _ = lax.optimization_barrier((value, chain[-2]))
            crossed_y[steps, wide] = shift(value, holders[steps], 0, wide)
            chain.append(crossed_y[steps, wide])
    gathered = [tiles]
    for wide in range(along):
        def pick(steps):
            return crossed_y[steps, wide] if wide else held[steps]

        if wide:
            gathered.append(pick(0))
        for steps in range(1, Z_CHIPS):
            gathered += [pick(steps), pick(steps - Z_CHIPS)]
    place = lax.axis_index("gx").astype(jnp.int32).reshape(1)
    deep_place = deep_at.reshape(1)
    gy = lax.axis_index("gy")
    matrices, phases = depth_tables(planes)
    matrix = lax.dynamic_index_in_dim(jnp.asarray(matrices), gy, 0, keepdims=False)
    phase_rows = lax.dynamic_index_in_dim(jnp.asarray(phases), gy, 0, keepdims=False)
    column = jnp.asarray(column_tables())
    def whole(shape):
        return pl.BlockSpec(shape, lambda step: (0,) * len(shape), pipeline_mode=pl.Buffered(1))

    half = NX // 2
    width = 16
    kept = NY // 2
    spectra = pltpu.VMEM((16 * TILE * TILE, LANES), F32)
    columns = pl.pallas_call(
        functools.partial(tiles_kernel, len(gathered)),
        grid=(half // width,),
        out_shape=jax.ShapeDtypeStruct((half, kept, LANES), F32),
        in_specs=[pl.BlockSpec(memory_space=pltpu.SMEM)]
        + [pl.BlockSpec(memory_space=pl.ANY)] * len(gathered)
        + [whole(array.shape) for array in (matrix, phase_rows, column)],
        out_specs=pl.BlockSpec((width, kept, LANES), lambda step: (step, 0, 0)),
        scratch_shapes=[
            pltpu.VMEM((grid_cols, blocks // 2) + tiles.shape[1:], F32),
            pltpu.SMEM((grid_cols, TILE, LANES), F32),
            pltpu.VMEM((half * NY, LANES), F32),
            spectra,
            spectra,
            pltpu.SemaphoreType.DMA((2, grid_cols)),
        ],
        compiler_params=params,
        name="tiles",
    )(deep_place, *gathered, matrix, phase_rows, column)

    row_table = jnp.asarray(row_tables())
    part_shape = (3, 2 * planes_padded, LANES)

    def rows_for(relative, first, count, addends, after):
        def block(step, residue, place_ref):
            device = jnp.bitwise_xor(place_ref[0], relative)
            return (0, (residue * grid_rows + device) * chunks + first + step, 0)

        part = pl.BlockSpec((slots,) + part_shape, lambda step, residue, place_ref: (step, 0, 0, 0))
        addend = pl.BlockSpec((slots,) + part_shape, lambda step, residue, place_ref: (first + step, 0, 0, 0))

        def body(*refs):
            rows_kernel(planes_padded, len(addends), *refs[: 3 + len(addends)], refs[-1])

        return pl.pallas_call(
            body,
            grid_spec=pltpu.PrefetchScalarGridSpec(
                num_scalar_prefetch=1,
                grid=(count, 3),
                in_specs=[
                    pl.BlockSpec((half, TILE, LANES), block),
                    pl.BlockSpec(row_table.shape, lambda step, residue, place_ref: (0, 0, 0, 0)),
                ]
                + [addend] * len(addends)
                + [pl.BlockSpec(memory_space=pl.ANY)] * len(after),
                out_specs=part,
            ),
            out_shape=jax.ShapeDtypeStruct((count * slots,) + part_shape, F32),
            compiler_params=params,
            cost_estimate=pl.CostEstimate(flops=1, bytes_accessed=1, transcendentals=0),
            name="rows",
        )(place, columns, row_table, *addends, *after)

    def swap(value, bit):
        return lax.ppermute(value, "gx", [(index, index ^ bit) for index in range(grid_rows)])

    last = []

    def rows_next(relative, first, count, addends):
        part = rows_for(relative, first, count, addends, last)
        last[:] = [part]
        return part

    def arrivals(relative, top):
        arrived = []
        bit = 1
        while bit <= top:
            arrived.append(swap(rows_next(relative | bit, 0, chunks, arrivals(relative | bit, bit // 2)), bit))
            bit *= 2
        return arrived

    top = grid_rows // 2
    far = arrivals(top, top // 2)
    near = arrivals(0, top // 2)
    crossed = [swap(rows_next(top, chunk, 1, far), top) for chunk in range(chunks)]
    kept_parts = [rows_next(0, 0, chunks, [])] + near

    image = None
    for chunk in range(chunks):

        def finish(*refs):
            finish_kernel(planes_padded, len(kept_parts) + 1, refs)

        earlier = [] if image is None else [image]
        image = pl.pallas_call(
            finish,
            grid=(1,),
            out_shape=jax.ShapeDtypeStruct((2, planes, per_device, NX // 2), F32),
            in_specs=[pl.BlockSpec((slots,) + part_shape, lambda step, chunk=chunk: (chunk, 0, 0, 0))] * len(kept_parts)
            + [
                pl.BlockSpec((slots,) + part_shape, lambda step: (0, 0, 0, 0)),
                pl.BlockSpec((4 * LANES, NX // 2), lambda step: (0, 0)),
                pl.BlockSpec((1, NX // 2), lambda step: (0, 0)),
                pl.BlockSpec((CHUNK, 1), lambda step, chunk=chunk: (chunk, 0)),
                pl.BlockSpec(memory_space=pltpu.SMEM),
            ]
            + [pl.BlockSpec(memory_space=pl.ANY)] * len(earlier),
            out_specs=pl.BlockSpec((2, planes, CHUNK, NX // 2), lambda step, chunk=chunk: (0, 0, chunk, 0)),
            input_output_aliases={len(kept_parts) + 5: 0} if earlier else {},
            compiler_params=params,
            name="finish",
        )(
            *kept_parts,
            crossed[chunk],
            jnp.asarray(order_tables()),
            deapod_first[None, :],
            deapod_second[:, None],
            deapod_third,
            *earlier,
        )
    return image


def solution(mesh):
    in_specs = (
        P(("gx", "gy"), None, None),
        P(("gx", "gy"), None, None, None),
        P(("gx", "gy"), None, None),
        P(("gx", "gy"), None),
        P(("gx", "gy")),
        P(),
        P("gx"),
        P("gy"),
    )
    out_specs = P(None, "gy", "gx", None)
    return jax.shard_map(
        on_device, mesh=mesh, in_specs=in_specs, out_specs=out_specs, check_vma=False
    )
```

```python
import functools
import math

import jax
import jax.numpy as jnp
import ml_dtypes
import numpy as np
from jax import lax
from jax.experimental import pallas as pl
from jax.experimental.pallas import tpu as pltpu
from jax.sharding import PartitionSpec as P

NX = 384
NY = 384
NZ = 384
TILE = 8
LANES = 128
PLANES = 32
CHUNK = 24
Z_CHIPS = 4
PHASES = 128
BF16 = jnp.bfloat16
F32 = jnp.float32
VMEM_LIMIT = 8 * 1024 * 1024


def halves(array):
    high = array.astype(ml_dtypes.bfloat16)
    low = (array - high.astype(np.float64)).astype(ml_dtypes.bfloat16)
    return high, low


def split(value):
    high = value.astype(BF16)
    return high, (value - high.astype(F32)).astype(BF16)


def waves(freq, position, length):
    steps = np.mod(freq[:, None] * position[None, :], length)
    phase = 2.0 * math.pi * steps / length
    return np.cos(phase), np.sin(phase)


def depth_tables(planes):
    matrices, phases = [], []
    lane_part = np.arange(LANES) // 64
    lane_odd = np.arange(LANES) // 32 % 2
    lane_plane = np.arange(LANES) % 32
    used = (lane_plane < planes).astype(np.float64)
    for index in range(NZ // 2 // planes):
        position = index * planes + lane_plane - NZ // 4
        cos, sin = waves(np.arange(TILE) - NZ // 2, position, NZ)
        cos, sin = cos * used / math.sqrt(NZ), sin * used / math.sqrt(NZ)
        real = np.where(lane_part == 0, cos, sin)
        imag = np.where(lane_part == 0, -sin, cos)
        high, low = halves(np.concatenate((real, imag)))
        matrices.append(np.concatenate((high, high, low)))
        cos, sin = waves(np.arange(NZ // TILE), position, NZ // TILE)
        sign = np.where(lane_odd == 1, -1.0, 1.0)[None, :]
        sin = sin * np.where(lane_part == 0, -1.0, 1.0)[None, :]
        phases.append(np.stack((np.concatenate((cos, cos * sign)), np.concatenate((sin, sin * sign)))))
    return np.stack(matrices), np.stack(phases).astype(np.float32)


def column_tables():
    third = NY // 3
    out = []
    for residue in range(3):
        cos, sin = waves(3 * np.arange(NY // 6) + residue - NY // 4, np.arange(third) - NY // 2, NY)
        high, low = halves(np.concatenate((cos, sin)) / math.sqrt(NY))
        out.append(np.block([[high, high], [low, np.zeros_like(low)]]))
    return np.stack(out)


def row_tables():
    half = NX // 2
    freq = np.arange(half).reshape(-1, 2, TILE // 2).transpose(1, 0, 2).reshape(-1) - half
    quarter = NX // 4
    out = []
    for parity in range(2):
        position = 2 * np.arange(quarter) + parity - NX // 4
        cos, sin = waves(freq, position, NX)
        table = np.zeros((half, 2 * LANES))
        lanes = (np.arange(quarter) + parity * quarter) % LANES
        table[:, lanes] = cos / math.sqrt(NX)
        table[:, LANES + lanes] = sin / math.sqrt(NX)
        out.append(np.stack(halves(table)))
    return np.stack(out)


def order_tables():
    first = np.zeros((LANES, NX // 2))
    second = np.zeros((LANES, NX // 2))
    quarter = NX // 4
    for m1 in range(NX // 2):
        place = m1 // 2 + m1 % 2 * quarter
        if place < LANES:
            first[place, m1] = 1.0
        else:
            second[place - LANES, m1] = 1.0
    return np.concatenate((first, first, second, second)).astype(ml_dtypes.bfloat16)


def divide(value, divisor, limit):
    for shift in range(8, 24):
        factor = (1 << shift) // divisor + 1
        tried = np.arange(limit, dtype=np.int64)
        if factor * limit < 1 << 31 and np.array_equal(tried * factor >> shift, tried // divisor):
            return lax.shift_right_logical(value * factor, shift)
    raise ValueError(divisor)


def spread_kernel(tile_rows, tile_cols, grid_cols, devices, samples_ref, kernel_ref, offsets_ref, owners_ref, ids_ref, out_ref):
    owner, tile_id = owners_ref[...], ids_ref[...]
    tile_depth = NZ // TILE
    tiles_device = tile_rows * tile_cols * tile_depth
    owner_row = divide(owner, grid_cols, devices)
    tile_row = divide(tile_id, tile_cols * tile_depth, tiles_device)
    tile_col = divide(tile_id, tile_depth, tiles_device)
    row = owner_row * tile_rows + tile_row
    col = (owner - owner_row * grid_cols) * tile_cols + tile_col - tile_row * tile_cols
    folds = NX // TILE // 2
    upper = (row >= folds).astype(jnp.int32)
    base = (row - upper * folds) * (NY // 2) + col
    phase = tile_id - tile_col * tile_depth + upper * tile_depth
    codes = (base * PHASES + phase).astype(F32)

    blocks = samples_ref.shape[0]
    taps = kernel_ref.shape[2]
    cell = lax.broadcasted_iota(jnp.int32, (TILE, LANES), 0)
    left = lax.broadcasted_iota(jnp.int32, (2 * TILE, LANES), 1) < LANES // 2

    def weights(block):
        placed = []
        for dim in range(3):
            shifted = cell - offsets_ref[dim, pl.ds(block, 1), :]
            value = jnp.zeros((TILE, LANES), F32)
            for tap in range(taps):
                value = jnp.where(shifted == tap, kernel_ref[block, dim, pl.ds(tap, 1), :], value)
            placed.append(value)
        plane = jnp.concatenate([placed[0][i : i + 1] * placed[1] for i in range(TILE)], axis=0)
        depth = jnp.concatenate([samples_ref[block, pl.ds(c, 1), :] * placed[2] for c in range(2)], axis=0)
        return depth, plane

    def pair_body(pair, carry):
        depth_a, plane_a = weights(2 * pair)
        depth_b, plane_b = weights(2 * pair + 1)
        depth_high, depth_low = split(jnp.concatenate((depth_a, depth_b), axis=0))
        plane_high, plane_low = split(jnp.concatenate((plane_a, plane_b), axis=0))
        piece = lax.dot_general(
            jnp.concatenate((depth_high, depth_low, depth_high), axis=1),
            jnp.concatenate((plane_high, plane_high, plane_low), axis=1),
            (((1,), (1,)), ((), ())),
            preferred_element_type=F32,
        )
        out_ref[pair] = jnp.where(left, piece[: 2 * TILE], piece[2 * TILE :])
        return carry

    lax.fori_loop(0, blocks // 2, pair_body, 0, unroll=4)
    out_ref[blocks // 2] = jnp.broadcast_to(codes, (2 * TILE, LANES))


def tiles_kernel(conditions, first, *refs):
    arrays = len(conditions)
    deep_ref = refs[0]
    source_refs = refs[1 : 1 + arrays]
    depth_ref, phases_ref = refs[1 + arrays : 3 + arrays]
    low_ref, high_ref, token_ref, codes_ref, even_ref, odd_ref, arrived = refs[-7:]
    token_ref[...] = jnp.zeros_like(token_ref)
    stride = NY
    pairs = source_refs[0].shape[0] - 1
    batch = 8
    batches = pairs // batch
    assert batches % 2 == 0

    def copies(index):
        return pltpu.make_async_copy(
            source_refs[index].at[pairs, pl.ds(0, TILE)], codes_ref.at[index], arrived.at[index]
        )

    for index in range(arrays):
        copies(index).start()

    if first:

        def clear(step, carry):
            at = pl.ds(pl.multiple_of(step * stride, stride), stride)
            low_ref[at, :] = jnp.zeros((stride, LANES), F32)
            high_ref[at, :] = jnp.zeros((stride, LANES), F32)
            return carry

        lax.fori_loop(0, NX // 4, clear, 0)

    for index in range(arrays):
        copies(index).wait()

    def add_source(index):
        tiles_ref = source_refs[index]

        def spectrum(number, to_ref):
            tiles = jnp.concatenate([tiles_ref[number * batch + place] for place in range(batch)], axis=1)
            high, low = split(tiles)
            to_ref[...] = lax.dot_general(
                jnp.concatenate((high, low, high), axis=0),
                depth_ref[...],
                (((0,), (0,)), ((), ())),
                preferred_element_type=F32,
            )

        def accumulate(number, from_ref):
            for tile in range(2 * batch):
                code = codes_ref[index, 0, number * 2 * batch + tile].astype(jnp.int32)
                base = lax.shift_right_logical(code, 7)
                phase = jnp.bitwise_and(code, PHASES - 1)
                cos = phases_ref[0, pl.ds(phase, 1), :]
                sin = phases_ref[1, pl.ds(phase, 1), :]
                for i in range(TILE):
                    row = tile * TILE * TILE + i * TILE
                    value = from_ref[row : row + TILE, :]
                    value = value * cos + pltpu.roll(value, LANES // 2, 1) * sin
                    acc_ref = high_ref if i >= TILE // 2 else low_ref
                    at = pl.ds(pl.multiple_of(base * TILE + i % (TILE // 2) * stride, TILE), TILE)
                    acc_ref[at, :] = acc_ref[at, :] + value

        spectrum(0, even_ref)

        def add_pair(step, carry):
            number = 2 * step
            spectrum(number + 1, odd_ref)
            accumulate(number, even_ref)
            spectrum(jnp.minimum(number + 2, batches - 2), even_ref)
            accumulate(number + 1, odd_ref)
            return carry

        lax.fori_loop(0, batches // 2, add_pair, 0)

    for index, condition in enumerate(conditions):
        if condition is None:
            add_source(index)
        else:
            side, depth = condition
            holds = deep_ref[0] >= depth if side == "from" else deep_ref[0] < depth
            pl.when(holds)(functools.partial(add_source, index))


def columns_kernel(low_in, high_in, column_ref, low_ref, high_ref):
    del low_in, high_in
    stride = NY
    third = NY // 3
    rows = column_ref.shape[1] // 4
    turn = jnp.where(lax.broadcasted_iota(jnp.int32, (1, LANES), 1) < LANES // 2, -1.0, 1.0)

    def columns(step, carry):
        start = pl.multiple_of(step * stride, stride)
        folded = ([], [], [])
        for ref in (low_ref, high_ref):
            first, second, last = (ref[pl.ds(start + third * part, third), :] for part in range(3))
            both = second + last
            across = pltpu.roll(second - last, LANES // 2, 1) * (turn * math.sqrt(0.75))
            middle = first - 0.5 * both
            folded[0].append(first + both)
            folded[1].append(middle + across)
            folded[2].append(middle - across)
        for residue in range(3):
            high_low = split(jnp.concatenate(folded[residue], axis=1))
            product = jnp.dot(column_ref[residue], jnp.concatenate(high_low, axis=0), preferred_element_type=F32)
            product = product[: 2 * rows] + product[2 * rows :]
            for side, ref in enumerate((low_ref, high_ref)):
                lanes = slice(side * LANES, (side + 1) * LANES)
                ref[pl.ds(start + residue * rows, rows), :] = (
                    product[:rows, lanes] + pltpu.roll(product[rows:, lanes], LANES // 2, 1) * turn
                )
        return carry

    lax.fori_loop(0, NX // 4, columns, 0, unroll=2)


def rows_kernel(relative, first, count, chunks, grid_rows, addends, planes_padded, place_ref, low_ref, high_ref, row_ref, *refs):
    out_ref = refs[-1]
    rows = grid_rows * chunks * TILE
    device = jnp.bitwise_xor(place_ref[0], relative)
    lane = lax.broadcasted_iota(jnp.int32, (PLANES, LANES), 1)

    def block(step, carry):
        chunk, residue = step // 3, step % 3
        start = residue * rows + (device * chunks + first + chunk) * TILE
        turned = []
        for row in range(TILE):
            at = pl.ds(start + row, NX // 4, stride=NY)
            turned.append(jnp.concatenate((low_ref[at, :], high_ref[at, :]), axis=0).T)
        parts = []
        for odd in range(2):
            at = odd * PLANES
            stacked = [value[part * 64 + at : part * 64 + at + PLANES] for value in turned for part in range(2)]
            high, low = split(jnp.concatenate(stacked, axis=0))
            size = high.shape[0]
            both = jnp.dot(jnp.concatenate((high, low), axis=0), row_ref[odd, 0], preferred_element_type=F32)
            product = both[:size] + both[size:] + jnp.dot(high, row_ref[odd, 1], preferred_element_type=F32)
            sides = []
            for row in range(TILE):
                real = product[2 * row * PLANES : (2 * row + 1) * PLANES]
                imag = product[(2 * row + 1) * PLANES : (2 * row + 2) * PLANES]
                sides.append((real[:, :LANES] - imag[:, LANES:], real[:, LANES:] + imag[:, :LANES]))
            parts.append(sides)
        for slot in range(TILE // 2):
            place = chunk * (CHUNK // 2) + 3 * slot + residue
            for part in range(2):
                even = [parts[0][slot + side * TILE // 2][part] for side in range(2)]
                odd = [parts[1][slot + side * TILE // 2][part] for side in range(2)]
                values = [jnp.where(lane < NX // 4, even[side], odd[side]) for side in range(2)]
                values.append(jnp.where(lane < LANES // 2, odd[0], pltpu.roll(odd[1], LANES // 2, 1)))
                for number, value in enumerate(values):
                    planes = pl.ds(part * planes_padded, planes_padded)
                    total = value[:planes_padded]
                    for ref in refs[:addends]:
                        total = total + ref[first * (CHUNK // 2) + place, number, planes]
                    out_ref[place, number, planes] = total
        return carry

    lax.fori_loop(0, 3 * count, block, 0)


def finish_kernel(planes_padded, parts, refs):
    part_refs = refs[:parts]
    order_ref, first_ref, second_ref, third_ref = refs[parts : parts + 4]
    out_ref = refs[-1]
    planes = out_ref.shape[1]
    slots = part_refs[0].shape[0]
    stride = 6 * planes_padded
    flats = [ref.reshape(slots * stride, LANES) for ref in part_refs]
    order = order_ref[...]
    scale = second_ref[...] * first_ref[...]
    for part in range(2):
        for group in range(0, planes, TILE):
            members = range(group, min(group + TILE, planes))
            mains, rests = [], []
            for plane in members:
                values = []
                for number in range(3):
                    at = pl.ds((number * 2 + part) * planes_padded + plane, slots, stride=stride)
                    total = flats[0][at, :]
                    for flat in flats[1:]:
                        total = total + flat[at, :]
                    values.append(total)
                mains.append(jnp.concatenate(values[:2], axis=0))
                rests.append(jnp.concatenate((values[2], pltpu.roll(values[2], LANES // 2, 1)), axis=0))
            main = split(jnp.concatenate(mains, axis=0))
            rest = split(jnp.concatenate(rests, axis=0))
            ordered = jnp.dot(jnp.concatenate(main + rest, axis=1), order, preferred_element_type=F32)
            for index, plane in enumerate(members):
                out_ref[part, plane] = ordered[index * 2 * slots : (index + 1) * 2 * slots] * (scale * third_ref[plane])


def on_device(samples, kernel, offsets, owners, tile_ids, deapod_first, deapod_second, deapod_third):
    grid_rows = lax.axis_size("gx")
    grid_cols = lax.axis_size("gy")
    blocks = samples.shape[0]
    block_width = samples.shape[2]
    assert block_width == LANES and blocks == LANES
    tile_rows = NX // (TILE * grid_rows)
    tile_cols = NY // (TILE * grid_cols)
    planes = deapod_third.shape[0]
    per_device = deapod_second.shape[0]
    assert per_device % CHUNK == 0
    chunks = per_device // CHUNK
    slots = CHUNK // 2
    planes_padded = -(-planes // 8) * 8
    vmem = pl.BlockSpec(memory_space=pltpu.VMEM)
    params = pltpu.CompilerParams(vmem_limit_bytes=VMEM_LIMIT)

    tiles = pl.pallas_call(
        functools.partial(spread_kernel, tile_rows, tile_cols, grid_cols, grid_rows * grid_cols),
        out_shape=pltpu.HBM((blocks // 2 + 1, 2 * TILE, LANES), F32),
        in_specs=[vmem] * 5,
        out_specs=vmem,
        compiler_params=params,
        name="spread",
    )(samples, kernel, offsets.transpose(1, 0, 2), owners.reshape(1, blocks), tile_ids.reshape(1, blocks))

    along = grid_cols // Z_CHIPS
    deep_at = lax.div(lax.axis_index("gy").astype(jnp.int32), jnp.int32(along))

    def shift(value, senders, deep, wide):
        moves = [
            (z * along + y, (z + deep) * along + (y + wide) % along) for z in senders for y in range(along)
        ]
        return lax.ppermute(value, "gy", moves)

    place = lax.axis_index("gx").astype(jnp.int32).reshape(1)
    deep_place = deep_at.reshape(1)
    gy = lax.axis_index("gy")
    matrices, phases = depth_tables(planes)
    matrix = lax.dynamic_index_in_dim(jnp.asarray(matrices), gy, 0, keepdims=False)
    phase_rows = lax.dynamic_index_in_dim(jnp.asarray(phases), gy, 0, keepdims=False)
    column = jnp.asarray(column_tables())
    half = NX // 2
    smem = pl.BlockSpec(memory_space=pltpu.SMEM)
    acc_shape = (half // 2 * NY, LANES)

    def in_vmem(arrays):
        return [pltpu.with_memory_space_constraint(array, pltpu.VMEM) for array in arrays]

    def in_hbm(arrays):
        return [pltpu.with_memory_space_constraint(array, pltpu.HBM) for array in arrays]

    def condition(steps):
        if steps == 0:
            return None
        return ("from", steps) if steps > 0 else ("below", Z_CHIPS + steps)

    def add_tiles(sources, acc):
        conditions = [condition(steps) for steps, _ in sources]
        spectra = pltpu.VMEM((16 * TILE * TILE, LANES), F32)
        kept = [jax.ShapeDtypeStruct(acc_shape, F32)] * 2 if acc else [pltpu.VMEM(acc_shape, F32)] * 2
        inputs = len(sources) + 3
        *acc, token = pl.pallas_call(
            functools.partial(tiles_kernel, conditions, not acc),
            out_shape=kept + [jax.ShapeDtypeStruct((TILE, LANES), F32)],
            in_specs=[smem] + [vmem] * (inputs - 1 + len(acc)),
            out_specs=[vmem] * 3,
            input_output_aliases={inputs: 0, inputs + 1: 1} if acc else {},
            scratch_shapes=[
                pltpu.SMEM((len(sources), TILE, LANES), F32),
                spectra,
                spectra,
                pltpu.SemaphoreType.DMA((len(sources),)),
            ],
            compiler_params=params,
            cost_estimate=pl.CostEstimate(flops=0, bytes_accessed=len(sources) << 23, transcendentals=0),
            name="tiles",
        )(deep_place, *in_hbm([array for _, array in sources] + [matrix, phase_rows]), *in_vmem(acc))
        return acc, token

    def after(value, token):
        return lax.optimization_barrier((value, token))[0]

    held, crossed_y = {0: tiles}, {}
    acc, waiting = [], [(0, tiles)]
    token = None
    for steps in range(1, Z_CHIPS + 1):
        if steps < Z_CHIPS:
            for signed in (steps, -steps):
                value = held[signed - signed // steps]
                value = value if token is None else after(value, token)
                senders = range(steps - 1, Z_CHIPS - 1) if signed > 0 else range(1, Z_CHIPS + 1 - steps)
                held[signed] = shift(value, senders, signed // steps, 0)
        behind = []
        for signed in sorted({steps - 1, 1 - steps}):
            holders = range(signed, Z_CHIPS) if signed >= 0 else range(Z_CHIPS + signed)
            for wide in range(1, along):
                value = held[signed] if token is None else after(held[signed], token)
                crossed_y[signed, wide] = shift(value, holders, 0, wide)
                behind.append((signed, crossed_y[signed, wide]))
        acc, token = add_tiles(waiting, acc)
        waiting = behind
        if steps < Z_CHIPS:
            waiting = [(steps, held[steps]), (-steps, held[-steps])] + behind
    acc, _ = add_tiles(waiting, acc)

    acc = pl.pallas_call(
        columns_kernel,
        out_shape=[jax.ShapeDtypeStruct(acc_shape, F32)] * 2,
        in_specs=[vmem] * 3,
        out_specs=[vmem] * 2,
        input_output_aliases={0: 0, 1: 1},
        compiler_params=params,
        name="columns",
    )(*in_vmem(acc), *in_hbm([column]))

    row_table = jnp.asarray(row_tables())
    part_shape = (3, 2 * planes_padded, LANES)

    def rows_for(relative, first, count, addends, after):
        def body(*refs):
            operands = 4 + len(addends)
            rows_kernel(
                relative, first, count, chunks, grid_rows, len(addends), planes_padded, *refs[:operands], refs[-1]
            )

        return pl.pallas_call(
            body,
            in_specs=[smem] + [vmem] * (3 + len(addends)) + [pl.BlockSpec(memory_space=pl.ANY)] * len(after),
            out_specs=vmem,
            out_shape=pltpu.HBM((count * slots,) + part_shape, F32),
            compiler_params=params,
            cost_estimate=pl.CostEstimate(flops=1, bytes_accessed=1, transcendentals=0),
            name="rows",
        )(place, *in_vmem(acc), *in_hbm([row_table] + addends + after))

    def swap(value, bit):
        return lax.ppermute(value, "gx", [(index, index ^ bit) for index in range(grid_rows)])

    last = []

    def rows_next(relative, first, count, addends):
        part = rows_for(relative, first, count, addends, last)
        last[:] = [part]
        return part

    def arrivals(relative, top):
        arrived = []
        bit = 1
        while bit <= top:
            arrived.append(swap(rows_next(relative | bit, 0, chunks, arrivals(relative | bit, bit // 2)), bit))
            bit *= 2
        return arrived

    top = grid_rows // 2
    far = arrivals(top, top // 2)
    near = arrivals(0, top // 2)
    crossed = [swap(rows_next(top, chunk, 1, far), top) for chunk in range(chunks)]
    kept_parts = [rows_next(0, 0, chunks, [])] + near

    image = None
    for chunk in range(chunks):

        def finish(*refs):
            finish_kernel(planes_padded, len(kept_parts) + 1, refs)

        earlier = [] if image is None else [image]
        image = pl.pallas_call(
            finish,
            grid=(1,),
            out_shape=jax.ShapeDtypeStruct((2, planes, per_device, NX // 2), F32),
            in_specs=[pl.BlockSpec((slots,) + part_shape, lambda step, chunk=chunk: (chunk, 0, 0, 0))] * len(kept_parts)
            + [
                pl.BlockSpec((slots,) + part_shape, lambda step: (0, 0, 0, 0)),
                pl.BlockSpec((4 * LANES, NX // 2), lambda step: (0, 0)),
                pl.BlockSpec((1, NX // 2), lambda step: (0, 0)),
                pl.BlockSpec((CHUNK, 1), lambda step, chunk=chunk: (chunk, 0)),
                pl.BlockSpec(memory_space=pltpu.SMEM),
            ]
            + [pl.BlockSpec(memory_space=pl.ANY)] * len(earlier),
            out_specs=pl.BlockSpec((2, planes, CHUNK, NX // 2), lambda step, chunk=chunk: (0, 0, chunk, 0)),
            input_output_aliases={len(kept_parts) + 5: 0} if earlier else {},
            compiler_params=params,
            name="finish",
        )(
            *in_hbm(kept_parts + [crossed[chunk]]),
            jnp.asarray(order_tables()),
            deapod_first[None, :],
            deapod_second[:, None],
            deapod_third,
            *earlier,
        )
    return image


def solution(mesh):
    in_specs = (
        P(("gx", "gy"), None, None),
        P(("gx", "gy"), None, None, None),
        P(("gx", "gy"), None, None),
        P(("gx", "gy"), None),
        P(("gx", "gy")),
        P(),
        P("gx"),
        P("gy"),
    )
    out_specs = P(None, "gy", "gx", None)
    return jax.shard_map(
        on_device, mesh=mesh, in_specs=in_specs, out_specs=out_specs, check_vma=False
    )
```

```python
import functools
import math

import jax
import jax.numpy as jnp
import ml_dtypes
import numpy as np
from jax import lax
from jax.experimental import pallas as pl
from jax.experimental.pallas import tpu as pltpu
from jax.sharding import PartitionSpec as P

NX = 384
NY = 384
NZ = 384
TILE = 8
LANES = 128
PLANES = 32
CHUNK = 24
Z_CHIPS = 4
PARTS = 4
CELLS = TILE // PARTS
STRIDE = NY + TILE
PHASES = 128
BF16 = jnp.bfloat16
F32 = jnp.float32
VMEM_LIMIT = 8 * 1024 * 1024


def halves(array):
    high = array.astype(ml_dtypes.bfloat16)
    low = (array - high.astype(np.float64)).astype(ml_dtypes.bfloat16)
    return high, low


def split(value):
    high = value.astype(BF16)
    return high, (value - high.astype(F32)).astype(BF16)


def waves(freq, position, length):
    steps = np.mod(freq[:, None] * position[None, :], length)
    phase = 2.0 * math.pi * steps / length
    return np.cos(phase), np.sin(phase)


def depth_tables(planes):
    matrices, phases = [], []
    lane_part = np.arange(LANES) // 64
    lane_odd = np.arange(LANES) // 32 % 2
    lane_plane = np.arange(LANES) % 32
    used = (lane_plane < planes).astype(np.float64)
    for index in range(NZ // 2 // planes):
        position = index * planes + lane_plane - NZ // 4
        cos, sin = waves(np.arange(TILE) - NZ // 2, position, NZ)
        cos, sin = cos * used / math.sqrt(NZ), sin * used / math.sqrt(NZ)
        real = np.where(lane_part == 0, cos, sin)
        imag = np.where(lane_part == 0, -sin, cos)
        high, low = halves(np.concatenate((real, imag)))
        matrices.append(np.concatenate((high, high, low)))
        cos, sin = waves(np.arange(NZ // TILE), position, NZ // TILE)
        sign = np.where(lane_odd == 1, -1.0, 1.0)[None, :]
        sin = sin * np.where(lane_part == 0, -1.0, 1.0)[None, :]
        phases.append(np.stack((np.concatenate((cos, cos * sign)), np.concatenate((sin, sin * sign)))))
    return np.stack(matrices), np.stack(phases).astype(np.float32)


def column_tables():
    third = NY // 3
    out = []
    for residue in range(3):
        cos, sin = waves(3 * np.arange(NY // 6) + residue - NY // 4, np.arange(third) - NY // 2, NY)
        high, low = halves(np.concatenate((cos, sin)) / math.sqrt(NY))
        out.append(np.concatenate((high, high, low), axis=1))
    return np.stack(out)


def row_tables():
    half = NX // 2
    freq = np.arange(half).reshape(-1, PARTS, CELLS).transpose(1, 0, 2).reshape(-1) - half
    quarter = NX // 4
    out = []
    for parity in range(2):
        position = 2 * np.arange(quarter) + parity - NX // 4
        cos, sin = waves(freq, position, NX)
        table = np.zeros((half, 2 * LANES))
        lanes = (np.arange(quarter) + parity * quarter) % LANES
        table[:, lanes] = cos / math.sqrt(NX)
        table[:, LANES + lanes] = sin / math.sqrt(NX)
        out.append(np.stack(halves(table)))
    return np.stack(out)


def order_tables():
    first = np.zeros((LANES, NX // 2))
    second = np.zeros((LANES, NX // 2))
    quarter = NX // 4
    for m1 in range(NX // 2):
        place = m1 // 2 + m1 % 2 * quarter
        if place < LANES:
            first[place, m1] = 1.0
        else:
            second[place - LANES, m1] = 1.0
    return np.concatenate((first, first, second, second)).astype(ml_dtypes.bfloat16)


def divide(value, divisor, limit):
    for shift in range(8, 24):
        factor = (1 << shift) // divisor + 1
        tried = np.arange(limit, dtype=np.int64)
        if factor * limit < 1 << 31 and np.array_equal(tried * factor >> shift, tried // divisor):
            return lax.shift_right_logical(value * factor, shift)
    raise ValueError(divisor)


def spread_kernel(tile_rows, tile_cols, grid_cols, devices, samples_ref, kernel_ref, offsets_ref, owners_ref, ids_ref, out_ref):
    owner, tile_id = owners_ref[...], ids_ref[...]
    tile_depth = NZ // TILE
    tiles_device = tile_rows * tile_cols * tile_depth
    owner_row = divide(owner, grid_cols, devices)
    tile_row = divide(tile_id, tile_cols * tile_depth, tiles_device)
    tile_col = divide(tile_id, tile_depth, tiles_device)
    row = owner_row * tile_rows + tile_row
    col = (owner - owner_row * grid_cols) * tile_cols + tile_col - tile_row * tile_cols
    folds = NX // TILE // 2
    upper = (row >= folds).astype(jnp.int32)
    base = (row - upper * folds) * (CELLS * STRIDE // TILE) + col
    phase = tile_id - tile_col * tile_depth + upper * tile_depth
    codes = (base * PHASES + phase).astype(F32)

    blocks = samples_ref.shape[0]
    taps = kernel_ref.shape[2]
    cell = lax.broadcasted_iota(jnp.int32, (TILE, LANES), 0)
    left = lax.broadcasted_iota(jnp.int32, (2 * TILE, LANES), 1) < LANES // 2

    def weights(block):
        placed = []
        for dim in range(3):
            shifted = cell - offsets_ref[dim, pl.ds(block, 1), :]
            value = jnp.zeros((TILE, LANES), F32)
            for tap in range(taps):
                value = jnp.where(shifted == tap, kernel_ref[block, dim, pl.ds(tap, 1), :], value)
            placed.append(value)
        plane = jnp.concatenate([placed[0][i : i + 1] * placed[1] for i in range(TILE)], axis=0)
        depth = jnp.concatenate([samples_ref[block, pl.ds(c, 1), :] * placed[2] for c in range(2)], axis=0)
        return depth, plane

    def pair_body(pair, carry):
        depth_a, plane_a = weights(2 * pair)
        depth_b, plane_b = weights(2 * pair + 1)
        depth_high, depth_low = split(jnp.concatenate((depth_a, depth_b), axis=0))
        plane_high, plane_low = split(jnp.concatenate((plane_a, plane_b), axis=0))
        piece = lax.dot_general(
            jnp.concatenate((depth_high, depth_low, depth_high), axis=1),
            jnp.concatenate((plane_high, plane_high, plane_low), axis=1),
            (((1,), (1,)), ((), ())),
            preferred_element_type=F32,
        )
        out_ref[pair] = jnp.where(left, piece[: 2 * TILE], piece[2 * TILE :])
        return carry

    lax.fori_loop(0, blocks // 2, pair_body, 0, unroll=4)
    out_ref[blocks // 2] = jnp.broadcast_to(codes, (2 * TILE, LANES))


def tiles_kernel(conditions, first, *refs):
    arrays = len(conditions)
    deep_ref = refs[0]
    source_refs = refs[1 : 1 + arrays]
    depth_ref, phases_ref = refs[1 + arrays : 3 + arrays]
    acc_refs = refs[-5 - PARTS : -5]
    token_ref, codes_ref, even_ref, odd_ref, arrived = refs[-5:]
    token_ref[...] = jnp.zeros_like(token_ref)
    stride = STRIDE
    pairs = source_refs[0].shape[0] - 1
    batch = 8
    batches = pairs // batch
    assert batches % 2 == 0

    def copies(index):
        return pltpu.make_async_copy(
            source_refs[index].at[pairs, pl.ds(0, TILE)], codes_ref.at[index], arrived.at[index]
        )

    for index in range(arrays):
        copies(index).start()

    if first:

        def clear(step, carry):
            at = pl.ds(pl.multiple_of(step * stride, stride), stride)
            for ref in acc_refs:
                ref[at, :] = jnp.zeros((stride, LANES), F32)
            return carry

        lax.fori_loop(0, NX // 2 // PARTS, clear, 0)

    for index in range(arrays):
        copies(index).wait()

    def add_source(index):
        tiles_ref = source_refs[index]

        def spectrum(number, to_ref):
            tiles = jnp.concatenate([tiles_ref[number * batch + place] for place in range(batch)], axis=1)
            high, low = split(tiles)
            to_ref[...] = lax.dot_general(
                jnp.concatenate((high, low, high), axis=0),
                depth_ref[...],
                (((0,), (0,)), ((), ())),
                preferred_element_type=F32,
            )

        def accumulate(number, from_ref):
            for tile in range(2 * batch):
                code = codes_ref[index, 0, number * 2 * batch + tile].astype(jnp.int32)
                base = lax.shift_right_logical(code, 7)
                phase = jnp.bitwise_and(code, PHASES - 1)
                cos = phases_ref[0, pl.ds(phase, 1), :]
                sin = phases_ref[1, pl.ds(phase, 1), :]
                for i in range(TILE):
                    row = tile * TILE * TILE + i * TILE
                    value = from_ref[row : row + TILE, :]
                    value = value * cos + pltpu.roll(value, LANES // 2, 1) * sin
                    acc_ref = acc_refs[i // CELLS]
                    at = pl.ds(pl.multiple_of(base * TILE + i % CELLS * stride, TILE), TILE)
                    acc_ref[at, :] = acc_ref[at, :] + value

        spectrum(0, even_ref)

        def add_pair(step, carry):
            number = 2 * step
            spectrum(number + 1, odd_ref)
            accumulate(number, even_ref)
            spectrum(jnp.minimum(number + 2, batches - 2), even_ref)
            accumulate(number + 1, odd_ref)
            return carry

        lax.fori_loop(0, batches // 2, add_pair, 0)

    for index, condition in enumerate(conditions):
        if condition is None:
            add_source(index)
        else:
            side, depth = condition
            holds = deep_ref[0] >= depth if side == "from" else deep_ref[0] < depth
            pl.when(holds)(functools.partial(add_source, index))


def columns_kernel(*refs):
    column_ref = refs[PARTS]
    acc_refs = refs[PARTS + 1 :]
    third = NY // 3
    rows = column_ref.shape[1] // 2
    turn = jnp.where(lax.broadcasted_iota(jnp.int32, (1, LANES), 1) < LANES // 2, -1.0, 1.0)

    def columns(step, carry):
        start = pl.multiple_of(step * STRIDE, TILE)
        for pair in range(0, PARTS, 2):
            folded = ([], [], [])
            for ref in acc_refs[pair : pair + 2]:
                first, second, last = (ref[pl.ds(start + third * part, third), :] for part in range(3))
                both = second + last
                across = pltpu.roll(second - last, LANES // 2, 1) * (turn * math.sqrt(0.75))
                middle = first - 0.5 * both
                folded[0].append(first + both)
                folded[1].append(middle + across)
                folded[2].append(middle - across)
            for residue in range(3):
                high, low = split(jnp.concatenate(folded[residue], axis=1))
                product = jnp.dot(
                    column_ref[residue], jnp.concatenate((high, low, high), axis=0), preferred_element_type=F32
                )
                for side, ref in enumerate(acc_refs[pair : pair + 2]):
                    lanes = slice(side * LANES, (side + 1) * LANES)
                    ref[pl.ds(start + residue * rows, rows), :] = (
                        product[:rows, lanes] + pltpu.roll(product[rows:, lanes], LANES // 2, 1) * turn
                    )
        return carry

    lax.fori_loop(0, NX // 2 // PARTS, columns, 0)


def rows_kernel(relative, first, count, chunks, grid_rows, addends, planes_padded, place_ref, *refs):
    acc_refs, row_ref, addend_refs, out_ref = refs[:PARTS], refs[PARTS], refs[PARTS + 1 : -1], refs[-1]
    assert len(addend_refs) == addends
    rows = grid_rows * chunks * TILE
    device = jnp.bitwise_xor(place_ref[0], relative)
    lane = lax.broadcasted_iota(jnp.int32, (PLANES, LANES), 1)

    def block(step, carry):
        chunk, residue = step // 3, step % 3
        start = residue * rows + (device * chunks + first + chunk) * TILE
        turned = []
        for row in range(TILE):
            at = pl.ds(start + row, NX // 2 // PARTS, stride=STRIDE)
            turned.append(jnp.concatenate([ref[at, :] for ref in acc_refs], axis=0).T)
        parts = []
        for odd in range(2):
            at = odd * PLANES
            stacked = [value[part * 64 + at : part * 64 + at + PLANES] for value in turned for part in range(2)]
            high, low = split(jnp.concatenate(stacked, axis=0))
            size = high.shape[0]
            both = jnp.dot(jnp.concatenate((high, low), axis=0), row_ref[odd, 0], preferred_element_type=F32)
            product = both[:size] + both[size:] + jnp.dot(high, row_ref[odd, 1], preferred_element_type=F32)
            sides = []
            for row in range(TILE):
                real = product[2 * row * PLANES : (2 * row + 1) * PLANES]
                imag = product[(2 * row + 1) * PLANES : (2 * row + 2) * PLANES]
                sides.append((real[:, :LANES] - imag[:, LANES:], real[:, LANES:] + imag[:, :LANES]))
            parts.append(sides)
        for slot in range(TILE // 2):
            place = chunk * (CHUNK // 2) + 3 * slot + residue
            for part in range(2):
                even = [parts[0][slot + side * TILE // 2][part] for side in range(2)]
                odd = [parts[1][slot + side * TILE // 2][part] for side in range(2)]
                values = [jnp.where(lane < NX // 4, even[side], odd[side]) for side in range(2)]
                values.append(jnp.where(lane < LANES // 2, odd[0], pltpu.roll(odd[1], LANES // 2, 1)))
                for number, value in enumerate(values):
                    planes = pl.ds(part * planes_padded, planes_padded)
                    total = value[:planes_padded]
                    for ref in addend_refs:
                        total = total + ref[first * (CHUNK // 2) + place, number, planes]
                    out_ref[place, number, planes] = total
        return carry

    lax.fori_loop(0, 3 * count, block, 0)


def finish_kernel(chunk, planes_padded, parts, refs):
    part_refs = refs[:parts]
    order_ref, first_ref, second_ref, third_ref = refs[parts : parts + 4]
    out_ref = refs[-1]
    planes = out_ref.shape[1]
    slots = part_refs[0].shape[0]
    stride = 6 * planes_padded
    flats = [ref.reshape(slots * stride, LANES) for ref in part_refs]
    order = order_ref[...]
    shape = (CHUNK, second_ref.shape[1])
    here = lax.broadcasted_iota(jnp.int32, shape, 1) == lax.broadcasted_iota(jnp.int32, shape, 0) + chunk * CHUNK
    second = jnp.sum(jnp.where(here, second_ref[...], 0.0), axis=1, keepdims=True)
    scale = second * first_ref[...]
    for part in range(2):
        for group in range(0, planes, TILE):
            members = range(group, min(group + TILE, planes))
            mains, rests = [], []
            for plane in members:
                values = []
                for number in range(3):
                    at = pl.ds((number * 2 + part) * planes_padded + plane, slots, stride=stride)
                    total = flats[0][at, :]
                    for flat in flats[1:]:
                        total = total + flat[at, :]
                    values.append(total)
                mains.append(jnp.concatenate(values[:2], axis=0))
                rests.append(jnp.concatenate((values[2], pltpu.roll(values[2], LANES // 2, 1)), axis=0))
            main = split(jnp.concatenate(mains, axis=0))
            rest = split(jnp.concatenate(rests, axis=0))
            ordered = jnp.dot(jnp.concatenate(main + rest, axis=1), order, preferred_element_type=F32)
            for index, plane in enumerate(members):
                out_ref[part, plane] = ordered[index * 2 * slots : (index + 1) * 2 * slots] * (scale * third_ref[plane])


def on_device(samples, kernel, offsets, owners, tile_ids, deapod_first, deapod_second, deapod_third):
    grid_rows = lax.axis_size("gx")
    grid_cols = lax.axis_size("gy")
    blocks = samples.shape[0]
    block_width = samples.shape[2]
    assert block_width == LANES and blocks == LANES
    tile_rows = NX // (TILE * grid_rows)
    tile_cols = NY // (TILE * grid_cols)
    planes = deapod_third.shape[0]
    per_device = deapod_second.shape[0]
    assert per_device % CHUNK == 0
    chunks = per_device // CHUNK
    slots = CHUNK // 2
    planes_padded = -(-planes // 8) * 8
    vmem = pl.BlockSpec(memory_space=pltpu.VMEM)
    params = pltpu.CompilerParams(vmem_limit_bytes=VMEM_LIMIT)

    def in_hbm(arrays):
        return [pltpu.with_memory_space_constraint(array, pltpu.HBM) for array in arrays]

    tiles = pl.pallas_call(
        functools.partial(spread_kernel, tile_rows, tile_cols, grid_cols, grid_rows * grid_cols),
        out_shape=pltpu.HBM((blocks // 2 + 1, 2 * TILE, LANES), F32),
        in_specs=[vmem] * 5,
        out_specs=vmem,
        compiler_params=params,
        name="spread",
    )(*in_hbm([samples, kernel, offsets.transpose(1, 0, 2), owners.reshape(1, blocks), tile_ids.reshape(1, blocks)]))

    along = grid_cols // Z_CHIPS
    deep_at = lax.div(lax.axis_index("gy").astype(jnp.int32), jnp.int32(along))

    def shift(value, senders, deep, wide):
        moves = [
            (z * along + y, (z + deep) * along + (y + wide) % along) for z in senders for y in range(along)
        ]
        return lax.ppermute(value, "gy", moves)

    place = lax.axis_index("gx").astype(jnp.int32).reshape(1)
    deep_place = deep_at.reshape(1)
    gy = lax.axis_index("gy")
    matrices, phases = depth_tables(planes)
    matrix = lax.dynamic_index_in_dim(jnp.asarray(matrices), gy, 0, keepdims=False)
    phase_rows = lax.dynamic_index_in_dim(jnp.asarray(phases), gy, 0, keepdims=False)
    column = jnp.asarray(column_tables())
    half = NX // 2
    smem = pl.BlockSpec(memory_space=pltpu.SMEM)
    acc_shape = (half // PARTS * STRIDE, LANES)

    def in_vmem(arrays):
        return [pltpu.with_memory_space_constraint(array, pltpu.VMEM) for array in arrays]

    def condition(steps):
        if steps == 0:
            return None
        return ("from", steps) if steps > 0 else ("below", Z_CHIPS + steps)

    def add_tiles(sources, acc):
        conditions = [condition(steps) for steps, _ in sources]
        spectra = pltpu.VMEM((16 * TILE * TILE, LANES), F32)
        kept = [jax.ShapeDtypeStruct(acc_shape, F32) if acc else pltpu.VMEM(acc_shape, F32)] * PARTS
        inputs = len(sources) + 3
        *acc, token = pl.pallas_call(
            functools.partial(tiles_kernel, conditions, not acc),
            out_shape=kept + [jax.ShapeDtypeStruct((TILE, LANES), F32)],
            in_specs=[smem] + [vmem] * (inputs - 1 + len(acc)),
            out_specs=[vmem] * (PARTS + 1),
            input_output_aliases={inputs + part: part for part in range(PARTS)} if acc else {},
            scratch_shapes=[
                pltpu.SMEM((len(sources), TILE, LANES), F32),
                spectra,
                spectra,
                pltpu.SemaphoreType.DMA((len(sources),)),
            ],
            compiler_params=params,
            cost_estimate=pl.CostEstimate(flops=0, bytes_accessed=len(sources) << 23, transcendentals=0),
            name="tiles",
        )(deep_place, *in_hbm([array for _, array in sources] + [matrix, phase_rows]), *in_vmem(acc))
        return acc, token

    def after(value, token):
        return lax.optimization_barrier((value, token))[0]

    held, crossed_y = {0: tiles}, {}
    acc, waiting = [], [(0, tiles)]
    token = None
    for steps in range(1, Z_CHIPS + 1):
        if steps < Z_CHIPS:
            for signed in (steps, -steps):
                value = held[signed - signed // steps]
                value = value if token is None else after(value, token)
                senders = range(steps - 1, Z_CHIPS - 1) if signed > 0 else range(1, Z_CHIPS + 1 - steps)
                held[signed] = shift(value, senders, signed // steps, 0)
        behind = []
        for signed in sorted({steps - 1, 1 - steps}):
            holders = range(signed, Z_CHIPS) if signed >= 0 else range(Z_CHIPS + signed)
            for wide in range(1, along):
                value = held[signed] if token is None else after(held[signed], token)
                crossed_y[signed, wide] = shift(value, holders, 0, wide)
                behind.append((signed, crossed_y[signed, wide]))
        acc, token = add_tiles(waiting, acc)
        waiting = behind
        if steps < Z_CHIPS:
            waiting = [(steps, held[steps]), (-steps, held[-steps])] + behind
    acc, _ = add_tiles(waiting, acc)

    acc = pl.pallas_call(
        columns_kernel,
        out_shape=[jax.ShapeDtypeStruct(acc_shape, F32)] * PARTS,
        in_specs=[vmem] * (PARTS + 1),
        out_specs=[vmem] * PARTS,
        input_output_aliases={part: part for part in range(PARTS)},
        compiler_params=params,
        name="columns",
    )(*in_vmem(acc), *in_hbm([column]))

    row_table = jnp.asarray(row_tables())
    part_shape = (3, 2 * planes_padded, LANES)

    def rows_for(relative, first, count, addends, after):
        def body(*refs):
            operands = 2 + PARTS + len(addends)
            rows_kernel(
                relative, first, count, chunks, grid_rows, len(addends), planes_padded, *refs[:operands], refs[-1]
            )

        return pl.pallas_call(
            body,
            in_specs=[smem] + [vmem] * (1 + PARTS + len(addends)) + [pl.BlockSpec(memory_space=pl.ANY)] * len(after),
            out_specs=vmem,
            out_shape=pltpu.HBM((count * slots,) + part_shape, F32),
            compiler_params=params,
            cost_estimate=pl.CostEstimate(flops=1, bytes_accessed=1, transcendentals=0),
            name="rows",
        )(place, *in_vmem(acc), *in_hbm([row_table] + addends + after))

    def swap(value, bit):
        return lax.ppermute(value, "gx", [(index, index ^ bit) for index in range(grid_rows)])

    last = []

    def rows_next(relative, first, count, addends):
        part = rows_for(relative, first, count, addends, last)
        last[:] = [part]
        return part

    def arrivals(relative, top):
        arrived = []
        bit = 1
        while bit <= top:
            arrived.append(swap(rows_next(relative | bit, 0, chunks, arrivals(relative | bit, bit // 2)), bit))
            bit *= 2
        return arrived

    top = grid_rows // 2
    far = arrivals(top, top // 2)
    near = arrivals(0, top // 2)
    crossed = [swap(rows_next(top, chunk, 1, far), top) for chunk in range(chunks)]
    kept_parts = [rows_next(0, 0, chunks, [])] + near

    image = None
    for chunk in range(chunks):

        def finish(*refs, chunk=chunk):
            finish_kernel(chunk, planes_padded, len(kept_parts) + 1, refs)

        earlier = [] if image is None else [image]
        image = pl.pallas_call(
            finish,
            grid=(1,),
            out_shape=jax.ShapeDtypeStruct((2, planes, per_device, NX // 2), F32),
            in_specs=[pl.BlockSpec((slots,) + part_shape, lambda step, chunk=chunk: (chunk, 0, 0, 0))] * len(kept_parts)
            + [
                pl.BlockSpec((slots,) + part_shape, lambda step: (0, 0, 0, 0)),
                pl.BlockSpec((4 * LANES, NX // 2), lambda step: (0, 0)),
                pl.BlockSpec((1, NX // 2), lambda step: (0, 0)),
                pl.BlockSpec((1, per_device), lambda step: (0, 0)),
                pl.BlockSpec(memory_space=pltpu.SMEM),
            ]
            + [pl.BlockSpec(memory_space=pl.ANY)] * len(earlier),
            out_specs=pl.BlockSpec((2, planes, CHUNK, NX // 2), lambda step, chunk=chunk: (0, 0, chunk, 0)),
            input_output_aliases={len(kept_parts) + 5: 0} if earlier else {},
            compiler_params=params,
            name="finish",
        )(
            *in_hbm(kept_parts + [crossed[chunk]]),
            jnp.asarray(order_tables()),
            deapod_first[None, :],
            deapod_second[None, :],
            deapod_third,
            *earlier,
        )
    return image


def solution(mesh):
    in_specs = (
        P(("gx", "gy"), None, None),
        P(("gx", "gy"), None, None, None),
        P(("gx", "gy"), None, None),
        P(("gx", "gy"), None),
        P(("gx", "gy")),
        P(),
        P("gx"),
        P("gy"),
    )
    out_specs = P(None, "gy", "gx", None)
    return jax.shard_map(
        on_device, mesh=mesh, in_specs=in_specs, out_specs=out_specs, check_vma=False
    )
```

```python
import functools
import math

import jax
import jax.numpy as jnp
import ml_dtypes
import numpy as np
from jax import lax
from jax.experimental import pallas as pl
from jax.experimental.pallas import tpu as pltpu
from jax.sharding import PartitionSpec as P

NX = 384
NY = 384
NZ = 384
TILE = 8
LANES = 128
PLANES = 32
CHUNK = 24
Z_CHIPS = 4
PARTS = 4
CELLS = TILE // PARTS
STRIDE = NY + TILE
PHASES = 128
BF16 = jnp.bfloat16
F32 = jnp.float32
VMEM_LIMIT = 8 * 1024 * 1024


def halves(array):
    high = array.astype(ml_dtypes.bfloat16)
    low = (array - high.astype(np.float64)).astype(ml_dtypes.bfloat16)
    return high, low


def split(value):
    high = value.astype(BF16)
    return high, (value - high.astype(F32)).astype(BF16)


def waves(freq, position, length):
    steps = np.mod(freq[:, None] * position[None, :], length)
    phase = 2.0 * math.pi * steps / length
    return np.cos(phase), np.sin(phase)


def depth_tables(planes):
    matrices, phases = [], []
    lane_part = np.arange(LANES) // 64
    lane_odd = np.arange(LANES) // 32 % 2
    lane_plane = np.arange(LANES) % 32
    used = (lane_plane < planes).astype(np.float64)
    for index in range(NZ // 2 // planes):
        position = index * planes + lane_plane - NZ // 4
        cos, sin = waves(np.arange(TILE) - NZ // 2, position, NZ)
        cos, sin = cos * used / math.sqrt(NZ), sin * used / math.sqrt(NZ)
        real = np.where(lane_part == 0, cos, sin)
        imag = np.where(lane_part == 0, -sin, cos)
        high, low = halves(np.concatenate((real, imag)))
        matrices.append(np.concatenate((high, high, low)))
        cos, sin = waves(np.arange(NZ // TILE), position, NZ // TILE)
        sign = np.where(lane_odd == 1, -1.0, 1.0)[None, :]
        sin = sin * np.where(lane_part == 0, -1.0, 1.0)[None, :]
        phases.append(np.stack((np.concatenate((cos, cos * sign)), np.concatenate((sin, sin * sign)))))
    return np.stack(matrices), np.stack(phases).astype(np.float32)


def column_tables():
    third = NY // 3
    out = []
    for residue in range(3):
        cos, sin = waves(3 * np.arange(NY // 6) + residue - NY // 4, np.arange(third) - NY // 2, NY)
        high, low = halves(np.concatenate((cos, sin)) / math.sqrt(NY))
        out.append(np.concatenate((high, high, low), axis=1))
    return np.stack(out)


def row_tables():
    half = NX // 2
    freq = np.arange(half).reshape(-1, PARTS, CELLS).transpose(1, 0, 2).reshape(-1) - half
    quarter = NX // 4
    out = []
    for parity in range(2):
        position = 2 * np.arange(quarter) + parity - NX // 4
        cos, sin = waves(freq, position, NX)
        table = np.zeros((half, 2 * LANES))
        lanes = (np.arange(quarter) + parity * quarter) % LANES
        table[:, lanes] = cos / math.sqrt(NX)
        table[:, LANES + lanes] = sin / math.sqrt(NX)
        out.append(np.stack(halves(table)))
    return np.stack(out)


def order_tables():
    first = np.zeros((LANES, NX // 2))
    second = np.zeros((LANES, NX // 2))
    quarter = NX // 4
    for m1 in range(NX // 2):
        place = m1 // 2 + m1 % 2 * quarter
        if place < LANES:
            first[place, m1] = 1.0
        else:
            second[place - LANES, m1] = 1.0
    return np.concatenate((first, first, second, second)).astype(ml_dtypes.bfloat16)


def divide(value, divisor, limit):
    for shift in range(8, 24):
        factor = (1 << shift) // divisor + 1
        tried = np.arange(limit, dtype=np.int64)
        if factor * limit < 1 << 31 and np.array_equal(tried * factor >> shift, tried // divisor):
            return lax.shift_right_logical(value * factor, shift)
    raise ValueError(divisor)


def spread_kernel(tile_rows, tile_cols, grid_cols, devices, samples_ref, kernel_ref, offsets_ref, owners_ref, ids_ref, out_ref):
    owner, tile_id = owners_ref[...], ids_ref[...]
    tile_depth = NZ // TILE
    tiles_device = tile_rows * tile_cols * tile_depth
    owner_row = divide(owner, grid_cols, devices)
    tile_row = divide(tile_id, tile_cols * tile_depth, tiles_device)
    tile_col = divide(tile_id, tile_depth, tiles_device)
    row = owner_row * tile_rows + tile_row
    col = (owner - owner_row * grid_cols) * tile_cols + tile_col - tile_row * tile_cols
    folds = NX // TILE // 2
    upper = (row >= folds).astype(jnp.int32)
    base = (row - upper * folds) * (CELLS * STRIDE // TILE) + col
    phase = tile_id - tile_col * tile_depth + upper * tile_depth
    codes = (base * PHASES + phase).astype(F32)

    blocks = samples_ref.shape[0]
    taps = kernel_ref.shape[2]
    cell = lax.broadcasted_iota(jnp.int32, (TILE, LANES), 0)
    left = lax.broadcasted_iota(jnp.int32, (2 * TILE, LANES), 1) < LANES // 2

    def weights(block):
        placed = []
        for dim in range(3):
            shifted = cell - offsets_ref[dim, pl.ds(block, 1), :]
            value = jnp.zeros((TILE, LANES), F32)
            for tap in range(taps):
                value = jnp.where(shifted == tap, kernel_ref[block, dim, pl.ds(tap, 1), :], value)
            placed.append(value)
        plane = jnp.concatenate([placed[0][i : i + 1] * placed[1] for i in range(TILE)], axis=0)
        depth = jnp.concatenate([samples_ref[block, pl.ds(c, 1), :] * placed[2] for c in range(2)], axis=0)
        return depth, plane

    def pair_body(pair, carry):
        depth_a, plane_a = weights(2 * pair)
        depth_b, plane_b = weights(2 * pair + 1)
        depth_high, depth_low = split(jnp.concatenate((depth_a, depth_b), axis=0))
        plane_high, plane_low = split(jnp.concatenate((plane_a, plane_b), axis=0))
        piece = lax.dot_general(
            jnp.concatenate((depth_high, depth_low, depth_high), axis=1),
            jnp.concatenate((plane_high, plane_high, plane_low), axis=1),
            (((1,), (1,)), ((), ())),
            preferred_element_type=F32,
        )
        out_ref[pair] = jnp.where(left, piece[: 2 * TILE], piece[2 * TILE :])
        return carry

    lax.fori_loop(0, blocks // 2, pair_body, 0, unroll=4)
    out_ref[blocks // 2] = jnp.broadcast_to(codes, (2 * TILE, LANES))


def tiles_kernel(conditions, first, *refs):
    arrays = len(conditions)
    places_ref = refs[0]
    source_refs = refs[1 : 1 + arrays]
    depth_ref, phases_ref = refs[1 + arrays : 3 + arrays]
    acc_refs = refs[-5 - PARTS : -5]
    token_ref, codes_ref, even_ref, odd_ref, arrived = refs[-5:]
    token_ref[...] = jnp.zeros_like(token_ref)
    stride = STRIDE
    pairs = source_refs[0].shape[0] - 1
    batch = 8
    batches = pairs // batch
    assert batches % 2 == 0

    def copies(index):
        return pltpu.make_async_copy(
            source_refs[index].at[pairs, pl.ds(0, TILE)], codes_ref.at[index], arrived.at[index]
        )

    for index in range(arrays):
        copies(index).start()

    if first:

        def clear(step, carry):
            at = pl.ds(pl.multiple_of(step * stride, stride), stride)
            for ref in acc_refs:
                ref[at, :] = jnp.zeros((stride, LANES), F32)
            return carry

        lax.fori_loop(0, NX // 2 // PARTS, clear, 0)

    for index in range(arrays):
        copies(index).wait()

    def add_source(index):
        tiles_ref = source_refs[index]

        def spectrum(number, to_ref):
            tiles = jnp.concatenate([tiles_ref[number * batch + place] for place in range(batch)], axis=1)
            high, low = split(tiles)
            to_ref[...] = lax.dot_general(
                jnp.concatenate((high, low, high), axis=0),
                depth_ref[...],
                (((0,), (0,)), ((), ())),
                preferred_element_type=F32,
            )

        def accumulate(number, from_ref):
            for tile in range(2 * batch):
                code = codes_ref[index, 0, number * 2 * batch + tile].astype(jnp.int32)
                base = lax.shift_right_logical(code, 7)
                phase = jnp.bitwise_and(code, PHASES - 1)
                cos = phases_ref[0, pl.ds(phase, 1), :]
                sin = phases_ref[1, pl.ds(phase, 1), :]
                for i in range(TILE):
                    row = tile * TILE * TILE + i * TILE
                    value = from_ref[row : row + TILE, :]
                    value = value * cos + pltpu.roll(value, LANES // 2, 1) * sin
                    acc_ref = acc_refs[i // CELLS]
                    at = pl.ds(pl.multiple_of(base * TILE + i % CELLS * stride, TILE), TILE)
                    acc_ref[at, :] = acc_ref[at, :] + value

        spectrum(0, even_ref)

        def add_pair(step, carry):
            number = 2 * step
            spectrum(number + 1, odd_ref)
            accumulate(number, even_ref)
            spectrum(jnp.minimum(number + 2, batches - 2), even_ref)
            accumulate(number + 1, odd_ref)
            return carry

        lax.fori_loop(0, batches // 2, add_pair, 0)

    for index, condition in enumerate(conditions):
        if condition is None:
            add_source(index)
        else:
            side, depth = condition
            holds = places_ref[0] >= depth if side == "from" else places_ref[0] < depth
            pl.when(holds)(functools.partial(add_source, index))


def columns_kernel(*refs):
    column_ref = refs[PARTS]
    acc_refs = refs[PARTS + 1 :]
    third = NY // 3
    rows = column_ref.shape[1] // 2
    turn = jnp.where(lax.broadcasted_iota(jnp.int32, (1, LANES), 1) < LANES // 2, -1.0, 1.0)

    def columns(step, carry):
        start = pl.multiple_of(step * STRIDE, TILE)
        for pair in range(0, PARTS, 2):
            folded = ([], [], [])
            for ref in acc_refs[pair : pair + 2]:
                first, second, last = (ref[pl.ds(start + third * part, third), :] for part in range(3))
                both = second + last
                across = pltpu.roll(second - last, LANES // 2, 1) * (turn * math.sqrt(0.75))
                middle = first - 0.5 * both
                folded[0].append(first + both)
                folded[1].append(middle + across)
                folded[2].append(middle - across)
            for residue in range(3):
                high, low = split(jnp.concatenate(folded[residue], axis=1))
                product = jnp.dot(
                    column_ref[residue], jnp.concatenate((high, low, high), axis=0), preferred_element_type=F32
                )
                for side, ref in enumerate(acc_refs[pair : pair + 2]):
                    lanes = slice(side * LANES, (side + 1) * LANES)
                    ref[pl.ds(start + residue * rows, rows), :] = (
                        product[:rows, lanes] + pltpu.roll(product[rows:, lanes], LANES // 2, 1) * turn
                    )
        return carry

    lax.fori_loop(0, NX // 2 // PARTS, columns, 0)


def rows_kernel(relative, first, count, chunks, grid_rows, addends, planes_padded, places_ref, *refs):
    acc_refs, row_ref, addend_refs, out_ref = refs[:PARTS], refs[PARTS], refs[PARTS + 1 : -1], refs[-1]
    assert len(addend_refs) == addends
    rows = grid_rows * chunks * TILE
    device = jnp.bitwise_xor(places_ref[1], relative)
    lane = lax.broadcasted_iota(jnp.int32, (PLANES, LANES), 1)

    def block(step, carry):
        chunk, residue = step // 3, step % 3
        start = residue * rows + (device * chunks + first + chunk) * TILE
        turned = []
        for row in range(TILE):
            at = pl.ds(start + row, NX // 2 // PARTS, stride=STRIDE)
            turned.append(jnp.concatenate([ref[at, :] for ref in acc_refs], axis=0).T)
        parts = []
        for odd in range(2):
            at = odd * PLANES
            stacked = [value[part * 64 + at : part * 64 + at + PLANES] for value in turned for part in range(2)]
            high, low = split(jnp.concatenate(stacked, axis=0))
            size = high.shape[0]
            both = jnp.dot(jnp.concatenate((high, low), axis=0), row_ref[odd, 0], preferred_element_type=F32)
            product = both[:size] + both[size:] + jnp.dot(high, row_ref[odd, 1], preferred_element_type=F32)
            sides = []
            for row in range(TILE):
                real = product[2 * row * PLANES : (2 * row + 1) * PLANES]
                imag = product[(2 * row + 1) * PLANES : (2 * row + 2) * PLANES]
                sides.append((real[:, :LANES] - imag[:, LANES:], real[:, LANES:] + imag[:, :LANES]))
            parts.append(sides)
        for slot in range(TILE // 2):
            place = chunk * (CHUNK // 2) + 3 * slot + residue
            for part in range(2):
                even = [parts[0][slot + side * TILE // 2][part] for side in range(2)]
                odd = [parts[1][slot + side * TILE // 2][part] for side in range(2)]
                values = [jnp.where(lane < NX // 4, even[side], odd[side]) for side in range(2)]
                values.append(jnp.where(lane < LANES // 2, odd[0], pltpu.roll(odd[1], LANES // 2, 1)))
                for number, value in enumerate(values):
                    planes = pl.ds(part * planes_padded, planes_padded)
                    total = value[:planes_padded]
                    for ref in addend_refs:
                        total = total + ref[first * (CHUNK // 2) + place, number, planes]
                    out_ref[place, number, planes] = total
        return carry

    lax.fori_loop(0, 3 * count, block, 0)


def finish_kernel(chunk, planes_padded, parts, refs):
    part_refs = refs[:parts]
    order_ref, first_ref, second_ref, third_ref = refs[parts : parts + 4]
    out_ref = refs[-1]
    planes = out_ref.shape[1]
    slots = part_refs[0].shape[0]
    stride = 6 * planes_padded
    flats = [ref.reshape(slots * stride, LANES) for ref in part_refs]
    order = order_ref[...]
    shape = (CHUNK, second_ref.shape[1])
    here = lax.broadcasted_iota(jnp.int32, shape, 1) == lax.broadcasted_iota(jnp.int32, shape, 0) + chunk * CHUNK
    second = jnp.sum(jnp.where(here, second_ref[...], 0.0), axis=1, keepdims=True)
    scale = second * first_ref[...]
    for part in range(2):
        for group in range(0, planes, TILE):
            members = range(group, min(group + TILE, planes))
            mains, rests = [], []
            for plane in members:
                values = []
                for number in range(3):
                    at = pl.ds((number * 2 + part) * planes_padded + plane, slots, stride=stride)
                    total = flats[0][at, :]
                    for flat in flats[1:]:
                        total = total + flat[at, :]
                    values.append(total)
                mains.append(jnp.concatenate(values[:2], axis=0))
                rests.append(jnp.concatenate((values[2], pltpu.roll(values[2], LANES // 2, 1)), axis=0))
            main = split(jnp.concatenate(mains, axis=0))
            rest = split(jnp.concatenate(rests, axis=0))
            ordered = jnp.dot(jnp.concatenate(main + rest, axis=1), order, preferred_element_type=F32)
            for index, plane in enumerate(members):
                out_ref[part, plane] = ordered[index * 2 * slots : (index + 1) * 2 * slots] * (scale * third_ref[plane])


def on_device(samples, kernel, offsets, owners, tile_ids, deapod_first, deapod_second, deapod_third):
    grid_rows = lax.axis_size("gx")
    grid_cols = lax.axis_size("gy")
    blocks = samples.shape[0]
    block_width = samples.shape[2]
    assert block_width == LANES and blocks == LANES
    tile_rows = NX // (TILE * grid_rows)
    tile_cols = NY // (TILE * grid_cols)
    planes = deapod_third.shape[0]
    per_device = deapod_second.shape[0]
    assert per_device % CHUNK == 0
    chunks = per_device // CHUNK
    slots = CHUNK // 2
    planes_padded = -(-planes // 8) * 8
    vmem = pl.BlockSpec(memory_space=pltpu.VMEM)
    params = pltpu.CompilerParams(vmem_limit_bytes=VMEM_LIMIT)

    def in_hbm(arrays):
        return [pltpu.with_memory_space_constraint(array, pltpu.HBM) for array in arrays]

    tiles = pl.pallas_call(
        functools.partial(spread_kernel, tile_rows, tile_cols, grid_cols, grid_rows * grid_cols),
        out_shape=pltpu.HBM((blocks // 2 + 1, 2 * TILE, LANES), F32),
        in_specs=[vmem] * 5,
        out_specs=vmem,
        compiler_params=params,
        name="spread",
    )(*in_hbm([samples, kernel, offsets.transpose(1, 0, 2), owners.reshape(1, blocks), tile_ids.reshape(1, blocks)]))

    along = grid_cols // Z_CHIPS
    deep_at = lax.div(lax.axis_index("gy").astype(jnp.int32), jnp.int32(along))

    def shift(value, senders, deep, wide):
        moves = [
            (z * along + y, (z + deep) * along + (y + wide) % along) for z in senders for y in range(along)
        ]
        return lax.ppermute(value, "gy", moves)

    places = jnp.stack((deep_at, lax.axis_index("gx").astype(jnp.int32)))
    gy = lax.axis_index("gy")
    matrices, phases = depth_tables(planes)
    matrix = lax.dynamic_index_in_dim(jnp.asarray(matrices), gy, 0, keepdims=False)
    phase_rows = lax.dynamic_index_in_dim(jnp.asarray(phases), gy, 0, keepdims=False)
    column = jnp.asarray(column_tables())
    half = NX // 2
    smem = pl.BlockSpec(memory_space=pltpu.SMEM)
    acc_shape = (half // PARTS * STRIDE, LANES)

    def in_vmem(arrays):
        return [pltpu.with_memory_space_constraint(array, pltpu.VMEM) for array in arrays]

    def condition(steps):
        if steps == 0:
            return None
        return ("from", steps) if steps > 0 else ("below", Z_CHIPS + steps)

    def add_tiles(sources, acc):
        conditions = [condition(steps) for steps, _ in sources]
        spectra = pltpu.VMEM((16 * TILE * TILE, LANES), F32)
        kept = [jax.ShapeDtypeStruct(acc_shape, F32) if acc else pltpu.VMEM(acc_shape, F32)] * PARTS
        inputs = len(sources) + 3
        *acc, token = pl.pallas_call(
            functools.partial(tiles_kernel, conditions, not acc),
            out_shape=kept + [jax.ShapeDtypeStruct((TILE, LANES), F32)],
            in_specs=[smem] + [vmem] * (inputs - 1 + len(acc)),
            out_specs=[vmem] * (PARTS + 1),
            input_output_aliases={inputs + part: part for part in range(PARTS)} if acc else {},
            scratch_shapes=[
                pltpu.SMEM((len(sources), TILE, LANES), F32),
                spectra,
                spectra,
                pltpu.SemaphoreType.DMA((len(sources),)),
            ],
            compiler_params=params,
            cost_estimate=pl.CostEstimate(flops=0, bytes_accessed=len(sources) << 23, transcendentals=0),
            name="tiles",
        )(places, *in_hbm([array for _, array in sources] + [matrix, phase_rows]), *in_vmem(acc))
        return acc, token

    def after(value, token):
        return lax.optimization_barrier((value, token))[0]

    held, crossed_y = {0: tiles}, {}
    acc, waiting = [], [(0, tiles)]
    token = None
    for steps in range(1, Z_CHIPS + 1):
        if steps < Z_CHIPS:
            for signed in (steps, -steps):
                value = held[signed - signed // steps]
                value = value if token is None else after(value, token)
                senders = range(steps - 1, Z_CHIPS - 1) if signed > 0 else range(1, Z_CHIPS + 1 - steps)
                held[signed] = shift(value, senders, signed // steps, 0)
        behind = []
        for signed in sorted({steps - 1, 1 - steps}):
            holders = range(signed, Z_CHIPS) if signed >= 0 else range(Z_CHIPS + signed)
            for wide in range(1, along):
                value = held[signed] if token is None else after(held[signed], token)
                crossed_y[signed, wide] = shift(value, holders, 0, wide)
                behind.append((signed, crossed_y[signed, wide]))
        acc, token = add_tiles(waiting, acc)
        waiting = behind
        if steps < Z_CHIPS:
            waiting = [(steps, held[steps]), (-steps, held[-steps])] + behind
    acc, _ = add_tiles(waiting, acc)

    acc = pl.pallas_call(
        columns_kernel,
        out_shape=[jax.ShapeDtypeStruct(acc_shape, F32)] * PARTS,
        in_specs=[vmem] * (PARTS + 1),
        out_specs=[vmem] * PARTS,
        input_output_aliases={part: part for part in range(PARTS)},
        compiler_params=params,
        name="columns",
    )(*in_vmem(acc), *in_hbm([column]))

    row_table = jnp.asarray(row_tables())
    part_shape = (3, 2 * planes_padded, LANES)

    def rows_for(relative, first, count, addends, after):
        def body(*refs):
            operands = 2 + PARTS + len(addends)
            rows_kernel(
                relative, first, count, chunks, grid_rows, len(addends), planes_padded, *refs[:operands], refs[-1]
            )

        return pl.pallas_call(
            body,
            in_specs=[smem] + [vmem] * (1 + PARTS + len(addends)) + [pl.BlockSpec(memory_space=pl.ANY)] * len(after),
            out_specs=vmem,
            out_shape=pltpu.HBM((count * slots,) + part_shape, F32),
            compiler_params=params,
            cost_estimate=pl.CostEstimate(flops=1, bytes_accessed=1, transcendentals=0),
            name="rows",
        )(places, *in_vmem(acc), *in_hbm([row_table] + addends + after))

    def swap(value, bit):
        return lax.ppermute(value, "gx", [(index, index ^ bit) for index in range(grid_rows)])

    last = []

    def rows_next(relative, first, count, addends):
        part = rows_for(relative, first, count, addends, last)
        last[:] = [part]
        return part

    def arrivals(relative, top):
        arrived = []
        bit = 1
        while bit <= top:
            arrived.append(swap(rows_next(relative | bit, 0, chunks, arrivals(relative | bit, bit // 2)), bit))
            bit *= 2
        return arrived

    top = grid_rows // 2
    far = arrivals(top, top // 2)
    near = arrivals(0, top // 2)
    crossed = [swap(rows_next(top, chunk, 1, far), top) for chunk in range(chunks)]
    kept_parts = [rows_next(0, 0, chunks, [])] + near

    image = None
    for chunk in range(chunks):

        def finish(*refs, chunk=chunk):
            finish_kernel(chunk, planes_padded, len(kept_parts) + 1, refs)

        earlier = [] if image is None else [image]
        image = pl.pallas_call(
            finish,
            grid=(1,),
            out_shape=jax.ShapeDtypeStruct((2, planes, per_device, NX // 2), F32),
            in_specs=[pl.BlockSpec((slots,) + part_shape, lambda step, chunk=chunk: (chunk, 0, 0, 0))] * len(kept_parts)
            + [
                pl.BlockSpec((slots,) + part_shape, lambda step: (0, 0, 0, 0)),
                pl.BlockSpec((4 * LANES, NX // 2), lambda step: (0, 0)),
                pl.BlockSpec((1, NX // 2), lambda step: (0, 0)),
                pl.BlockSpec((1, per_device), lambda step: (0, 0)),
                pl.BlockSpec(memory_space=pltpu.SMEM),
            ]
            + [pl.BlockSpec(memory_space=pl.ANY)] * len(earlier),
            out_specs=pl.BlockSpec((2, planes, CHUNK, NX // 2), lambda step, chunk=chunk: (0, 0, chunk, 0)),
            input_output_aliases={len(kept_parts) + 5: 0} if earlier else {},
            compiler_params=params,
            name="finish",
        )(
            *in_hbm(kept_parts + [crossed[chunk]]),
            jnp.asarray(order_tables()),
            deapod_first[None, :],
            deapod_second[None, :],
            deapod_third,
            *earlier,
        )
    return image


def solution(mesh):
    in_specs = (
        P(("gx", "gy"), None, None),
        P(("gx", "gy"), None, None, None),
        P(("gx", "gy"), None, None),
        P(("gx", "gy"), None),
        P(("gx", "gy")),
        P(),
        P("gx"),
        P("gy"),
    )
    out_specs = P(None, "gy", "gx", None)
    return jax.shard_map(
        on_device, mesh=mesh, in_specs=in_specs, out_specs=out_specs, check_vma=False
    )
```

```python
import functools
import math

import jax
import jax.numpy as jnp
import ml_dtypes
import numpy as np
from jax import lax
from jax.experimental import pallas as pl
from jax.experimental.pallas import tpu as pltpu
from jax.sharding import PartitionSpec as P

NX = 384
NY = 384
NZ = 384
TILE = 8
LANES = 128
PLANES = 32
CHUNK = 24
Z_CHIPS = 4
PARTS = 4
CELLS = TILE // PARTS
STRIDE = NY + TILE
PHASES = 128
BF16 = jnp.bfloat16
F32 = jnp.float32
VMEM_LIMIT = 8 * 1024 * 1024


def halves(array):
    high = array.astype(ml_dtypes.bfloat16)
    low = (array - high.astype(np.float64)).astype(ml_dtypes.bfloat16)
    return high, low


def split(value):
    high = value.astype(BF16)
    return high, (value - high.astype(F32)).astype(BF16)


def waves(freq, position, length):
    steps = np.mod(freq[:, None] * position[None, :], length)
    phase = 2.0 * math.pi * steps / length
    return np.cos(phase), np.sin(phase)


def depth_tables(planes):
    matrices, phases = [], []
    lane_part = np.arange(LANES) // 64
    lane_odd = np.arange(LANES) // 32 % 2
    lane_plane = np.arange(LANES) % 32
    used = (lane_plane < planes).astype(np.float64)
    for index in range(NZ // 2 // planes):
        position = index * planes + lane_plane - NZ // 4
        cos, sin = waves(np.arange(TILE) - NZ // 2, position, NZ)
        cos, sin = cos * used / math.sqrt(NZ), sin * used / math.sqrt(NZ)
        real = np.where(lane_part == 0, cos, sin)
        imag = np.where(lane_part == 0, -sin, cos)
        high, low = halves(np.concatenate((real, imag)))
        matrices.append(np.concatenate((high, high, low)))
        cos, sin = waves(np.arange(NZ // TILE), position, NZ // TILE)
        sign = np.where(lane_odd == 1, -1.0, 1.0)[None, :]
        sin = sin * np.where(lane_part == 0, -1.0, 1.0)[None, :]
        phases.append(np.stack((np.concatenate((cos, cos * sign)), np.concatenate((sin, sin * sign)))))
    return np.stack(matrices), np.stack(phases).astype(np.float32)


def column_tables():
    third = NY // 3
    out = []
    for residue in range(3):
        cos, sin = waves(3 * np.arange(NY // 6) + residue - NY // 4, np.arange(third) - NY // 2, NY)
        high, low = halves(np.concatenate((cos, sin)) / math.sqrt(NY))
        out.append(np.concatenate((high, high, low), axis=1))
    return np.stack(out)


def row_tables():
    half = NX // 2
    freq = np.arange(half).reshape(-1, PARTS, CELLS).transpose(1, 0, 2).reshape(-1) - half
    quarter = NX // 4
    out = []
    for parity in range(2):
        position = 2 * np.arange(quarter) + parity - NX // 4
        cos, sin = waves(freq, position, NX)
        table = np.zeros((half, 2 * LANES))
        lanes = (np.arange(quarter) + parity * quarter) % LANES
        table[:, lanes] = cos / math.sqrt(NX)
        table[:, LANES + lanes] = sin / math.sqrt(NX)
        out.append(np.stack(halves(table)))
    return np.stack(out)


def order_tables():
    first = np.zeros((LANES, NX // 2))
    second = np.zeros((LANES, NX // 2))
    quarter = NX // 4
    for m1 in range(NX // 2):
        place = m1 // 2 + m1 % 2 * quarter
        if place < LANES:
            first[place, m1] = 1.0
        else:
            second[place - LANES, m1] = 1.0
    return np.concatenate((first, first, second, second)).astype(ml_dtypes.bfloat16)


def divide(value, divisor, limit):
    for shift in range(8, 24):
        factor = (1 << shift) // divisor + 1
        tried = np.arange(limit, dtype=np.int64)
        if factor * limit < 1 << 31 and np.array_equal(tried * factor >> shift, tried // divisor):
            return lax.shift_right_logical(value * factor, shift)
    raise ValueError(divisor)


def spread_kernel(tile_rows, tile_cols, grid_cols, devices, samples_ref, kernel_ref, offsets_ref, owners_ref, ids_ref, out_ref):
    owner, tile_id = owners_ref[...], ids_ref[...]
    tile_depth = NZ // TILE
    tiles_device = tile_rows * tile_cols * tile_depth
    owner_row = divide(owner, grid_cols, devices)
    tile_row = divide(tile_id, tile_cols * tile_depth, tiles_device)
    tile_col = divide(tile_id, tile_depth, tiles_device)
    row = owner_row * tile_rows + tile_row
    col = (owner - owner_row * grid_cols) * tile_cols + tile_col - tile_row * tile_cols
    folds = NX // TILE // 2
    upper = (row >= folds).astype(jnp.int32)
    base = (row - upper * folds) * (CELLS * STRIDE // TILE) + col
    phase = tile_id - tile_col * tile_depth + upper * tile_depth
    codes = (base * PHASES + phase).astype(F32)

    blocks = samples_ref.shape[0]
    taps = kernel_ref.shape[2]
    cell = lax.broadcasted_iota(jnp.int32, (TILE, LANES), 0)
    left = lax.broadcasted_iota(jnp.int32, (2 * TILE, LANES), 1) < LANES // 2

    def weights(block):
        placed = []
        for dim in range(3):
            shifted = cell - offsets_ref[dim, pl.ds(block, 1), :]
            value = jnp.zeros((TILE, LANES), F32)
            for tap in range(taps):
                value = jnp.where(shifted == tap, kernel_ref[block, dim, pl.ds(tap, 1), :], value)
            placed.append(value)
        plane = jnp.concatenate([placed[0][i : i + 1] * placed[1] for i in range(TILE)], axis=0)
        depth = jnp.concatenate([samples_ref[block, pl.ds(c, 1), :] * placed[2] for c in range(2)], axis=0)
        return depth, plane

    def pair_body(pair, carry):
        depth_a, plane_a = weights(2 * pair)
        depth_b, plane_b = weights(2 * pair + 1)
        depth_high, depth_low = split(jnp.concatenate((depth_a, depth_b), axis=0))
        plane_high, plane_low = split(jnp.concatenate((plane_a, plane_b), axis=0))
        piece = lax.dot_general(
            jnp.concatenate((depth_high, depth_low, depth_high), axis=1),
            jnp.concatenate((plane_high, plane_high, plane_low), axis=1),
            (((1,), (1,)), ((), ())),
            preferred_element_type=F32,
        )
        out_ref[pair] = jnp.where(left, piece[: 2 * TILE], piece[2 * TILE :])
        return carry

    lax.fori_loop(0, blocks // 2, pair_body, 0, unroll=4)
    out_ref[blocks // 2] = jnp.broadcast_to(codes, (2 * TILE, LANES))


def tiles_kernel(conditions, first, *refs):
    arrays = len(conditions)
    places_ref = refs[0]
    source_refs = refs[1 : 1 + arrays]
    depth_ref, phases_ref = refs[1 + arrays : 3 + arrays]
    acc_refs = refs[-5 - PARTS : -5]
    token_ref, codes_ref, even_ref, odd_ref, arrived = refs[-5:]
    token_ref[...] = jnp.zeros_like(token_ref)
    stride = STRIDE
    pairs = source_refs[0].shape[0] - 1
    batch = 8
    batches = pairs // batch
    assert batches % 2 == 0

    def copies(index):
        return pltpu.make_async_copy(
            source_refs[index].at[pairs, pl.ds(0, TILE)], codes_ref.at[index], arrived.at[index]
        )

    for index in range(arrays):
        copies(index).start()

    if first:

        def clear(step, carry):
            at = pl.ds(pl.multiple_of(step * stride, stride), stride)
            for ref in acc_refs:
                ref[at, :] = jnp.zeros((stride, LANES), F32)
            return carry

        lax.fori_loop(0, NX // 2 // PARTS, clear, 0)

    for index in range(arrays):
        copies(index).wait()

    def add_source(index):
        tiles_ref = source_refs[index]

        def spectrum(number, to_ref):
            tiles = jnp.concatenate([tiles_ref[number * batch + place] for place in range(batch)], axis=1)
            high, low = split(tiles)
            to_ref[...] = lax.dot_general(
                jnp.concatenate((high, low, high), axis=0),
                depth_ref[...],
                (((0,), (0,)), ((), ())),
                preferred_element_type=F32,
            )

        def accumulate(number, from_ref):
            for tile in range(2 * batch):
                code = codes_ref[index, 0, number * 2 * batch + tile].astype(jnp.int32)
                base = lax.shift_right_logical(code, 7)
                phase = jnp.bitwise_and(code, PHASES - 1)
                cos = phases_ref[0, pl.ds(phase, 1), :]
                sin = phases_ref[1, pl.ds(phase, 1), :]
                for i in range(TILE):
                    row = tile * TILE * TILE + i * TILE
                    value = from_ref[row : row + TILE, :]
                    value = value * cos + pltpu.roll(value, LANES // 2, 1) * sin
                    acc_ref = acc_refs[i // CELLS]
                    at = pl.ds(pl.multiple_of(base * TILE + i % CELLS * stride, TILE), TILE)
                    acc_ref[at, :] = acc_ref[at, :] + value

        spectrum(0, even_ref)

        def add_pair(step, carry):
            number = 2 * step
            spectrum(number + 1, odd_ref)
            accumulate(number, even_ref)
            spectrum(jnp.minimum(number + 2, batches - 2), even_ref)
            accumulate(number + 1, odd_ref)
            return carry

        lax.fori_loop(0, batches // 2, add_pair, 0)

    for index, condition in enumerate(conditions):
        if condition is None:
            add_source(index)
        else:
            side, depth = condition
            holds = places_ref[0] >= depth if side == "from" else places_ref[0] < depth
            pl.when(holds)(functools.partial(add_source, index))


def columns_kernel(*refs):
    column_ref = refs[PARTS]
    acc_refs = refs[PARTS + 1 :]
    third = NY // 3
    rows = column_ref.shape[1] // 2
    turn = jnp.where(lax.broadcasted_iota(jnp.int32, (1, LANES), 1) < LANES // 2, -1.0, 1.0)

    def columns(step, carry):
        start = pl.multiple_of(step * STRIDE, TILE)
        for pair in range(0, PARTS, 2):
            folded = ([], [], [])
            for ref in acc_refs[pair : pair + 2]:
                first, second, last = (ref[pl.ds(start + third * part, third), :] for part in range(3))
                both = second + last
                across = pltpu.roll(second - last, LANES // 2, 1) * (turn * math.sqrt(0.75))
                middle = first - 0.5 * both
                folded[0].append(first + both)
                folded[1].append(middle + across)
                folded[2].append(middle - across)
            for residue in range(3):
                high, low = split(jnp.concatenate(folded[residue], axis=1))
                product = jnp.dot(
                    column_ref[residue], jnp.concatenate((high, low, high), axis=0), preferred_element_type=F32
                )
                for side, ref in enumerate(acc_refs[pair : pair + 2]):
                    lanes = slice(side * LANES, (side + 1) * LANES)
                    ref[pl.ds(start + residue * rows, rows), :] = (
                        product[:rows, lanes] + pltpu.roll(product[rows:, lanes], LANES // 2, 1) * turn
                    )
        return carry

    lax.fori_loop(0, NX // 2 // PARTS, columns, 0, unroll=4)


def rows_kernel(relative, first, count, chunks, grid_rows, addends, planes_padded, places_ref, *refs):
    acc_refs, row_ref, addend_refs, out_ref = refs[:PARTS], refs[PARTS], refs[PARTS + 1 : -1], refs[-1]
    assert len(addend_refs) == addends
    rows = grid_rows * chunks * TILE
    device = jnp.bitwise_xor(places_ref[1], relative)
    lane = lax.broadcasted_iota(jnp.int32, (PLANES, LANES), 1)

    def block(step, carry):
        chunk, residue = step // 3, step % 3
        start = residue * rows + (device * chunks + first + chunk) * TILE
        turned = []
        for row in range(TILE):
            at = pl.ds(start + row, NX // 2 // PARTS, stride=STRIDE)
            turned.append(jnp.concatenate([ref[at, :] for ref in acc_refs], axis=0).T)
        parts = []
        for odd in range(2):
            at = odd * PLANES
            stacked = [value[part * 64 + at : part * 64 + at + PLANES] for value in turned for part in range(2)]
            high, low = split(jnp.concatenate(stacked, axis=0))
            size = high.shape[0]
            both = jnp.dot(jnp.concatenate((high, low), axis=0), row_ref[odd, 0], preferred_element_type=F32)
            product = both[:size] + both[size:] + jnp.dot(high, row_ref[odd, 1], preferred_element_type=F32)
            sides = []
            for row in range(TILE):
                real = product[2 * row * PLANES : (2 * row + 1) * PLANES]
                imag = product[(2 * row + 1) * PLANES : (2 * row + 2) * PLANES]
                sides.append((real[:, :LANES] - imag[:, LANES:], real[:, LANES:] + imag[:, :LANES]))
            parts.append(sides)
        for slot in range(TILE // 2):
            place = chunk * (CHUNK // 2) + 3 * slot + residue
            for part in range(2):
                even = [parts[0][slot + side * TILE // 2][part] for side in range(2)]
                odd = [parts[1][slot + side * TILE // 2][part] for side in range(2)]
                values = [jnp.where(lane < NX // 4, even[side], odd[side]) for side in range(2)]
                values.append(jnp.where(lane < LANES // 2, odd[0], pltpu.roll(odd[1], LANES // 2, 1)))
                for number, value in enumerate(values):
                    planes = pl.ds(part * planes_padded, planes_padded)
                    total = value[:planes_padded]
                    for ref in addend_refs:
                        total = total + ref[first * (CHUNK // 2) + place, number, planes]
                    out_ref[place, number, planes] = total
        return carry

    lax.fori_loop(0, 3 * count, block, 0, unroll=3)


def finish_kernel(chunk, planes_padded, parts, refs):
    part_refs = refs[:parts]
    order_ref, first_ref, second_ref, third_ref = refs[parts : parts + 4]
    out_ref = refs[-1]
    planes = out_ref.shape[1]
    slots = part_refs[0].shape[0]
    stride = 6 * planes_padded
    flats = [ref.reshape(slots * stride, LANES) for ref in part_refs]
    order = order_ref[...]
    shape = (CHUNK, second_ref.shape[1])
    here = lax.broadcasted_iota(jnp.int32, shape, 1) == lax.broadcasted_iota(jnp.int32, shape, 0) + chunk * CHUNK
    second = jnp.sum(jnp.where(here, second_ref[...], 0.0), axis=1, keepdims=True)
    scale = second * first_ref[...]
    for part in range(2):
        for group in range(0, planes, TILE):
            members = range(group, min(group + TILE, planes))
            mains, rests = [], []
            for plane in members:
                values = []
                for number in range(3):
                    at = pl.ds((number * 2 + part) * planes_padded + plane, slots, stride=stride)
                    total = flats[0][at, :]
                    for flat in flats[1:]:
                        total = total + flat[at, :]
                    values.append(total)
                mains.append(jnp.concatenate(values[:2], axis=0))
                rests.append(jnp.concatenate((values[2], pltpu.roll(values[2], LANES // 2, 1)), axis=0))
            main = split(jnp.concatenate(mains, axis=0))
            rest = split(jnp.concatenate(rests, axis=0))
            ordered = jnp.dot(jnp.concatenate(main + rest, axis=1), order, preferred_element_type=F32)
            for index, plane in enumerate(members):
                out_ref[part, plane] = ordered[index * 2 * slots : (index + 1) * 2 * slots] * (scale * third_ref[plane])


def on_device(samples, kernel, offsets, owners, tile_ids, deapod_first, deapod_second, deapod_third):
    grid_rows = lax.axis_size("gx")
    grid_cols = lax.axis_size("gy")
    blocks = samples.shape[0]
    block_width = samples.shape[2]
    assert block_width == LANES and blocks == LANES
    tile_rows = NX // (TILE * grid_rows)
    tile_cols = NY // (TILE * grid_cols)
    planes = deapod_third.shape[0]
    per_device = deapod_second.shape[0]
    assert per_device % CHUNK == 0
    chunks = per_device // CHUNK
    slots = CHUNK // 2
    planes_padded = -(-planes // 8) * 8
    vmem = pl.BlockSpec(memory_space=pltpu.VMEM)
    params = pltpu.CompilerParams(vmem_limit_bytes=VMEM_LIMIT)

    def in_hbm(arrays):
        return [pltpu.with_memory_space_constraint(array, pltpu.HBM) for array in arrays]

    tiles = pl.pallas_call(
        functools.partial(spread_kernel, tile_rows, tile_cols, grid_cols, grid_rows * grid_cols),
        out_shape=pltpu.HBM((blocks // 2 + 1, 2 * TILE, LANES), F32),
        in_specs=[vmem] * 5,
        out_specs=vmem,
        compiler_params=params,
        name="spread",
    )(*in_hbm([samples, kernel, offsets.transpose(1, 0, 2), owners.reshape(1, blocks), tile_ids.reshape(1, blocks)]))

    along = grid_cols // Z_CHIPS
    deep_at = lax.div(lax.axis_index("gy").astype(jnp.int32), jnp.int32(along))

    def shift(value, senders, deep, wide):
        moves = [
            (z * along + y, (z + deep) * along + (y + wide) % along) for z in senders for y in range(along)
        ]
        return lax.ppermute(value, "gy", moves)

    places = jnp.stack((deep_at, lax.axis_index("gx").astype(jnp.int32)))
    gy = lax.axis_index("gy")
    matrices, phases = depth_tables(planes)
    matrix = lax.dynamic_index_in_dim(jnp.asarray(matrices), gy, 0, keepdims=False)
    phase_rows = lax.dynamic_index_in_dim(jnp.asarray(phases), gy, 0, keepdims=False)
    column = jnp.asarray(column_tables())
    half = NX // 2
    smem = pl.BlockSpec(memory_space=pltpu.SMEM)
    acc_shape = (half // PARTS * STRIDE, LANES)

    def in_vmem(arrays):
        return [pltpu.with_memory_space_constraint(array, pltpu.VMEM) for array in arrays]

    def condition(steps):
        if steps == 0:
            return None
        return ("from", steps) if steps > 0 else ("below", Z_CHIPS + steps)

    def add_tiles(sources, acc):
        conditions = [condition(steps) for steps, _ in sources]
        spectra = pltpu.VMEM((16 * TILE * TILE, LANES), F32)
        kept = [jax.ShapeDtypeStruct(acc_shape, F32) if acc else pltpu.VMEM(acc_shape, F32)] * PARTS
        inputs = len(sources) + 3
        *acc, token = pl.pallas_call(
            functools.partial(tiles_kernel, conditions, not acc),
            out_shape=kept + [jax.ShapeDtypeStruct((TILE, LANES), F32)],
            in_specs=[smem] + [vmem] * (inputs - 1 + len(acc)),
            out_specs=[vmem] * (PARTS + 1),
            input_output_aliases={inputs + part: part for part in range(PARTS)} if acc else {},
            scratch_shapes=[
                pltpu.SMEM((len(sources), TILE, LANES), F32),
                spectra,
                spectra,
                pltpu.SemaphoreType.DMA((len(sources),)),
            ],
            compiler_params=params,
            cost_estimate=pl.CostEstimate(flops=0, bytes_accessed=len(sources) << 23, transcendentals=0),
            name="tiles",
        )(places, *[array for _, array in sources], *in_hbm([matrix, phase_rows]), *in_vmem(acc))
        return acc, token

    def after(value, token):
        return lax.optimization_barrier((value, token))[0]

    held, crossed_y = {0: tiles}, {}
    acc, waiting = [], [(0, tiles)]
    token = None
    for steps in range(1, Z_CHIPS + 1):
        if steps < Z_CHIPS:
            for signed in (steps, -steps):
                value = held[signed - signed // steps]
                value = value if token is None else after(value, token)
                senders = range(steps - 1, Z_CHIPS - 1) if signed > 0 else range(1, Z_CHIPS + 1 - steps)
                held[signed] = shift(value, senders, signed // steps, 0)
        behind = []
        for signed in sorted({steps - 1, 1 - steps}):
            holders = range(signed, Z_CHIPS) if signed >= 0 else range(Z_CHIPS + signed)
            for wide in range(1, along):
                value = held[signed] if token is None else after(held[signed], token)
                crossed_y[signed, wide] = shift(value, holders, 0, wide)
                behind.append((signed, crossed_y[signed, wide]))
        acc, token = add_tiles(waiting, acc)
        waiting = behind
        if steps < Z_CHIPS:
            waiting = [(steps, held[steps]), (-steps, held[-steps])] + behind
    acc, _ = add_tiles(waiting, acc)

    acc = pl.pallas_call(
        columns_kernel,
        out_shape=[jax.ShapeDtypeStruct(acc_shape, F32)] * PARTS,
        in_specs=[vmem] * (PARTS + 1),
        out_specs=[vmem] * PARTS,
        input_output_aliases={part: part for part in range(PARTS)},
        compiler_params=params,
        name="columns",
    )(*in_vmem(acc), *in_hbm([column]))

    row_table = jnp.asarray(row_tables())
    part_shape = (3, 2 * planes_padded, LANES)

    def rows_for(relative, first, count, addends, after):
        def body(*refs):
            operands = 2 + PARTS + len(addends)
            rows_kernel(
                relative, first, count, chunks, grid_rows, len(addends), planes_padded, *refs[:operands], refs[-1]
            )

        return pl.pallas_call(
            body,
            in_specs=[smem] + [vmem] * (1 + PARTS + len(addends)) + [pl.BlockSpec(memory_space=pl.ANY)] * len(after),
            out_specs=vmem,
            out_shape=pltpu.HBM((count * slots,) + part_shape, F32),
            compiler_params=params,
            cost_estimate=pl.CostEstimate(flops=1, bytes_accessed=1, transcendentals=0),
            name="rows",
        )(places, *in_vmem(acc), *in_hbm([row_table] + addends + after))

    def swap(value, bit):
        return lax.ppermute(value, "gx", [(index, index ^ bit) for index in range(grid_rows)])

    last = []

    def rows_next(relative, first, count, addends):
        part = rows_for(relative, first, count, addends, last)
        last[:] = [part]
        return part

    def arrivals(relative, top):
        arrived = []
        bit = 1
        while bit <= top:
            arrived.append(swap(rows_next(relative | bit, 0, chunks, arrivals(relative | bit, bit // 2)), bit))
            bit *= 2
        return arrived

    top = grid_rows // 2
    far = arrivals(top, top // 2)
    parts = []
    for chunk in range(chunks):
        if top == 2:
            near = [(swap(rows_next(1, chunk, 1, []), 1), 0)]
        elif chunk == 0:
            near = [(array, None) for array in arrivals(0, top // 2)]
        parts.append([(array, chunk if place is None else place) for array, place in near])
        parts[-1].append((swap(rows_next(top, chunk, 1, far), top), 0))
    kept = rows_next(0, 0, chunks, [])
    parts = [[(kept, chunk)] + arrays for chunk, arrays in enumerate(parts)]

    image = None
    for chunk in range(chunks):

        def finish(*refs, chunk=chunk):
            finish_kernel(chunk, planes_padded, len(parts[chunk]), refs)

        earlier = [] if image is None else [image]
        image = pl.pallas_call(
            finish,
            grid=(1,),
            out_shape=jax.ShapeDtypeStruct((2, planes, per_device, NX // 2), F32),
            in_specs=[
                pl.BlockSpec((slots,) + part_shape, lambda step, place=place: (place, 0, 0, 0))
                for _, place in parts[chunk]
            ]
            + [
                pl.BlockSpec((4 * LANES, NX // 2), lambda step: (0, 0)),
                pl.BlockSpec((1, NX // 2), lambda step: (0, 0)),
                pl.BlockSpec((1, per_device), lambda step: (0, 0)),
                pl.BlockSpec(memory_space=pltpu.SMEM),
            ]
            + [pl.BlockSpec(memory_space=pl.ANY)] * len(earlier),
            out_specs=pl.BlockSpec((2, planes, CHUNK, NX // 2), lambda step, chunk=chunk: (0, 0, chunk, 0)),
            input_output_aliases={len(parts[chunk]) + 4: 0} if earlier else {},
            compiler_params=params,
            name="finish",
        )(
            *in_hbm([array for array, _ in parts[chunk]]),
            jnp.asarray(order_tables()),
            deapod_first[None, :],
            deapod_second[None, :],
            deapod_third,
            *earlier,
        )
    return image


def solution(mesh):
    in_specs = (
        P(("gx", "gy"), None, None),
        P(("gx", "gy"), None, None, None),
        P(("gx", "gy"), None, None),
        P(("gx", "gy"), None),
        P(("gx", "gy")),
        P(),
        P("gx"),
        P("gy"),
    )
    out_specs = P(None, "gy", "gx", None)
    return jax.shard_map(
        on_device, mesh=mesh, in_specs=in_specs, out_specs=out_specs, check_vma=False
    )
```

```python
import functools
import math

import jax
import jax.numpy as jnp
import ml_dtypes
import numpy as np
from jax import lax
from jax.experimental import pallas as pl
from jax.experimental.pallas import tpu as pltpu
from jax.sharding import PartitionSpec as P

NX = 384
NY = 384
NZ = 384
TILE = 8
LANES = 128
PLANES = 32
CHUNK = 24
Z_CHIPS = 4
PARTS = 4
CELLS = TILE // PARTS
STRIDE = NY + TILE
PHASES = 128
BF16 = jnp.bfloat16
F32 = jnp.float32
VMEM_LIMIT = 8 * 1024 * 1024


def halves(array):
    high = array.astype(ml_dtypes.bfloat16)
    low = (array - high.astype(np.float64)).astype(ml_dtypes.bfloat16)
    return high, low


def split(value):
    high = value.astype(BF16)
    return high, (value - high.astype(F32)).astype(BF16)


def waves(freq, position, length):
    steps = np.mod(freq[:, None] * position[None, :], length)
    phase = 2.0 * math.pi * steps / length
    return np.cos(phase), np.sin(phase)


def depth_tables(planes):
    matrices, phases = [], []
    lane_part = np.arange(LANES) // 64
    lane_odd = np.arange(LANES) // 32 % 2
    lane_plane = np.arange(LANES) % 32
    used = (lane_plane < planes).astype(np.float64)
    for index in range(NZ // 2 // planes):
        position = index * planes + lane_plane - NZ // 4
        cos, sin = waves(np.arange(TILE) - NZ // 2, position, NZ)
        cos, sin = cos * used / math.sqrt(NZ), sin * used / math.sqrt(NZ)
        real = np.where(lane_part == 0, cos, sin)
        imag = np.where(lane_part == 0, -sin, cos)
        high, low = halves(np.concatenate((real, imag)))
        matrices.append(np.concatenate((high, high, low)))
        cos, sin = waves(np.arange(NZ // TILE), position, NZ // TILE)
        sign = np.where(lane_odd == 1, -1.0, 1.0)[None, :]
        sin = sin * np.where(lane_part == 0, -1.0, 1.0)[None, :]
        phases.append(np.stack((np.concatenate((cos, cos * sign)), np.concatenate((sin, sin * sign)))))
    return np.stack(matrices), np.stack(phases).astype(np.float32)


def column_tables():
    third = NY // 3
    out = []
    for residue in range(3):
        cos, sin = waves(3 * np.arange(NY // 6) + residue - NY // 4, np.arange(third) - NY // 2, NY)
        high, low = halves(np.concatenate((cos, sin)) / math.sqrt(NY))
        out.append(np.concatenate((high, high, low), axis=1))
    return np.stack(out)


def row_tables():
    half = NX // 2
    freq = np.arange(half).reshape(-1, PARTS, CELLS).transpose(1, 0, 2).reshape(-1) - half
    quarter = NX // 4
    out = []
    for parity in range(2):
        position = 2 * np.arange(quarter) + parity - NX // 4
        cos, sin = waves(freq, position, NX)
        table = np.zeros((half, 2 * LANES))
        lanes = (np.arange(quarter) + parity * quarter) % LANES
        table[:, lanes] = cos / math.sqrt(NX)
        table[:, LANES + lanes] = sin / math.sqrt(NX)
        out.append(np.stack(halves(table)))
    return np.stack(out)


def order_tables():
    first = np.zeros((LANES, NX // 2))
    second = np.zeros((LANES, NX // 2))
    quarter = NX // 4
    for m1 in range(NX // 2):
        place = m1 // 2 + m1 % 2 * quarter
        if place < LANES:
            first[place, m1] = 1.0
        else:
            second[place - LANES, m1] = 1.0
    return np.concatenate((first, first, second, second)).astype(ml_dtypes.bfloat16)


def divide(value, divisor, limit):
    for shift in range(8, 24):
        factor = (1 << shift) // divisor + 1
        tried = np.arange(limit, dtype=np.int64)
        if factor * limit < 1 << 31 and np.array_equal(tried * factor >> shift, tried // divisor):
            return lax.shift_right_logical(value * factor, shift)
    raise ValueError(divisor)


def spread_kernel(tile_rows, tile_cols, grid_cols, devices, samples_ref, kernel_ref, offsets_ref, owners_ref, ids_ref, out_ref):
    owner, tile_id = owners_ref[...], ids_ref[...]
    tile_depth = NZ // TILE
    tiles_device = tile_rows * tile_cols * tile_depth
    owner_row = divide(owner, grid_cols, devices)
    tile_row = divide(tile_id, tile_cols * tile_depth, tiles_device)
    tile_col = divide(tile_id, tile_depth, tiles_device)
    row = owner_row * tile_rows + tile_row
    col = (owner - owner_row * grid_cols) * tile_cols + tile_col - tile_row * tile_cols
    folds = NX // TILE // 2
    upper = (row >= folds).astype(jnp.int32)
    base = (row - upper * folds) * (CELLS * STRIDE // TILE) + col
    phase = tile_id - tile_col * tile_depth + upper * tile_depth
    codes = (base * PHASES + phase).astype(F32)

    blocks = samples_ref.shape[0]
    taps = kernel_ref.shape[2]
    cell = lax.broadcasted_iota(jnp.int32, (TILE, LANES), 0)
    left = lax.broadcasted_iota(jnp.int32, (2 * TILE, LANES), 1) < LANES // 2

    def weights(block):
        placed = []
        for dim in range(3):
            shifted = cell - offsets_ref[dim, pl.ds(block, 1), :]
            value = jnp.zeros((TILE, LANES), F32)
            for tap in range(taps):
                value = jnp.where(shifted == tap, kernel_ref[block, dim, pl.ds(tap, 1), :], value)
            placed.append(value)
        plane = jnp.concatenate([placed[0][i : i + 1] * placed[1] for i in range(TILE)], axis=0)
        depth = jnp.concatenate([samples_ref[block, pl.ds(c, 1), :] * placed[2] for c in range(2)], axis=0)
        return depth, plane

    def pair_body(pair, carry):
        depth_a, plane_a = weights(2 * pair)
        depth_b, plane_b = weights(2 * pair + 1)
        depth_high, depth_low = split(jnp.concatenate((depth_a, depth_b), axis=0))
        plane_high, plane_low = split(jnp.concatenate((plane_a, plane_b), axis=0))
        piece = lax.dot_general(
            jnp.concatenate((depth_high, depth_low, depth_high), axis=1),
            jnp.concatenate((plane_high, plane_high, plane_low), axis=1),
            (((1,), (1,)), ((), ())),
            preferred_element_type=F32,
        )
        out_ref[pair] = jnp.where(left, piece[: 2 * TILE], piece[2 * TILE :])
        return carry

    lax.fori_loop(0, blocks // 2, pair_body, 0, unroll=4)
    out_ref[blocks // 2] = jnp.broadcast_to(codes, (2 * TILE, LANES))


def tiles_kernel(conditions, first, *refs):
    arrays = len(conditions)
    places_ref = refs[0]
    source_refs = refs[1 : 1 + arrays]
    depth_tables_ref, phase_tables_ref = refs[1 + arrays : 3 + arrays]
    acc_refs = refs[-7 - PARTS : -7]
    token_ref, codes_ref, depth_ref, phases_ref, even_ref, odd_ref, arrived = refs[-7:]
    token_ref[...] = jnp.zeros_like(token_ref)
    stride = STRIDE
    pairs = source_refs[0].shape[0] - 1
    batch = 8
    batches = pairs // batch
    assert batches % 2 == 0

    def copies(index):
        return pltpu.make_async_copy(
            source_refs[index].at[pairs, pl.ds(0, TILE)], codes_ref.at[index], arrived.at[index]
        )

    tables = [
        pltpu.make_async_copy(depth_tables_ref.at[places_ref[2]], depth_ref, arrived.at[arrays]),
        pltpu.make_async_copy(phase_tables_ref.at[places_ref[2]], phases_ref, arrived.at[arrays + 1]),
    ]
    for index in range(arrays):
        copies(index).start()
    for table in tables:
        table.start()

    if first:

        def clear(step, carry):
            at = pl.ds(pl.multiple_of(step * stride, stride), stride)
            for ref in acc_refs:
                ref[at, :] = jnp.zeros((stride, LANES), F32)
            return carry

        lax.fori_loop(0, NX // 2 // PARTS, clear, 0)

    for index in range(arrays):
        copies(index).wait()
    for table in tables:
        table.wait()

    def add_source(index):
        tiles_ref = source_refs[index]

        def spectrum(number, to_ref):
            tiles = jnp.concatenate([tiles_ref[number * batch + place] for place in range(batch)], axis=1)
            high, low = split(tiles)
            to_ref[...] = lax.dot_general(
                jnp.concatenate((high, low, high), axis=0),
                depth_ref[...],
                (((0,), (0,)), ((), ())),
                preferred_element_type=F32,
            )

        def accumulate(number, from_ref):
            for tile in range(2 * batch):
                code = codes_ref[index, 0, number * 2 * batch + tile].astype(jnp.int32)
                base = lax.shift_right_logical(code, 7)
                phase = jnp.bitwise_and(code, PHASES - 1)
                cos = phases_ref[0, pl.ds(phase, 1), :]
                sin = phases_ref[1, pl.ds(phase, 1), :]
                for i in range(TILE):
                    row = tile * TILE * TILE + i * TILE
                    value = from_ref[row : row + TILE, :]
                    value = value * cos + pltpu.roll(value, LANES // 2, 1) * sin
                    acc_ref = acc_refs[i // CELLS]
                    at = pl.ds(pl.multiple_of(base * TILE + i % CELLS * stride, TILE), TILE)
                    acc_ref[at, :] = acc_ref[at, :] + value

        spectrum(0, even_ref)

        def add_pair(step, carry):
            number = 2 * step
            spectrum(number + 1, odd_ref)
            accumulate(number, even_ref)
            spectrum(jnp.minimum(number + 2, batches - 2), even_ref)
            accumulate(number + 1, odd_ref)
            return carry

        lax.fori_loop(0, batches // 2, add_pair, 0, unroll=2)

    for index, condition in enumerate(conditions):
        if condition is None:
            add_source(index)
        else:
            holds = places_ref[0] == condition[0]
            for depth in condition[1:]:
                holds = jnp.logical_or(holds, places_ref[0] == depth)
            pl.when(holds)(functools.partial(add_source, index))


def columns_kernel(*refs):
    column_ref = refs[PARTS]
    acc_refs = refs[PARTS + 1 :]
    third = NY // 3
    rows = column_ref.shape[1] // 2
    turn = jnp.where(lax.broadcasted_iota(jnp.int32, (1, LANES), 1) < LANES // 2, -1.0, 1.0)

    def columns(step, carry):
        start = pl.multiple_of(step * STRIDE, TILE)
        for pair in range(0, PARTS, 2):
            folded = ([], [], [])
            for ref in acc_refs[pair : pair + 2]:
                first, second, last = (ref[pl.ds(start + third * part, third), :] for part in range(3))
                both = second + last
                across = pltpu.roll(second - last, LANES // 2, 1) * (turn * math.sqrt(0.75))
                middle = first - 0.5 * both
                folded[0].append(first + both)
                folded[1].append(middle + across)
                folded[2].append(middle - across)
            for residue in range(3):
                high, low = split(jnp.concatenate(folded[residue], axis=1))
                product = jnp.dot(
                    column_ref[residue], jnp.concatenate((high, low, high), axis=0), preferred_element_type=F32
                )
                for side, ref in enumerate(acc_refs[pair : pair + 2]):
                    lanes = slice(side * LANES, (side + 1) * LANES)
                    ref[pl.ds(start + residue * rows, rows), :] = (
                        product[:rows, lanes] + pltpu.roll(product[rows:, lanes], LANES // 2, 1) * turn
                    )
        return carry

    lax.fori_loop(0, NX // 2 // PARTS, columns, 0, unroll=8)


def rows_kernel(relative, first, count, chunks, grid_rows, addends, planes_padded, places_ref, *refs):
    acc_refs, row_ref, addend_refs, out_ref = refs[:PARTS], refs[PARTS], refs[PARTS + 1 : -1], refs[-1]
    assert len(addend_refs) == addends
    rows = grid_rows * chunks * TILE
    device = jnp.bitwise_xor(places_ref[1], relative)
    lane = lax.broadcasted_iota(jnp.int32, (PLANES, LANES), 1)

    def block(step, carry):
        chunk, residue = step // 3, step % 3
        start = residue * rows + (device * chunks + first + chunk) * TILE
        turned = []
        for row in range(TILE):
            at = pl.ds(start + row, NX // 2 // PARTS, stride=STRIDE)
            turned.append(jnp.concatenate([ref[at, :] for ref in acc_refs], axis=0).T)
        parts = []
        for odd in range(2):
            at = odd * PLANES
            stacked = [value[part * 64 + at : part * 64 + at + PLANES] for value in turned for part in range(2)]
            high, low = split(jnp.concatenate(stacked, axis=0))
            size = high.shape[0]
            both = jnp.dot(jnp.concatenate((high, low), axis=0), row_ref[odd, 0], preferred_element_type=F32)
            product = both[:size] + both[size:] + jnp.dot(high, row_ref[odd, 1], preferred_element_type=F32)
            sides = []
            for row in range(TILE):
                real = product[2 * row * PLANES : (2 * row + 1) * PLANES]
                imag = product[(2 * row + 1) * PLANES : (2 * row + 2) * PLANES]
                sides.append((real[:, :LANES] - imag[:, LANES:], real[:, LANES:] + imag[:, :LANES]))
            parts.append(sides)
        for slot in range(TILE // 2):
            place = chunk * (CHUNK // 2) + 3 * slot + residue
            for part in range(2):
                even = [parts[0][slot + side * TILE // 2][part] for side in range(2)]
                odd = [parts[1][slot + side * TILE // 2][part] for side in range(2)]
                values = [jnp.where(lane < NX // 4, even[side], odd[side]) for side in range(2)]
                values.append(jnp.where(lane < LANES // 2, odd[0], pltpu.roll(odd[1], LANES // 2, 1)))
                for number, value in enumerate(values):
                    planes = pl.ds(part * planes_padded, planes_padded)
                    total = value[:planes_padded]
                    for ref in addend_refs:
                        shift = first * (CHUNK // 2) if ref.shape[0] > out_ref.shape[0] else 0
                        total = total + ref[shift + place, number, planes]
                    out_ref[place, number, planes] = total
        return carry

    lax.fori_loop(0, 3 * count, block, 0, unroll=3)


def finish_kernel(chunk, planes_padded, parts, refs):
    part_refs = refs[:parts]
    order_ref, first_ref, second_ref, third_ref = refs[parts : parts + 4]
    out_ref = refs[-1]
    planes = out_ref.shape[1]
    slots = part_refs[0].shape[0]
    stride = 6 * planes_padded
    flats = [ref.reshape(slots * stride, LANES) for ref in part_refs]
    order = order_ref[...]
    shape = (CHUNK, second_ref.shape[1])
    here = lax.broadcasted_iota(jnp.int32, shape, 1) == lax.broadcasted_iota(jnp.int32, shape, 0) + chunk * CHUNK
    second = jnp.sum(jnp.where(here, second_ref[...], 0.0), axis=1, keepdims=True)
    scale = second * first_ref[...]
    for part in range(2):
        for group in range(0, planes, TILE):
            members = range(group, min(group + TILE, planes))
            mains, rests = [], []
            for plane in members:
                values = []
                for number in range(3):
                    at = pl.ds((number * 2 + part) * planes_padded + plane, slots, stride=stride)
                    total = flats[0][at, :]
                    for flat in flats[1:]:
                        total = total + flat[at, :]
                    values.append(total)
                mains.append(jnp.concatenate(values[:2], axis=0))
                rests.append(jnp.concatenate((values[2], pltpu.roll(values[2], LANES // 2, 1)), axis=0))
            main = split(jnp.concatenate(mains, axis=0))
            rest = split(jnp.concatenate(rests, axis=0))
            ordered = jnp.dot(jnp.concatenate(main + rest, axis=1), order, preferred_element_type=F32)
            for index, plane in enumerate(members):
                out_ref[part, plane] = ordered[index * 2 * slots : (index + 1) * 2 * slots] * (scale * third_ref[plane])


def on_device(samples, kernel, offsets, owners, tile_ids, deapod_first, deapod_second, deapod_third):
    grid_rows = lax.axis_size("gx")
    grid_cols = lax.axis_size("gy")
    blocks = samples.shape[0]
    block_width = samples.shape[2]
    assert block_width == LANES and blocks == LANES
    tile_rows = NX // (TILE * grid_rows)
    tile_cols = NY // (TILE * grid_cols)
    planes = deapod_third.shape[0]
    per_device = deapod_second.shape[0]
    assert per_device % CHUNK == 0
    chunks = per_device // CHUNK
    slots = CHUNK // 2
    planes_padded = -(-planes // 8) * 8
    vmem = pl.BlockSpec(memory_space=pltpu.VMEM)
    params = pltpu.CompilerParams(vmem_limit_bytes=VMEM_LIMIT)

    def in_hbm(arrays):
        return [pltpu.with_memory_space_constraint(array, pltpu.HBM) for array in arrays]

    tiles = pl.pallas_call(
        functools.partial(spread_kernel, tile_rows, tile_cols, grid_cols, grid_rows * grid_cols),
        out_shape=pltpu.HBM((blocks // 2 + 1, 2 * TILE, LANES), F32),
        in_specs=[vmem] * 5,
        out_specs=vmem,
        compiler_params=params,
        name="spread",
    )(*in_hbm([samples, kernel, offsets.transpose(1, 0, 2), owners.reshape(1, blocks), tile_ids.reshape(1, blocks)]))

    along = grid_cols // Z_CHIPS
    deep_at = lax.div(lax.axis_index("gy").astype(jnp.int32), jnp.int32(along))

    def send(value, moves_z, wide):
        moves = [(a * along + y, b * along + (y + wide) % along) for a, b in moves_z for y in range(along)]
        return lax.ppermute(value, "gy", moves)

    places = jnp.stack((deep_at, lax.axis_index("gx").astype(jnp.int32), lax.axis_index("gy").astype(jnp.int32)))
    matrices, phases = (jnp.asarray(table) for table in depth_tables(planes))
    column = jnp.asarray(column_tables())
    half = NX // 2
    smem = pl.BlockSpec(memory_space=pltpu.SMEM)
    acc_shape = (half // PARTS * STRIDE, LANES)

    def in_vmem(arrays):
        return [pltpu.with_memory_space_constraint(array, pltpu.VMEM) for array in arrays]

    def add_tiles(sources, acc):
        conditions = [None if len(holders) == Z_CHIPS else tuple(holders) for holders, _ in sources]
        spectra = pltpu.VMEM((16 * TILE * TILE, LANES), F32)
        kept = [jax.ShapeDtypeStruct(acc_shape, F32) if acc else pltpu.VMEM(acc_shape, F32)] * PARTS
        inputs = len(sources) + 3
        *acc, token = pl.pallas_call(
            functools.partial(tiles_kernel, conditions, not acc),
            out_shape=kept + [jax.ShapeDtypeStruct((TILE, LANES), F32)],
            in_specs=[smem] + [vmem] * len(sources) + [pl.BlockSpec(memory_space=pl.ANY)] * 2 + [vmem] * len(acc),
            out_specs=[vmem] * (PARTS + 1),
            input_output_aliases={inputs + part: part for part in range(PARTS)} if acc else {},
            scratch_shapes=[
                pltpu.SMEM((len(sources), TILE, LANES), F32),
                pltpu.VMEM(matrices.shape[1:], BF16),
                pltpu.VMEM(phases.shape[1:], F32),
                spectra,
                spectra,
                pltpu.SemaphoreType.DMA((len(sources) + 2,)),
            ],
            compiler_params=params,
            cost_estimate=pl.CostEstimate(flops=0, bytes_accessed=len(sources) << 23, transcendentals=0),
            name="tiles",
        )(places, *[array for _, array in sources], *in_hbm([matrices, phases]), *in_vmem(acc))
        return acc, token

    def after(value, token):
        return lax.optimization_barrier((value, token))[0]

    def across(value, holders):
        return [(holders, send(value, [(z, z) for z in holders], wide)) for wide in range(1, along)]

    every, ends = range(Z_CHIPS), (0, Z_CHIPS - 1)
    above, below = range(1, Z_CHIPS), range(Z_CHIPS - 1)
    upper, lower = range(2, Z_CHIPS), range(Z_CHIPS - 2)
    from_below = send(tiles, [(z, z + 1) for z in below], 0)
    from_above = send(tiles, [(z, z - 1) for z in above], 0)
    from_end = send(tiles, [ends, ends[::-1]], 0)
    partner = across(tiles, every)
    acc, token = add_tiles([(every, tiles)], [])
    near_below, near_above = after(from_below, token), after(from_above, token)
    from_lower = send(near_below, [(z - 1, z) for z in upper], 0)
    from_upper = send(near_above, [(z + 1, z) for z in lower], 0)
    partner_near = across(near_below, above) + across(near_above, below)
    acc, token = add_tiles([(above, from_below), (below, from_above)] + partner, acc)
    partner_end = across(after(from_end, token), ends)
    partner_far = across(after(from_lower, token), upper) + across(after(from_upper, token), lower)
    acc, token = add_tiles([(ends, from_end)] + partner_near, acc)
    acc, token = add_tiles([(upper, from_lower), (lower, from_upper)] + partner_end, acc)
    acc, _ = add_tiles(partner_far, acc)

    acc = pl.pallas_call(
        columns_kernel,
        out_shape=[jax.ShapeDtypeStruct(acc_shape, F32)] * PARTS,
        in_specs=[vmem] * (PARTS + 1),
        out_specs=[vmem] * PARTS,
        input_output_aliases={part: part for part in range(PARTS)},
        compiler_params=params,
        name="columns",
    )(*in_vmem(acc), *in_hbm([column]))

    row_table = jnp.asarray(row_tables())
    part_shape = (3, 2 * planes_padded, LANES)

    def rows_for(relative, first, count, addends, after):
        def body(*refs):
            operands = 2 + PARTS + len(addends)
            rows_kernel(
                relative, first, count, chunks, grid_rows, len(addends), planes_padded, *refs[:operands], refs[-1]
            )

        return pl.pallas_call(
            body,
            in_specs=[smem] + [vmem] * (1 + PARTS + len(addends)) + [pl.BlockSpec(memory_space=pl.ANY)] * len(after),
            out_specs=vmem,
            out_shape=pltpu.HBM((count * slots,) + part_shape, F32),
            compiler_params=params,
            cost_estimate=pl.CostEstimate(flops=1, bytes_accessed=1, transcendentals=0),
            name="rows",
        )(places, *in_vmem(acc), *in_hbm([row_table] + addends + after))

    def swap(value, bit):
        return lax.ppermute(value, "gx", [(index, index ^ bit) for index in range(grid_rows)])

    last = []

    def rows_next(relative, first, count, addends):
        part = rows_for(relative, first, count, addends, last)
        last[:] = [part]
        return part

    def arrivals(relative, top):
        arrived = []
        bit = 1
        while bit <= top:
            arrived.append(swap(rows_next(relative | bit, 0, chunks, arrivals(relative | bit, bit // 2)), bit))
            bit *= 2
        return arrived

    top = grid_rows // 2
    far = arrivals(top, top // 2)
    near, crossed = [], []
    for chunk in range(chunks):
        if top == 2:
            near.append([(swap(rows_next(1, chunk, 1, []), 1), 0)])
        elif chunk == 0:
            arrived = arrivals(0, top // 2)
            near += [[(array, place) for array in arrived] for place in range(chunks)]
        crossed.append(swap(rows_next(top, chunk, 1, far), top))
    kept = rows_next(0, 0, chunks, [])
    parts = [[(kept, chunk), *near[chunk], (crossed[chunk], 0)] for chunk in range(chunks)]

    image = None
    for chunk in range(chunks):

        def finish(*refs, chunk=chunk):
            finish_kernel(chunk, planes_padded, len(parts[chunk]), refs)

        earlier = [] if image is None else [image]
        image = pl.pallas_call(
            finish,
            grid=(1,),
            out_shape=jax.ShapeDtypeStruct((2, planes, per_device, NX // 2), F32),
            in_specs=[
                pl.BlockSpec((slots,) + part_shape, lambda step, place=place: (place, 0, 0, 0))
                for _, place in parts[chunk]
            ]
            + [
                pl.BlockSpec((4 * LANES, NX // 2), lambda step: (0, 0)),
                pl.BlockSpec((1, NX // 2), lambda step: (0, 0)),
                pl.BlockSpec((1, per_device), lambda step: (0, 0)),
                pl.BlockSpec(memory_space=pltpu.SMEM),
            ]
            + [pl.BlockSpec(memory_space=pl.ANY)] * len(earlier),
            out_specs=pl.BlockSpec((2, planes, CHUNK, NX // 2), lambda step, chunk=chunk: (0, 0, chunk, 0)),
            input_output_aliases={len(parts[chunk]) + 4: 0} if earlier else {},
            compiler_params=params,
            name="finish",
        )(
            *in_hbm([array for array, _ in parts[chunk]]),
            jnp.asarray(order_tables()),
            deapod_first[None, :],
            deapod_second[None, :],
            deapod_third,
            *earlier,
        )
    return image


def solution(mesh):
    in_specs = (
        P(("gx", "gy"), None, None),
        P(("gx", "gy"), None, None, None),
        P(("gx", "gy"), None, None),
        P(("gx", "gy"), None),
        P(("gx", "gy")),
        P(),
        P("gx"),
        P("gy"),
    )
    out_specs = P(None, "gy", "gx", None)
    return jax.shard_map(
        on_device, mesh=mesh, in_specs=in_specs, out_specs=out_specs, check_vma=False
    )
```

```python
import functools
import math

import jax
import jax.numpy as jnp
import ml_dtypes
import numpy as np
from jax import lax
from jax.experimental import pallas as pl
from jax.experimental.pallas import tpu as pltpu
from jax.sharding import PartitionSpec as P

NX = 384
NY = 384
NZ = 384
TILE = 8
LANES = 128
PLANES = 32
CHUNK = 24
Z_CHIPS = 4
PARTS = 4
CELLS = TILE // PARTS
STRIDE = NY + TILE
PHASES = 128
BF16 = jnp.bfloat16
F32 = jnp.float32
VMEM_LIMIT = 8 * 1024 * 1024


def halves(array):
    high = array.astype(ml_dtypes.bfloat16)
    low = (array - high.astype(np.float64)).astype(ml_dtypes.bfloat16)
    return high, low


def split(value):
    high = value.astype(BF16)
    return high, (value - high.astype(F32)).astype(BF16)


def waves(freq, position, length):
    steps = np.mod(freq[:, None] * position[None, :], length)
    phase = 2.0 * math.pi * steps / length
    return np.cos(phase), np.sin(phase)


def depth_tables(planes):
    matrices, phases = [], []
    lane_part = np.arange(LANES) // 64
    lane_odd = np.arange(LANES) // 32 % 2
    lane_plane = np.arange(LANES) % 32
    used = (lane_plane < planes).astype(np.float64)
    for index in range(NZ // 2 // planes):
        position = index * planes + lane_plane - NZ // 4
        cos, sin = waves(np.arange(TILE) - NZ // 2, position, NZ)
        cos, sin = cos * used / math.sqrt(NZ), sin * used / math.sqrt(NZ)
        real = np.where(lane_part == 0, cos, sin)
        imag = np.where(lane_part == 0, -sin, cos)
        high, low = halves(np.concatenate((real, imag)))
        matrices.append(np.concatenate((high, high, low)))
        cos, sin = waves(np.arange(NZ // TILE), position, NZ // TILE)
        sign = np.where(lane_odd == 1, -1.0, 1.0)[None, :]
        sin = sin * np.where(lane_part == 0, -1.0, 1.0)[None, :]
        phases.append(np.stack((np.concatenate((cos, cos * sign)), np.concatenate((sin, sin * sign)))))
    return np.stack(matrices), np.stack(phases).astype(np.float32)


def column_tables():
    third = NY // 3
    out = []
    for residue in range(3):
        cos, sin = waves(3 * np.arange(NY // 6) + residue - NY // 4, np.arange(third) - NY // 2, NY)
        high, low = halves(np.concatenate((cos, sin)) / math.sqrt(NY))
        out.append(np.block([[high, high], [low, np.zeros_like(low)]]))
    return np.stack(out)


def row_tables():
    half = NX // 2
    freq = np.arange(half).reshape(-1, PARTS, CELLS).transpose(1, 0, 2).reshape(-1) - half
    quarter = NX // 4
    out = []
    for parity in range(2):
        position = 2 * np.arange(quarter) + parity - NX // 4
        cos, sin = waves(freq, position, NX)
        table = np.zeros((half, 2 * LANES))
        lanes = (np.arange(quarter) + parity * quarter) % LANES
        table[:, lanes] = cos / math.sqrt(NX)
        table[:, LANES + lanes] = sin / math.sqrt(NX)
        out.append(np.stack(halves(table)))
    return np.stack(out)


def order_tables():
    first = np.zeros((LANES, NX // 2))
    second = np.zeros((LANES, NX // 2))
    quarter = NX // 4
    for m1 in range(NX // 2):
        place = m1 // 2 + m1 % 2 * quarter
        if place < LANES:
            first[place, m1] = 1.0
        else:
            second[place - LANES, m1] = 1.0
    return np.concatenate((first, first, second, second)).astype(ml_dtypes.bfloat16)


def divide(value, divisor, limit):
    for shift in range(8, 24):
        factor = (1 << shift) // divisor + 1
        tried = np.arange(limit, dtype=np.int64)
        if factor * limit < 1 << 31 and np.array_equal(tried * factor >> shift, tried // divisor):
            return lax.shift_right_logical(value * factor, shift)
    raise ValueError(divisor)


def spread_kernel(tile_rows, tile_cols, grid_cols, devices, samples_ref, kernel_ref, offsets_ref, owners_ref, ids_ref, out_ref):
    owner, tile_id = owners_ref[...], ids_ref[...]
    tile_depth = NZ // TILE
    tiles_device = tile_rows * tile_cols * tile_depth
    owner_row = divide(owner, grid_cols, devices)
    tile_row = divide(tile_id, tile_cols * tile_depth, tiles_device)
    tile_col = divide(tile_id, tile_depth, tiles_device)
    row = owner_row * tile_rows + tile_row
    col = (owner - owner_row * grid_cols) * tile_cols + tile_col - tile_row * tile_cols
    folds = NX // TILE // 2
    upper = (row >= folds).astype(jnp.int32)
    base = (row - upper * folds) * (CELLS * STRIDE // TILE) + col
    phase = tile_id - tile_col * tile_depth + upper * tile_depth
    codes = (base * PHASES + phase).astype(F32)

    blocks = samples_ref.shape[0]
    taps = kernel_ref.shape[2]
    cell = lax.broadcasted_iota(jnp.int32, (TILE, LANES), 0)
    left = lax.broadcasted_iota(jnp.int32, (2 * TILE, LANES), 1) < LANES // 2

    def weights(block):
        placed = []
        for dim in range(3):
            shifted = cell - offsets_ref[dim, pl.ds(block, 1), :]
            value = jnp.zeros((TILE, LANES), F32)
            for tap in range(taps):
                value = jnp.where(shifted == tap, kernel_ref[block, dim, pl.ds(tap, 1), :], value)
            placed.append(value)
        plane = jnp.concatenate([placed[0][i : i + 1] * placed[1] for i in range(TILE)], axis=0)
        depth = jnp.concatenate([samples_ref[block, pl.ds(c, 1), :] * placed[2] for c in range(2)], axis=0)
        return depth, plane

    def pair_body(pair, carry):
        depth_a, plane_a = weights(2 * pair)
        depth_b, plane_b = weights(2 * pair + 1)
        depth_high, depth_low = split(jnp.concatenate((depth_a, depth_b), axis=0))
        plane_high, plane_low = split(jnp.concatenate((plane_a, plane_b), axis=0))
        piece = lax.dot_general(
            jnp.concatenate((depth_high, depth_low, depth_high), axis=1),
            jnp.concatenate((plane_high, plane_high, plane_low), axis=1),
            (((1,), (1,)), ((), ())),
            preferred_element_type=F32,
        )
        out_ref[pair] = jnp.where(left, piece[: 2 * TILE], piece[2 * TILE :])
        return carry

    lax.fori_loop(0, blocks // 2, pair_body, 0, unroll=8)
    out_ref[blocks // 2] = jnp.broadcast_to(codes, (2 * TILE, LANES))


def tiles_kernel(conditions, first, *refs):
    arrays = len(conditions)
    places_ref = refs[0]
    source_refs = refs[1 : 1 + arrays]
    depth_tables_ref, phase_tables_ref = refs[1 + arrays : 3 + arrays]
    acc_refs = refs[-7 - PARTS : -7]
    token_ref, codes_ref, depth_ref, phases_ref, even_ref, odd_ref, arrived = refs[-7:]
    token_ref[...] = jnp.zeros_like(token_ref)
    stride = STRIDE
    pairs = source_refs[0].shape[0] - 1
    batch = 8
    batches = pairs // batch
    assert batches % 2 == 0

    def copies(index):
        return pltpu.make_async_copy(
            source_refs[index].at[pairs, pl.ds(0, TILE)], codes_ref.at[index], arrived.at[index]
        )

    tables = [
        pltpu.make_async_copy(depth_tables_ref.at[places_ref[2]], depth_ref, arrived.at[arrays]),
        pltpu.make_async_copy(phase_tables_ref.at[places_ref[2]], phases_ref, arrived.at[arrays + 1]),
    ]
    for index in range(arrays):
        copies(index).start()
    for table in tables:
        table.start()

    if first:

        def clear(step, carry):
            at = pl.ds(pl.multiple_of(step * stride, stride), stride)
            for ref in acc_refs:
                ref[at, :] = jnp.zeros((stride, LANES), F32)
            return carry

        lax.fori_loop(0, NX // 2 // PARTS, clear, 0)

    for index in range(arrays):
        copies(index).wait()
    for table in tables:
        table.wait()

    def add_source(index):
        tiles_ref = source_refs[index]

        def spectrum(number, to_ref):
            tiles = jnp.concatenate([tiles_ref[number * batch + place] for place in range(batch)], axis=1)
            high, low = split(tiles)
            to_ref[...] = lax.dot_general(
                jnp.concatenate((high, low, high), axis=0),
                depth_ref[...],
                (((0,), (0,)), ((), ())),
                preferred_element_type=F32,
            )

        def accumulate(number, from_ref):
            for tile in range(2 * batch):
                code = codes_ref[index, 0, number * 2 * batch + tile].astype(jnp.int32)
                base = lax.shift_right_logical(code, 7)
                phase = jnp.bitwise_and(code, PHASES - 1)
                cos = phases_ref[0, pl.ds(phase, 1), :]
                sin = phases_ref[1, pl.ds(phase, 1), :]
                for i in range(TILE):
                    row = tile * TILE * TILE + i * TILE
                    value = from_ref[row : row + TILE, :]
                    value = value * cos + pltpu.roll(value, LANES // 2, 1) * sin
                    acc_ref = acc_refs[i // CELLS]
                    at = pl.ds(pl.multiple_of(base * TILE + i % CELLS * stride, TILE), TILE)
                    acc_ref[at, :] = acc_ref[at, :] + value

        spectrum(0, even_ref)

        def add_pair(step, carry):
            number = 2 * step
            spectrum(number + 1, odd_ref)
            accumulate(number, even_ref)
            spectrum(jnp.minimum(number + 2, batches - 2), even_ref)
            accumulate(number + 1, odd_ref)
            return carry

        lax.fori_loop(0, batches // 2, add_pair, 0, unroll=2)

    for index, condition in enumerate(conditions):
        if condition is None:
            add_source(index)
        else:
            holds = places_ref[0] == condition[0]
            for depth in condition[1:]:
                holds = jnp.logical_or(holds, places_ref[0] == depth)
            pl.when(holds)(functools.partial(add_source, index))


def columns_kernel(*refs):
    column_ref = refs[PARTS]
    acc_refs = refs[PARTS + 1 :]
    third = NY // 3
    rows = column_ref.shape[1] // 4
    turn = jnp.where(lax.broadcasted_iota(jnp.int32, (1, LANES), 1) < LANES // 2, -1.0, 1.0)

    def columns(step, carry):
        start = pl.multiple_of(step * STRIDE, TILE)
        for pair in range(0, PARTS, 2):
            folded = ([], [], [])
            for ref in acc_refs[pair : pair + 2]:
                first, second, last = (ref[pl.ds(start + third * part, third), :] for part in range(3))
                both = second + last
                across = pltpu.roll(second - last, LANES // 2, 1) * (turn * math.sqrt(0.75))
                middle = first - 0.5 * both
                folded[0].append(first + both)
                folded[1].append(middle + across)
                folded[2].append(middle - across)
            for residue in range(3):
                high, low = split(jnp.concatenate(folded[residue], axis=1))
                product = jnp.dot(
                    column_ref[residue], jnp.concatenate((high, low), axis=0), preferred_element_type=F32
                )
                product = product[: 2 * rows] + product[2 * rows :]
                for side, ref in enumerate(acc_refs[pair : pair + 2]):
                    lanes = slice(side * LANES, (side + 1) * LANES)
                    ref[pl.ds(start + residue * rows, rows), :] = (
                        product[:rows, lanes] + pltpu.roll(product[rows:, lanes], LANES // 2, 1) * turn
                    )
        return carry

    lax.fori_loop(0, NX // 2 // PARTS, columns, 0, unroll=8)


def rows_kernel(relative, first, count, chunks, grid_rows, addends, planes_padded, places_ref, *refs):
    acc_refs, row_ref, addend_refs, out_ref = refs[:PARTS], refs[PARTS], refs[PARTS + 1 : -1], refs[-1]
    assert len(addend_refs) == addends
    rows = grid_rows * chunks * TILE
    device = jnp.bitwise_xor(places_ref[1], relative)
    lane = lax.broadcasted_iota(jnp.int32, (PLANES, LANES), 1)

    def block(step, carry):
        chunk, residue = step // 3, step % 3
        start = residue * rows + (device * chunks + first + chunk) * TILE
        turned = []
        for row in range(TILE):
            at = pl.ds(start + row, NX // 2 // PARTS, stride=STRIDE)
            turned.append(jnp.concatenate([ref[at, :] for ref in acc_refs], axis=0).T)
        parts = []
        for odd in range(2):
            at = odd * PLANES
            stacked = [value[part * 64 + at : part * 64 + at + PLANES] for value in turned for part in range(2)]
            high, low = split(jnp.concatenate(stacked, axis=0))
            size = high.shape[0]
            both = jnp.dot(jnp.concatenate((high, low), axis=0), row_ref[odd, 0], preferred_element_type=F32)
            product = both[:size] + both[size:] + jnp.dot(high, row_ref[odd, 1], preferred_element_type=F32)
            sides = []
            for row in range(TILE):
                real = product[2 * row * PLANES : (2 * row + 1) * PLANES]
                imag = product[(2 * row + 1) * PLANES : (2 * row + 2) * PLANES]
                sides.append((real[:, :LANES] - imag[:, LANES:], real[:, LANES:] + imag[:, :LANES]))
            parts.append(sides)
        for slot in range(TILE // 2):
            place = chunk * (CHUNK // 2) + 3 * slot + residue
            for part in range(2):
                even = [parts[0][slot + side * TILE // 2][part] for side in range(2)]
                odd = [parts[1][slot + side * TILE // 2][part] for side in range(2)]
                values = [jnp.where(lane < NX // 4, even[side], odd[side]) for side in range(2)]
                values.append(jnp.where(lane < LANES // 2, odd[0], pltpu.roll(odd[1], LANES // 2, 1)))
                for number, value in enumerate(values):
                    planes = pl.ds(part * planes_padded, planes_padded)
                    total = value[:planes_padded]
                    for ref in addend_refs:
                        shift = first * (CHUNK // 2) if ref.shape[0] > out_ref.shape[0] else 0
                        total = total + ref[shift + place, number, planes]
                    out_ref[place, number, planes] = total
        return carry

    lax.fori_loop(0, 3 * count, block, 0, unroll=3)


def finish_kernel(chunk, planes_padded, parts, refs):
    part_refs = refs[:parts]
    order_ref, first_ref, second_ref, third_ref = refs[parts : parts + 4]
    out_ref = refs[-1]
    planes = out_ref.shape[1]
    slots = part_refs[0].shape[0]
    stride = 6 * planes_padded
    flats = [ref.reshape(slots * stride, LANES) for ref in part_refs]
    order = order_ref[...]
    shape = (CHUNK, second_ref.shape[1])
    here = lax.broadcasted_iota(jnp.int32, shape, 1) == lax.broadcasted_iota(jnp.int32, shape, 0) + chunk * CHUNK
    second = jnp.sum(jnp.where(here, second_ref[...], 0.0), axis=1, keepdims=True)
    scale = second * first_ref[...]
    for part in range(2):
        for group in range(0, planes, TILE):
            members = range(group, min(group + TILE, planes))
            mains, rests = [], []
            for plane in members:
                values = []
                for number in range(3):
                    at = pl.ds((number * 2 + part) * planes_padded + plane, slots, stride=stride)
                    total = flats[0][at, :]
                    for flat in flats[1:]:
                        total = total + flat[at, :]
                    values.append(total)
                mains.append(jnp.concatenate(values[:2], axis=0))
                rests.append(jnp.concatenate((values[2], pltpu.roll(values[2], LANES // 2, 1)), axis=0))
            main = split(jnp.concatenate(mains, axis=0))
            rest = split(jnp.concatenate(rests, axis=0))
            ordered = jnp.dot(jnp.concatenate(main + rest, axis=1), order, preferred_element_type=F32)
            for index, plane in enumerate(members):
                out_ref[part, plane] = ordered[index * 2 * slots : (index + 1) * 2 * slots] * (scale * third_ref[plane])


def on_device(samples, kernel, offsets, owners, tile_ids, deapod_first, deapod_second, deapod_third):
    grid_rows = lax.axis_size("gx")
    grid_cols = lax.axis_size("gy")
    blocks = samples.shape[0]
    block_width = samples.shape[2]
    assert block_width == LANES and blocks == LANES
    tile_rows = NX // (TILE * grid_rows)
    tile_cols = NY // (TILE * grid_cols)
    planes = deapod_third.shape[0]
    per_device = deapod_second.shape[0]
    assert per_device % CHUNK == 0
    chunks = per_device // CHUNK
    slots = CHUNK // 2
    planes_padded = -(-planes // 8) * 8
    vmem = pl.BlockSpec(memory_space=pltpu.VMEM)
    params = pltpu.CompilerParams(vmem_limit_bytes=VMEM_LIMIT)

    def in_hbm(arrays):
        return [pltpu.with_memory_space_constraint(array, pltpu.HBM) for array in arrays]

    tiles = pl.pallas_call(
        functools.partial(spread_kernel, tile_rows, tile_cols, grid_cols, grid_rows * grid_cols),
        out_shape=pltpu.HBM((blocks // 2 + 1, 2 * TILE, LANES), F32),
        in_specs=[vmem] * 5,
        out_specs=vmem,
        compiler_params=params,
        name="spread",
    )(*in_hbm([samples, kernel, offsets.transpose(1, 0, 2), owners.reshape(1, blocks), tile_ids.reshape(1, blocks)]))

    along = grid_cols // Z_CHIPS
    deep_at = lax.div(lax.axis_index("gy").astype(jnp.int32), jnp.int32(along))

    def send(value, moves_z, wide):
        moves = [(a * along + y, b * along + (y + wide) % along) for a, b in moves_z for y in range(along)]
        return lax.ppermute(value, "gy", moves)

    places = jnp.stack((deep_at, lax.axis_index("gx").astype(jnp.int32), lax.axis_index("gy").astype(jnp.int32)))
    matrices, phases = (jnp.asarray(table) for table in depth_tables(planes))
    column = jnp.asarray(column_tables())
    half = NX // 2
    smem = pl.BlockSpec(memory_space=pltpu.SMEM)
    acc_shape = (half // PARTS * STRIDE, LANES)

    def in_vmem(arrays):
        return [pltpu.with_memory_space_constraint(array, pltpu.VMEM) for array in arrays]

    def add_tiles(sources, acc):
        conditions = [None if len(holders) == Z_CHIPS else tuple(holders) for holders, _ in sources]
        spectra = pltpu.VMEM((16 * TILE * TILE, LANES), F32)
        kept = [jax.ShapeDtypeStruct(acc_shape, F32) if acc else pltpu.VMEM(acc_shape, F32)] * PARTS
        inputs = len(sources) + 3
        *acc, token = pl.pallas_call(
            functools.partial(tiles_kernel, conditions, not acc),
            out_shape=kept + [jax.ShapeDtypeStruct((TILE, LANES), F32)],
            in_specs=[smem] + [vmem] * len(sources) + [pl.BlockSpec(memory_space=pl.ANY)] * 2 + [vmem] * len(acc),
            out_specs=[vmem] * (PARTS + 1),
            input_output_aliases={inputs + part: part for part in range(PARTS)} if acc else {},
            scratch_shapes=[
                pltpu.SMEM((len(sources), TILE, LANES), F32),
                pltpu.VMEM(matrices.shape[1:], BF16),
                pltpu.VMEM(phases.shape[1:], F32),
                spectra,
                spectra,
                pltpu.SemaphoreType.DMA((len(sources) + 2,)),
            ],
            compiler_params=params,
            cost_estimate=pl.CostEstimate(flops=0, bytes_accessed=len(sources) << 23, transcendentals=0),
            name="tiles",
        )(places, *[array for _, array in sources], *in_hbm([matrices, phases]), *in_vmem(acc))
        return acc, token

    def after(value, token):
        return lax.optimization_barrier((value, token))[0]

    def across(value, holders):
        return [(holders, send(value, [(z, z) for z in holders], wide)) for wide in range(1, along)]

    every = range(Z_CHIPS)
    passed = {1: tiles, -1: tiles}
    arrived, token, acc = [(every, tiles)], None, []
    for steps in range(1, Z_CHIPS + 1):
        partners = []
        if steps == 1:
            partners += across(tiles, every)
        else:
            partners += [held for holders, array in arrived[:2] for held in across(after(array, token), holders)]
        moved = []
        if steps < Z_CHIPS:
            for way in (1, -1):
                moves = [(z, z + way) for z in every if 0 <= z + way < Z_CHIPS and 0 <= z - way * (steps - 1) < Z_CHIPS]
                value = passed[way] if token is None else after(passed[way], token)
                passed[way] = send(value, moves, 0)
                moved.append(([to for _, to in moves], passed[way]))
        acc, token = add_tiles(arrived, acc)
        arrived = moved + partners
    acc, _ = add_tiles(arrived, acc)

    acc = pl.pallas_call(
        columns_kernel,
        out_shape=[jax.ShapeDtypeStruct(acc_shape, F32)] * PARTS,
        in_specs=[vmem] * (PARTS + 1),
        out_specs=[vmem] * PARTS,
        input_output_aliases={part: part for part in range(PARTS)},
        compiler_params=params,
        name="columns",
    )(*in_vmem(acc), *in_hbm([column]))

    row_table = jnp.asarray(row_tables())
    part_shape = (3, 2 * planes_padded, LANES)

    def rows_for(relative, first, count, addends, after):
        def body(*refs):
            operands = 2 + PARTS + len(addends)
            rows_kernel(
                relative, first, count, chunks, grid_rows, len(addends), planes_padded, *refs[:operands], refs[-1]
            )

        return pl.pallas_call(
            body,
            in_specs=[smem] + [vmem] * (1 + PARTS + len(addends)) + [pl.BlockSpec(memory_space=pl.ANY)] * len(after),
            out_specs=vmem,
            out_shape=pltpu.HBM((count * slots,) + part_shape, F32),
            compiler_params=params,
            cost_estimate=pl.CostEstimate(flops=1, bytes_accessed=1, transcendentals=0),
            name="rows",
        )(places, *in_vmem(acc), *in_hbm([row_table]), *addends, *in_hbm(after))

    def swap(value, bit):
        return lax.ppermute(value, "gx", [(index, index ^ bit) for index in range(grid_rows)])

    last = []

    def rows_next(relative, first, count, addends):
        part = rows_for(relative, first, count, addends, last)
        last[:] = [part]
        return part

    def arrivals(relative, top):
        arrived = []
        bit = 1
        while bit <= top:
            arrived.append(swap(rows_next(relative | bit, 0, chunks, arrivals(relative | bit, bit // 2)), bit))
            bit *= 2
        return arrived

    top = grid_rows // 2
    far = arrivals(top, top // 2)
    near, crossed = [], []
    for chunk in range(chunks):
        if top == 2:
            near.append([(swap(rows_next(1, chunk, 1, []), 1), 0)])
        elif chunk == 0:
            arrived = arrivals(0, top // 2)
            near += [[(array, place) for array in arrived] for place in range(chunks)]
        crossed.append(swap(rows_next(top, chunk, 1, far), top))
    kept = rows_next(0, 0, chunks, [])
    parts = [[(kept, chunk), *near[chunk], (crossed[chunk], 0)] for chunk in range(chunks)]

    image = None
    for chunk in range(chunks):

        def finish(*refs, chunk=chunk):
            finish_kernel(chunk, planes_padded, len(parts[chunk]), refs)

        earlier = [] if image is None else [image]
        image = pl.pallas_call(
            finish,
            grid=(1,),
            out_shape=jax.ShapeDtypeStruct((2, planes, per_device, NX // 2), F32),
            in_specs=[
                pl.BlockSpec((slots,) + part_shape, lambda step, place=place: (place, 0, 0, 0))
                for _, place in parts[chunk]
            ]
            + [
                pl.BlockSpec((4 * LANES, NX // 2), lambda step: (0, 0)),
                pl.BlockSpec((1, NX // 2), lambda step: (0, 0)),
                pl.BlockSpec((1, per_device), lambda step: (0, 0)),
                pl.BlockSpec(memory_space=pltpu.SMEM),
            ]
            + [pl.BlockSpec(memory_space=pl.ANY)] * len(earlier),
            out_specs=pl.BlockSpec((2, planes, CHUNK, NX // 2), lambda step, chunk=chunk: (0, 0, chunk, 0)),
            input_output_aliases={len(parts[chunk]) + 4: 0} if earlier else {},
            compiler_params=params,
            name="finish",
        )(
            *[array for array, _ in parts[chunk]],
            jnp.asarray(order_tables()),
            deapod_first[None, :],
            deapod_second[None, :],
            deapod_third,
            *earlier,
        )
    return image


def solution(mesh):
    in_specs = (
        P(("gx", "gy"), None, None),
        P(("gx", "gy"), None, None, None),
        P(("gx", "gy"), None, None),
        P(("gx", "gy"), None),
        P(("gx", "gy")),
        P(),
        P("gx"),
        P("gy"),
    )
    out_specs = P(None, "gy", "gx", None)
    return jax.shard_map(
        on_device, mesh=mesh, in_specs=in_specs, out_specs=out_specs, check_vma=False
    )
```

```python
import functools
import math

import jax
import jax.numpy as jnp
import ml_dtypes
import numpy as np
from jax import lax
from jax.experimental import pallas as pl
from jax.experimental.pallas import tpu as pltpu
from jax.sharding import PartitionSpec as P

NX = 384
NY = 384
NZ = 384
TILE = 8
LANES = 128
PLANES = 32
CHUNK = 24
Z_CHIPS = 4
PARTS = 4
CELLS = TILE // PARTS
STRIDE = NY + TILE
PHASES = 128
BF16 = jnp.bfloat16
F32 = jnp.float32
VMEM_LIMIT = 8 * 1024 * 1024


def halves(array):
    high = array.astype(ml_dtypes.bfloat16)
    low = (array - high.astype(np.float64)).astype(ml_dtypes.bfloat16)
    return high, low


def split(value):
    high = value.astype(BF16)
    return high, (value - high.astype(F32)).astype(BF16)


def waves(freq, position, length):
    steps = np.mod(freq[:, None] * position[None, :], length)
    phase = 2.0 * math.pi * steps / length
    return np.cos(phase), np.sin(phase)


def depth_tables(planes):
    matrices, phases = [], []
    lane_part = np.arange(LANES) // 64
    lane_odd = np.arange(LANES) // 32 % 2
    lane_plane = np.arange(LANES) % 32
    used = (lane_plane < planes).astype(np.float64)
    for index in range(NZ // 2 // planes):
        position = index * planes + lane_plane - NZ // 4
        cos, sin = waves(np.arange(TILE) - NZ // 2, position, NZ)
        cos, sin = cos * used / math.sqrt(NZ), sin * used / math.sqrt(NZ)
        real = np.where(lane_part == 0, cos, sin)
        imag = np.where(lane_part == 0, -sin, cos)
        high, low = halves(np.concatenate((real, imag)))
        matrices.append(np.concatenate((high, high, low)))
        cos, sin = waves(np.arange(NZ // TILE), position, NZ // TILE)
        sign = np.where(lane_odd == 1, -1.0, 1.0)[None, :]
        sin = sin * np.where(lane_part == 0, -1.0, 1.0)[None, :]
        phases.append(np.stack((np.concatenate((cos, cos * sign)), np.concatenate((sin, sin * sign)))))
    return np.stack(matrices), np.stack(phases).astype(np.float32)


def column_tables():
    third = NY // 3
    out = []
    for residue in range(3):
        cos, sin = waves(3 * np.arange(NY // 6) + residue - NY // 4, np.arange(third) - NY // 2, NY)
        high, low = halves(np.concatenate((cos, sin)) / math.sqrt(NY))
        out.append(np.block([[high, high], [low, np.zeros_like(low)]]))
    return np.stack(out)


def row_tables():
    half = NX // 2
    freq = np.arange(half).reshape(-1, PARTS, CELLS).transpose(1, 0, 2).reshape(-1) - half
    quarter = NX // 4
    out = []
    for parity in range(2):
        position = 2 * np.arange(quarter) + parity - NX // 4
        cos, sin = waves(freq, position, NX)
        table = np.zeros((half, 2 * LANES))
        lanes = (np.arange(quarter) + parity * quarter) % LANES
        table[:, lanes] = cos / math.sqrt(NX)
        table[:, LANES + lanes] = sin / math.sqrt(NX)
        out.append(np.stack(halves(table)))
    return np.stack(out)


def order_tables():
    first = np.zeros((LANES, NX // 2))
    second = np.zeros((LANES, NX // 2))
    quarter = NX // 4
    for m1 in range(NX // 2):
        place = m1 // 2 + m1 % 2 * quarter
        if place < LANES:
            first[place, m1] = 1.0
        else:
            second[place - LANES, m1] = 1.0
    return np.concatenate((first, first, second, second)).astype(ml_dtypes.bfloat16)


def divide(value, divisor, limit):
    for shift in range(8, 24):
        factor = (1 << shift) // divisor + 1
        tried = np.arange(limit, dtype=np.int64)
        if factor * limit < 1 << 31 and np.array_equal(tried * factor >> shift, tried // divisor):
            return lax.shift_right_logical(value * factor, shift)
    raise ValueError(divisor)


def spread_kernel(tile_rows, tile_cols, grid_cols, devices, samples_ref, kernel_ref, offsets_ref, owners_ref, ids_ref, out_ref):
    owner, tile_id = owners_ref[...], ids_ref[...]
    tile_depth = NZ // TILE
    tiles_device = tile_rows * tile_cols * tile_depth
    owner_row = divide(owner, grid_cols, devices)
    tile_row = divide(tile_id, tile_cols * tile_depth, tiles_device)
    tile_col = divide(tile_id, tile_depth, tiles_device)
    row = owner_row * tile_rows + tile_row
    col = (owner - owner_row * grid_cols) * tile_cols + tile_col - tile_row * tile_cols
    folds = NX // TILE // 2
    upper = (row >= folds).astype(jnp.int32)
    base = (row - upper * folds) * (CELLS * STRIDE // TILE) + col
    phase = tile_id - tile_col * tile_depth + upper * tile_depth
    codes = (base * PHASES + phase).astype(F32)

    blocks = samples_ref.shape[0]
    taps = kernel_ref.shape[2]
    cell = lax.broadcasted_iota(jnp.int32, (TILE, LANES), 0)
    left = lax.broadcasted_iota(jnp.int32, (2 * TILE, LANES), 1) < LANES // 2

    def weights(block):
        placed = []
        for dim in range(3):
            shifted = cell - offsets_ref[dim, pl.ds(block, 1), :]
            value = jnp.zeros((TILE, LANES), F32)
            for tap in range(taps):
                value = jnp.where(shifted == tap, kernel_ref[block, dim, pl.ds(tap, 1), :], value)
            placed.append(value)
        plane = jnp.concatenate([placed[0][i : i + 1] * placed[1] for i in range(TILE)], axis=0)
        depth = jnp.concatenate([samples_ref[block, pl.ds(c, 1), :] * placed[2] for c in range(2)], axis=0)
        return depth, plane

    def pair_body(pair, carry):
        depth_a, plane_a = weights(2 * pair)
        depth_b, plane_b = weights(2 * pair + 1)
        depth_high, depth_low = split(jnp.concatenate((depth_a, depth_b), axis=0))
        plane_high, plane_low = split(jnp.concatenate((plane_a, plane_b), axis=0))
        piece = lax.dot_general(
            jnp.concatenate((depth_high, depth_low, depth_high), axis=1),
            jnp.concatenate((plane_high, plane_high, plane_low), axis=1),
            (((1,), (1,)), ((), ())),
            preferred_element_type=F32,
        )
        out_ref[pair] = jnp.where(left, piece[: 2 * TILE], piece[2 * TILE :])
        return carry

    lax.fori_loop(0, blocks // 2, pair_body, 0, unroll=8)
    out_ref[blocks // 2] = jnp.broadcast_to(codes, (2 * TILE, LANES))


def tiles_kernel(conditions, first, last, *refs):
    arrays = len(conditions)
    places_ref = refs[0]
    source_refs = refs[1 : 1 + arrays]
    depth_tables_ref, phase_tables_ref = refs[1 + arrays : 3 + arrays]
    acc_refs = refs[-7 - PARTS : -7]
    token_ref, codes_ref, depth_ref, phases_ref, even_ref, odd_ref, arrived = refs[-7:]
    token_ref[...] = jnp.zeros_like(token_ref)
    stride = STRIDE
    pairs = source_refs[0].shape[0] - 1
    batch = 8
    batches = pairs // batch
    assert batches % 2 == 0

    def copies(index):
        return pltpu.make_async_copy(
            source_refs[index].at[pairs, pl.ds(0, TILE)], codes_ref.at[index], arrived.at[index]
        )

    tables = [
        pltpu.make_async_copy(depth_tables_ref.at[places_ref[2]], depth_ref, arrived.at[arrays]),
        pltpu.make_async_copy(phase_tables_ref.at[places_ref[2]], phases_ref, arrived.at[arrays + 1]),
    ]
    for index in range(arrays):
        copies(index).start()
    for table in tables:
        table.start()

    if first:

        def clear(step, carry):
            at = pl.ds(pl.multiple_of(step * stride, stride), stride)
            for ref in acc_refs:
                ref[at, :] = jnp.zeros((stride, LANES), F32)
            return carry

        lax.fori_loop(0, NX // 2 // PARTS, clear, 0)

    for index in range(arrays):
        copies(index).wait()
    for table in tables:
        table.wait()

    def add_source(index):
        tiles_ref = source_refs[index]

        def spectrum(number, to_ref):
            tiles = jnp.concatenate([tiles_ref[number * batch + place] for place in range(batch)], axis=1)
            high, low = split(tiles)
            to_ref[...] = lax.dot_general(
                jnp.concatenate((high, low, high), axis=0),
                depth_ref[...],
                (((0,), (0,)), ((), ())),
                preferred_element_type=F32,
            )

        def accumulate(number, from_ref):
            for tile in range(2 * batch):
                code = codes_ref[index, 0, number * 2 * batch + tile].astype(jnp.int32)
                base = lax.shift_right_logical(code, 7)
                phase = jnp.bitwise_and(code, PHASES - 1)
                cos = phases_ref[0, pl.ds(phase, 1), :]
                sin = phases_ref[1, pl.ds(phase, 1), :]
                for i in range(TILE):
                    row = tile * TILE * TILE + i * TILE
                    value = from_ref[row : row + TILE, :]
                    value = value * cos + pltpu.roll(value, LANES // 2, 1) * sin
                    acc_ref = acc_refs[i // CELLS]
                    at = pl.ds(pl.multiple_of(base * TILE + i % CELLS * stride, TILE), TILE)
                    acc_ref[at, :] = acc_ref[at, :] + value

        spectrum(0, even_ref)

        def add_pair(step, carry):
            number = 2 * step
            spectrum(number + 1, odd_ref)
            accumulate(number, even_ref)
            spectrum(jnp.minimum(number + 2, batches - 2), even_ref)
            accumulate(number + 1, odd_ref)
            return carry

        lax.fori_loop(0, batches // 2, add_pair, 0, unroll=2)

    for index, condition in enumerate(conditions):
        if condition is None:
            add_source(index)
        else:
            holds = places_ref[0] == condition[0]
            for depth in condition[1:]:
                holds = jnp.logical_or(holds, places_ref[0] == depth)
            pl.when(holds)(functools.partial(add_source, index))

    if last:
        transform_columns(refs[3 + arrays], acc_refs)


def transform_columns(column_ref, acc_refs):
    third = NY // 3
    rows = column_ref.shape[1] // 4
    turn = jnp.where(lax.broadcasted_iota(jnp.int32, (1, LANES), 1) < LANES // 2, -1.0, 1.0)

    def columns(step, carry):
        start = pl.multiple_of(step * STRIDE, TILE)
        for pair in range(0, PARTS, 2):
            folded = ([], [], [])
            for ref in acc_refs[pair : pair + 2]:
                first, second, last = (ref[pl.ds(start + third * part, third), :] for part in range(3))
                both = second + last
                across = pltpu.roll(second - last, LANES // 2, 1) * (turn * math.sqrt(0.75))
                middle = first - 0.5 * both
                folded[0].append(first + both)
                folded[1].append(middle + across)
                folded[2].append(middle - across)
            for residue in range(3):
                high, low = split(jnp.concatenate(folded[residue], axis=1))
                product = jnp.dot(
                    column_ref[residue], jnp.concatenate((high, low), axis=0), preferred_element_type=F32
                )
                product = product[: 2 * rows] + product[2 * rows :]
                for side, ref in enumerate(acc_refs[pair : pair + 2]):
                    lanes = slice(side * LANES, (side + 1) * LANES)
                    ref[pl.ds(start + residue * rows, rows), :] = (
                        product[:rows, lanes] + pltpu.roll(product[rows:, lanes], LANES // 2, 1) * turn
                    )
        return carry

    lax.fori_loop(0, NX // 2 // PARTS, columns, 0, unroll=16)


def rows_kernel(relative, first, count, chunks, grid_rows, addends, planes_padded, places_ref, *refs):
    acc_refs, row_ref, addend_refs, out_ref = refs[:PARTS], refs[PARTS], refs[PARTS + 1 : -1], refs[-1]
    assert len(addend_refs) == addends
    rows = grid_rows * chunks * TILE
    device = jnp.bitwise_xor(places_ref[1], relative)
    lane = lax.broadcasted_iota(jnp.int32, (PLANES, LANES), 1)

    def block(step, carry):
        chunk, residue = step // 3, step % 3
        start = residue * rows + (device * chunks + first + chunk) * TILE
        turned = []
        for row in range(TILE):
            at = pl.ds(start + row, NX // 2 // PARTS, stride=STRIDE)
            turned.append(jnp.concatenate([ref[at, :] for ref in acc_refs], axis=0).T)
        parts = []
        for odd in range(2):
            at = odd * PLANES
            stacked = [value[part * 64 + at : part * 64 + at + PLANES] for value in turned for part in range(2)]
            high, low = split(jnp.concatenate(stacked, axis=0))
            size = high.shape[0]
            both = jnp.dot(jnp.concatenate((high, low), axis=0), row_ref[odd, 0], preferred_element_type=F32)
            product = both[:size] + both[size:] + jnp.dot(high, row_ref[odd, 1], preferred_element_type=F32)
            sides = []
            for row in range(TILE):
                real = product[2 * row * PLANES : (2 * row + 1) * PLANES]
                imag = product[(2 * row + 1) * PLANES : (2 * row + 2) * PLANES]
                sides.append((real[:, :LANES] - imag[:, LANES:], real[:, LANES:] + imag[:, :LANES]))
            parts.append(sides)
        for slot in range(TILE // 2):
            place = chunk * (CHUNK // 2) + 3 * slot + residue
            for part in range(2):
                even = [parts[0][slot + side * TILE // 2][part] for side in range(2)]
                odd = [parts[1][slot + side * TILE // 2][part] for side in range(2)]
                values = [jnp.where(lane < NX // 4, even[side], odd[side]) for side in range(2)]
                values.append(jnp.where(lane < LANES // 2, odd[0], pltpu.roll(odd[1], LANES // 2, 1)))
                for number, value in enumerate(values):
                    planes = pl.ds(part * planes_padded, planes_padded)
                    total = value[:planes_padded]
                    for ref in addend_refs:
                        shift = first * (CHUNK // 2) if ref.shape[0] > out_ref.shape[0] else 0
                        total = total + ref[shift + place, number, planes]
                    out_ref[place, number, planes] = total
        return carry

    lax.fori_loop(0, 3 * count, block, 0, unroll=3)


def finish_kernel(chunk, planes_padded, parts, refs):
    part_refs = refs[:parts]
    order_ref, first_ref, second_ref, third_ref = refs[parts : parts + 4]
    out_ref = refs[-1]
    planes = out_ref.shape[1]
    slots = part_refs[0].shape[0]
    stride = 6 * planes_padded
    flats = [ref.reshape(slots * stride, LANES) for ref in part_refs]
    order = order_ref[...]
    shape = (CHUNK, second_ref.shape[1])
    here = lax.broadcasted_iota(jnp.int32, shape, 1) == lax.broadcasted_iota(jnp.int32, shape, 0) + chunk * CHUNK
    second = jnp.sum(jnp.where(here, second_ref[...], 0.0), axis=1, keepdims=True)
    scale = second * first_ref[...]
    for part in range(2):
        for group in range(0, planes, TILE):
            members = range(group, min(group + TILE, planes))
            mains, rests = [], []
            for plane in members:
                values = []
                for number in range(3):
                    at = pl.ds((number * 2 + part) * planes_padded + plane, slots, stride=stride)
                    total = flats[0][at, :]
                    for flat in flats[1:]:
                        total = total + flat[at, :]
                    values.append(total)
                mains.append(jnp.concatenate(values[:2], axis=0))
                rests.append(jnp.concatenate((values[2], pltpu.roll(values[2], LANES // 2, 1)), axis=0))
            main = split(jnp.concatenate(mains, axis=0))
            rest = split(jnp.concatenate(rests, axis=0))
            ordered = jnp.dot(jnp.concatenate(main + rest, axis=1), order, preferred_element_type=F32)
            for index, plane in enumerate(members):
                out_ref[part, plane] = ordered[index * 2 * slots : (index + 1) * 2 * slots] * (scale * third_ref[plane])


def on_device(samples, kernel, offsets, owners, tile_ids, deapod_first, deapod_second, deapod_third):
    grid_rows = lax.axis_size("gx")
    grid_cols = lax.axis_size("gy")
    blocks = samples.shape[0]
    block_width = samples.shape[2]
    assert block_width == LANES and blocks == LANES
    tile_rows = NX // (TILE * grid_rows)
    tile_cols = NY // (TILE * grid_cols)
    planes = deapod_third.shape[0]
    per_device = deapod_second.shape[0]
    assert per_device % CHUNK == 0
    chunks = per_device // CHUNK
    slots = CHUNK // 2
    planes_padded = -(-planes // 8) * 8
    vmem = pl.BlockSpec(memory_space=pltpu.VMEM)
    params = pltpu.CompilerParams(vmem_limit_bytes=VMEM_LIMIT)

    def in_hbm(arrays):
        return [pltpu.with_memory_space_constraint(array, pltpu.HBM) for array in arrays]

    tiles = pl.pallas_call(
        functools.partial(spread_kernel, tile_rows, tile_cols, grid_cols, grid_rows * grid_cols),
        out_shape=pltpu.HBM((blocks // 2 + 1, 2 * TILE, LANES), F32),
        in_specs=[vmem] * 5,
        out_specs=vmem,
        compiler_params=params,
        name="spread",
    )(*in_hbm([samples, kernel, offsets.transpose(1, 0, 2), owners.reshape(1, blocks), tile_ids.reshape(1, blocks)]))

    along = grid_cols // Z_CHIPS
    deep_at = lax.div(lax.axis_index("gy").astype(jnp.int32), jnp.int32(along))

    def send(value, moves_z, wide):
        moves = [(a * along + y, b * along + (y + wide) % along) for a, b in moves_z for y in range(along)]
        return lax.ppermute(value, "gy", moves)

    places = jnp.stack((deep_at, lax.axis_index("gx").astype(jnp.int32), lax.axis_index("gy").astype(jnp.int32)))
    matrices, phases = (jnp.asarray(table) for table in depth_tables(planes))
    column = jnp.asarray(column_tables())
    half = NX // 2
    smem = pl.BlockSpec(memory_space=pltpu.SMEM)
    acc_shape = (half // PARTS * STRIDE, LANES)

    def in_vmem(arrays):
        return [pltpu.with_memory_space_constraint(array, pltpu.VMEM) for array in arrays]

    def add_tiles(sources, acc, columns=()):
        conditions = [None if len(holders) == Z_CHIPS else tuple(holders) for holders, _ in sources]
        spectra = pltpu.VMEM((16 * TILE * TILE, LANES), F32)
        kept = [jax.ShapeDtypeStruct(acc_shape, F32) if acc else pltpu.VMEM(acc_shape, F32)] * PARTS
        inputs = len(sources) + 3 + len(columns)
        *acc, token = pl.pallas_call(
            functools.partial(tiles_kernel, conditions, not acc, bool(columns)),
            out_shape=kept + [jax.ShapeDtypeStruct((TILE, LANES), F32)],
            in_specs=[smem] + [vmem] * len(sources) + [pl.BlockSpec(memory_space=pl.ANY)] * 2 + [vmem] * (len(columns) + len(acc)),
            out_specs=[vmem] * (PARTS + 1),
            input_output_aliases={inputs + part: part for part in range(PARTS)} if acc else {},
            scratch_shapes=[
                pltpu.SMEM((len(sources), TILE, LANES), F32),
                pltpu.VMEM(matrices.shape[1:], BF16),
                pltpu.VMEM(phases.shape[1:], F32),
                spectra,
                spectra,
                pltpu.SemaphoreType.DMA((len(sources) + 2,)),
            ],
            compiler_params=params,
            cost_estimate=pl.CostEstimate(flops=0, bytes_accessed=len(sources) << 23, transcendentals=0),
            name="tiles",
        )(places, *[array for _, array in sources], *in_hbm([matrices, phases, *columns]), *in_vmem(acc))
        return acc, token

    def after(value, token):
        return lax.optimization_barrier((value, token))[0]

    def across(value, holders):
        return [(holders, send(value, [(z, z) for z in holders], wide)) for wide in range(1, along)]

    every = range(Z_CHIPS)
    passed = {1: tiles, -1: tiles}
    arrived, token, acc = [(every, tiles)], None, []
    for steps in range(1, Z_CHIPS + 1):
        partners = []
        if steps == 1:
            partners += across(tiles, every)
        else:
            partners += [held for holders, array in arrived[:2] for held in across(after(array, token), holders)]
        moved = []
        if steps < Z_CHIPS:
            for way in (1, -1):
                moves = [(z, z + way) for z in every if 0 <= z + way < Z_CHIPS and 0 <= z - way * (steps - 1) < Z_CHIPS]
                value = passed[way] if token is None else after(passed[way], token)
                passed[way] = send(value, moves, 0)
                moved.append(([to for _, to in moves], passed[way]))
        acc, token = add_tiles(arrived, acc)
        arrived = moved + partners
    acc, _ = add_tiles(arrived, acc, [column])

    row_table = jnp.asarray(row_tables())
    part_shape = (3, 2 * planes_padded, LANES)

    def rows_for(relative, first, count, addends, after):
        def body(*refs):
            operands = 2 + PARTS + len(addends)
            rows_kernel(
                relative, first, count, chunks, grid_rows, len(addends), planes_padded, *refs[:operands], refs[-1]
            )

        return pl.pallas_call(
            body,
            in_specs=[smem] + [vmem] * (1 + PARTS + len(addends)) + [pl.BlockSpec(memory_space=pl.ANY)] * len(after),
            out_specs=vmem,
            out_shape=jax.ShapeDtypeStruct((count * slots,) + part_shape, F32),
            compiler_params=params,
            cost_estimate=pl.CostEstimate(flops=1, bytes_accessed=1, transcendentals=0),
            name="rows",
        )(places, *in_vmem(acc), row_table, *addends, *in_hbm(after))

    def swap(value, bit):
        return lax.ppermute(value, "gx", [(index, index ^ bit) for index in range(grid_rows)])

    last = []

    def rows_next(relative, first, count, addends):
        part = rows_for(relative, first, count, addends, last)
        last[:] = [part]
        return part

    def arrivals(relative, top):
        arrived = []
        bit = 1
        while bit <= top:
            arrived.append(swap(rows_next(relative | bit, 0, chunks, arrivals(relative | bit, bit // 2)), bit))
            bit *= 2
        return arrived

    top = grid_rows // 2
    far = arrivals(top, top // 2)
    near, crossed = [], []
    for chunk in range(chunks):
        if top == 2:
            near.append([(swap(rows_next(1, chunk, 1, []), 1), 0)])
        elif chunk == 0:
            arrived = arrivals(0, top // 2)
            near += [[(array, place) for array in arrived] for place in range(chunks)]
        crossed.append(swap(rows_next(top, chunk, 1, far), top))
    kept = rows_next(0, 0, chunks, [])
    parts = [[(kept, chunk), *near[chunk], (crossed[chunk], 0)] for chunk in range(chunks)]

    image = None
    for chunk in range(chunks):

        def finish(*refs, chunk=chunk):
            finish_kernel(chunk, planes_padded, len(parts[chunk]), refs)

        earlier = [] if image is None else [image]
        image = pl.pallas_call(
            finish,
            grid=(1,),
            out_shape=jax.ShapeDtypeStruct((2, planes, per_device, NX // 2), F32),
            in_specs=[
                pl.BlockSpec((slots,) + part_shape, lambda step, place=place: (place, 0, 0, 0))
                for _, place in parts[chunk]
            ]
            + [
                pl.BlockSpec((4 * LANES, NX // 2), lambda step: (0, 0)),
                pl.BlockSpec((1, NX // 2), lambda step: (0, 0)),
                pl.BlockSpec((1, per_device), lambda step: (0, 0)),
                pl.BlockSpec(memory_space=pltpu.SMEM),
            ]
            + [pl.BlockSpec(memory_space=pl.ANY)] * len(earlier),
            out_specs=pl.BlockSpec((2, planes, CHUNK, NX // 2), lambda step, chunk=chunk: (0, 0, chunk, 0)),
            input_output_aliases={len(parts[chunk]) + 4: 0} if earlier else {},
            compiler_params=params,
            name="finish",
        )(
            *[array for array, _ in parts[chunk]],
            jnp.asarray(order_tables()),
            deapod_first[None, :],
            deapod_second[None, :],
            deapod_third,
            *earlier,
        )
    return image


def solution(mesh):
    in_specs = (
        P(("gx", "gy"), None, None),
        P(("gx", "gy"), None, None, None),
        P(("gx", "gy"), None, None),
        P(("gx", "gy"), None),
        P(("gx", "gy")),
        P(),
        P("gx"),
        P("gy"),
    )
    out_specs = P(None, "gy", "gx", None)
    return jax.shard_map(
        on_device, mesh=mesh, in_specs=in_specs, out_specs=out_specs, check_vma=False
    )
```

```python
import functools
import math

import jax
import jax.numpy as jnp
import ml_dtypes
import numpy as np
from jax import lax
from jax.experimental import pallas as pl
from jax.experimental.pallas import tpu as pltpu
from jax.sharding import PartitionSpec as P

NX = 384
NY = 384
NZ = 384
TILE = 8
LANES = 128
PLANES = 32
CHUNK = 24
Z_CHIPS = 4
PARTS = 4
CELLS = TILE // PARTS
STRIDE = NY + TILE
PHASES = 128
BF16 = jnp.bfloat16
F32 = jnp.float32
VMEM_LIMIT = 8 * 1024 * 1024


def halves(array):
    high = array.astype(ml_dtypes.bfloat16)
    low = (array - high.astype(np.float64)).astype(ml_dtypes.bfloat16)
    return high, low


def split(value):
    high = value.astype(BF16)
    return high, (value - high.astype(F32)).astype(BF16)


def waves(freq, position, length):
    steps = np.mod(freq[:, None] * position[None, :], length)
    phase = 2.0 * math.pi * steps / length
    return np.cos(phase), np.sin(phase)


def depth_tables(planes):
    matrices, phases = [], []
    lane_part = np.arange(LANES) // 64
    lane_odd = np.arange(LANES) // 32 % 2
    lane_plane = np.arange(LANES) % 32
    used = (lane_plane < planes).astype(np.float64)
    for index in range(NZ // 2 // planes):
        position = index * planes + lane_plane - NZ // 4
        cos, sin = waves(np.arange(TILE) - NZ // 2, position, NZ)
        cos, sin = cos * used / math.sqrt(NZ), sin * used / math.sqrt(NZ)
        real = np.where(lane_part == 0, cos, sin)
        imag = np.where(lane_part == 0, -sin, cos)
        high, low = halves(np.concatenate((real, imag)))
        matrices.append(np.concatenate((high, high, low)))
        cos, sin = waves(np.arange(NZ // TILE), position, NZ // TILE)
        sign = np.where(lane_odd == 1, -1.0, 1.0)[None, :]
        sin = sin * np.where(lane_part == 0, -1.0, 1.0)[None, :]
        phases.append(np.stack((np.concatenate((cos, cos * sign)), np.concatenate((sin, sin * sign)))))
    return np.stack(matrices), np.stack(phases).astype(np.float32)


def column_tables():
    third = NY // 3
    out = []
    for residue in range(3):
        cos, sin = waves(3 * np.arange(NY // 6) + residue - NY // 4, np.arange(third) - NY // 2, NY)
        high, low = halves(np.concatenate((cos, sin)) / math.sqrt(NY))
        out.append(np.block([[high, high], [low, np.zeros_like(low)]]))
    return np.stack(out)


def row_tables():
    half = NX // 2
    freq = np.arange(half).reshape(-1, PARTS, CELLS).transpose(1, 0, 2).reshape(-1) - half
    quarter = NX // 4
    out = []
    for parity in range(2):
        position = 2 * np.arange(quarter) + parity - NX // 4
        cos, sin = waves(freq, position, NX)
        table = np.zeros((half, 2 * LANES))
        lanes = (np.arange(quarter) + parity * quarter) % LANES
        table[:, lanes] = cos / math.sqrt(NX)
        table[:, LANES + lanes] = sin / math.sqrt(NX)
        out.append(np.stack(halves(table)))
    return np.stack(out)


def order_tables():
    first = np.zeros((LANES, NX // 2))
    second = np.zeros((LANES, NX // 2))
    quarter = NX // 4
    for m1 in range(NX // 2):
        place = m1 // 2 + m1 % 2 * quarter
        if place < LANES:
            first[place, m1] = 1.0
        else:
            second[place - LANES, m1] = 1.0
    return np.concatenate((first, first, second, second)).astype(ml_dtypes.bfloat16)


def divide(value, divisor, limit):
    for shift in range(8, 24):
        factor = (1 << shift) // divisor + 1
        tried = np.arange(limit, dtype=np.int64)
        if factor * limit < 1 << 31 and np.array_equal(tried * factor >> shift, tried // divisor):
            return lax.shift_right_logical(value * factor, shift)
    raise ValueError(divisor)


def spread_kernel(tile_rows, tile_cols, grid_cols, devices, samples_ref, kernel_ref, offsets_ref, owners_ref, ids_ref, out_ref):
    owner, tile_id = owners_ref[...], ids_ref[...]
    tile_depth = NZ // TILE
    tiles_device = tile_rows * tile_cols * tile_depth
    owner_row = divide(owner, grid_cols, devices)
    tile_row = divide(tile_id, tile_cols * tile_depth, tiles_device)
    tile_col = divide(tile_id, tile_depth, tiles_device)
    row = owner_row * tile_rows + tile_row
    col = (owner - owner_row * grid_cols) * tile_cols + tile_col - tile_row * tile_cols
    folds = NX // TILE // 2
    upper = (row >= folds).astype(jnp.int32)
    base = (row - upper * folds) * (CELLS * STRIDE // TILE) + col
    phase = tile_id - tile_col * tile_depth + upper * tile_depth
    codes = (base * PHASES + phase).astype(F32)

    blocks = samples_ref.shape[0]
    taps = kernel_ref.shape[2]
    cell = lax.broadcasted_iota(jnp.int32, (TILE, LANES), 0)
    left = lax.broadcasted_iota(jnp.int32, (2 * TILE, LANES), 1) < LANES // 2

    def weights(block):
        placed = []
        for dim in range(3):
            shifted = cell - offsets_ref[dim, pl.ds(block, 1), :]
            value = jnp.zeros((TILE, LANES), F32)
            for tap in range(taps):
                value = jnp.where(shifted == tap, kernel_ref[block, dim, pl.ds(tap, 1), :], value)
            placed.append(value)
        plane = jnp.concatenate([placed[0][i : i + 1] * placed[1] for i in range(TILE)], axis=0)
        depth = jnp.concatenate([samples_ref[block, pl.ds(c, 1), :] * placed[2] for c in range(2)], axis=0)
        return depth, plane

    def pair_body(pair, carry):
        depth_a, plane_a = weights(2 * pair)
        depth_b, plane_b = weights(2 * pair + 1)
        depth_high, depth_low = split(jnp.concatenate((depth_a, depth_b), axis=0))
        plane_high, plane_low = split(jnp.concatenate((plane_a, plane_b), axis=0))
        piece = lax.dot_general(
            jnp.concatenate((depth_high, depth_low, depth_high), axis=1),
            jnp.concatenate((plane_high, plane_high, plane_low), axis=1),
            (((1,), (1,)), ((), ())),
            preferred_element_type=F32,
        )
        out_ref[pair] = jnp.where(left, piece[: 2 * TILE], piece[2 * TILE :])
        return carry

    lax.fori_loop(0, blocks // 2, pair_body, 0, unroll=8)
    out_ref[blocks // 2] = jnp.broadcast_to(codes, (2 * TILE, LANES))


def tiles_kernel(conditions, first, last, *refs):
    arrays = len(conditions)
    places_ref = refs[0]
    source_refs = refs[1 : 1 + arrays]
    depth_tables_ref, phase_tables_ref = refs[1 + arrays : 3 + arrays]
    acc_refs = refs[-5 - PARTS : -5]
    token_ref, codes_ref, depth_ref, phases_ref, arrived = refs[-5:]
    token_ref[...] = jnp.zeros_like(token_ref)
    stride = STRIDE
    pairs = source_refs[0].shape[0] - 1

    def copies(index):
        return pltpu.make_async_copy(
            source_refs[index].at[pairs, pl.ds(0, TILE)], codes_ref.at[index], arrived.at[index]
        )

    tables = [
        pltpu.make_async_copy(depth_tables_ref.at[places_ref[2]], depth_ref, arrived.at[arrays]),
        pltpu.make_async_copy(phase_tables_ref.at[places_ref[2]], phases_ref, arrived.at[arrays + 1]),
    ]
    for index in range(arrays):
        copies(index).start()
    for table in tables:
        table.start()

    if first:

        def clear(step, carry):
            at = pl.ds(pl.multiple_of(step * stride, stride), stride)
            for ref in acc_refs:
                ref[at, :] = jnp.zeros((stride, LANES), F32)
            return carry

        lax.fori_loop(0, NX // 2 // PARTS, clear, 0)

    for index in range(arrays):
        copies(index).wait()
    for table in tables:
        table.wait()

    def add_source(index):
        tiles_ref = source_refs[index]

        def add_pair(pair, carry):
            high, low = split(tiles_ref[pair])
            spectrum = lax.dot_general(
                jnp.concatenate((high, low, high), axis=0),
                depth_ref[...],
                (((0,), (0,)), ((), ())),
                preferred_element_type=F32,
            )
            for side in range(2):
                code = codes_ref[index, 0, 2 * pair + side].astype(jnp.int32)
                base = lax.shift_right_logical(code, 7)
                phase = jnp.bitwise_and(code, PHASES - 1)
                cos = phases_ref[0, pl.ds(phase, 1), :]
                sin = phases_ref[1, pl.ds(phase, 1), :]
                for i in range(TILE):
                    row = side * TILE * TILE + i * TILE
                    value = spectrum[row : row + TILE]
                    value = value * cos + pltpu.roll(value, LANES // 2, 1) * sin
                    acc_ref = acc_refs[i // CELLS]
                    at = pl.ds(pl.multiple_of(base * TILE + i % CELLS * stride, TILE), TILE)
                    acc_ref[at, :] = acc_ref[at, :] + value
            return carry

        lax.fori_loop(0, pairs, add_pair, 0, unroll=16)

    for index, condition in enumerate(conditions):
        if condition is None:
            add_source(index)
        else:
            holds = places_ref[0] == condition[0]
            for depth in condition[1:]:
                holds = jnp.logical_or(holds, places_ref[0] == depth)
            pl.when(holds)(functools.partial(add_source, index))

    if last:
        transform_columns(refs[3 + arrays], acc_refs)


def transform_columns(column_ref, acc_refs):
    third = NY // 3
    rows = column_ref.shape[1] // 4
    turn = jnp.where(lax.broadcasted_iota(jnp.int32, (1, LANES), 1) < LANES // 2, -1.0, 1.0)

    def columns(step, carry):
        start = pl.multiple_of(step * STRIDE, TILE)
        for pair in range(0, PARTS, 2):
            folded = ([], [], [])
            for ref in acc_refs[pair : pair + 2]:
                first, second, last = (ref[pl.ds(start + third * part, third), :] for part in range(3))
                both = second + last
                across = pltpu.roll(second - last, LANES // 2, 1) * (turn * math.sqrt(0.75))
                middle = first - 0.5 * both
                folded[0].append(first + both)
                folded[1].append(middle + across)
                folded[2].append(middle - across)
            for residue in range(3):
                high, low = split(jnp.concatenate(folded[residue], axis=1))
                product = jnp.dot(
                    column_ref[residue], jnp.concatenate((high, low), axis=0), preferred_element_type=F32
                )
                product = product[: 2 * rows] + product[2 * rows :]
                for side, ref in enumerate(acc_refs[pair : pair + 2]):
                    lanes = slice(side * LANES, (side + 1) * LANES)
                    ref[pl.ds(start + residue * rows, rows), :] = (
                        product[:rows, lanes] + pltpu.roll(product[rows:, lanes], LANES // 2, 1) * turn
                    )
        return carry

    lax.fori_loop(0, NX // 2 // PARTS, columns, 0, unroll=16)


def rows_kernel(relative, first, count, chunks, grid_rows, addends, planes_padded, places_ref, *refs):
    acc_refs, row_ref, addend_refs, out_ref = refs[:PARTS], refs[PARTS], refs[PARTS + 1 : -1], refs[-1]
    assert len(addend_refs) == addends
    rows = grid_rows * chunks * TILE
    device = jnp.bitwise_xor(places_ref[1], relative)
    lane = lax.broadcasted_iota(jnp.int32, (PLANES, LANES), 1)

    def block(step, carry):
        chunk, residue = step // 3, step % 3
        start = residue * rows + (device * chunks + first + chunk) * TILE
        turned = []
        for row in range(TILE):
            at = pl.ds(start + row, NX // 2 // PARTS, stride=STRIDE)
            turned.append(jnp.concatenate([ref[at, :] for ref in acc_refs], axis=0).T)
        parts = []
        for odd in range(2):
            at = odd * PLANES
            stacked = [value[part * 64 + at : part * 64 + at + PLANES] for value in turned for part in range(2)]
            high, low = split(jnp.concatenate(stacked, axis=0))
            size = high.shape[0]
            both = jnp.dot(jnp.concatenate((high, low), axis=0), row_ref[odd, 0], preferred_element_type=F32)
            product = both[:size] + both[size:] + jnp.dot(high, row_ref[odd, 1], preferred_element_type=F32)
            sides = []
            for row in range(TILE):
                real = product[2 * row * PLANES : (2 * row + 1) * PLANES]
                imag = product[(2 * row + 1) * PLANES : (2 * row + 2) * PLANES]
                sides.append((real[:, :LANES] - imag[:, LANES:], real[:, LANES:] + imag[:, :LANES]))
            parts.append(sides)
        for slot in range(TILE // 2):
            place = chunk * (CHUNK // 2) + 3 * slot + residue
            for part in range(2):
                even = [parts[0][slot + side * TILE // 2][part] for side in range(2)]
                odd = [parts[1][slot + side * TILE // 2][part] for side in range(2)]
                values = [jnp.where(lane < NX // 4, even[side], odd[side]) for side in range(2)]
                values.append(jnp.where(lane < LANES // 2, odd[0], pltpu.roll(odd[1], LANES // 2, 1)))
                for number, value in enumerate(values):
                    planes = pl.ds(part * planes_padded, planes_padded)
                    total = value[:planes_padded]
                    for ref in addend_refs:
                        shift = first * (CHUNK // 2) if ref.shape[0] > out_ref.shape[0] else 0
                        total = total + ref[shift + place, number, planes]
                    out_ref[place, number, planes] = total
        return carry

    lax.fori_loop(0, 3 * count, block, 0, unroll=3)


def finish_kernel(chunk, planes_padded, parts, refs):
    part_refs = refs[:parts]
    order_ref, first_ref, second_ref, third_ref = refs[parts : parts + 4]
    out_ref = refs[-1]
    planes = out_ref.shape[1]
    slots = part_refs[0].shape[0]
    stride = 6 * planes_padded
    flats = [ref.reshape(slots * stride, LANES) for ref in part_refs]
    order = order_ref[...]
    shape = (CHUNK, second_ref.shape[1])
    here = lax.broadcasted_iota(jnp.int32, shape, 1) == lax.broadcasted_iota(jnp.int32, shape, 0) + chunk * CHUNK
    second = jnp.sum(jnp.where(here, second_ref[...], 0.0), axis=1, keepdims=True)
    scale = second * first_ref[...]
    for part in range(2):
        for group in range(0, planes, TILE):
            members = range(group, min(group + TILE, planes))
            mains, rests = [], []
            for plane in members:
                values = []
                for number in range(3):
                    at = pl.ds((number * 2 + part) * planes_padded + plane, slots, stride=stride)
                    total = flats[0][at, :]
                    for flat in flats[1:]:
                        total = total + flat[at, :]
                    values.append(total)
                mains.append(jnp.concatenate(values[:2], axis=0))
                rests.append(jnp.concatenate((values[2], pltpu.roll(values[2], LANES // 2, 1)), axis=0))
            main = split(jnp.concatenate(mains, axis=0))
            rest = split(jnp.concatenate(rests, axis=0))
            ordered = jnp.dot(jnp.concatenate(main + rest, axis=1), order, preferred_element_type=F32)
            for index, plane in enumerate(members):
                out_ref[part, plane] = ordered[index * 2 * slots : (index + 1) * 2 * slots] * (scale * third_ref[plane])


def on_device(samples, kernel, offsets, owners, tile_ids, deapod_first, deapod_second, deapod_third):
    grid_rows = lax.axis_size("gx")
    grid_cols = lax.axis_size("gy")
    blocks = samples.shape[0]
    block_width = samples.shape[2]
    assert block_width == LANES and blocks == LANES
    tile_rows = NX // (TILE * grid_rows)
    tile_cols = NY // (TILE * grid_cols)
    planes = deapod_third.shape[0]
    per_device = deapod_second.shape[0]
    assert per_device % CHUNK == 0
    chunks = per_device // CHUNK
    slots = CHUNK // 2
    planes_padded = -(-planes // 8) * 8
    vmem = pl.BlockSpec(memory_space=pltpu.VMEM)
    params = pltpu.CompilerParams(vmem_limit_bytes=VMEM_LIMIT)

    def in_hbm(arrays):
        return [pltpu.with_memory_space_constraint(array, pltpu.HBM) for array in arrays]

    tiles = pl.pallas_call(
        functools.partial(spread_kernel, tile_rows, tile_cols, grid_cols, grid_rows * grid_cols),
        out_shape=pltpu.HBM((blocks // 2 + 1, 2 * TILE, LANES), F32),
        in_specs=[vmem] * 5,
        out_specs=vmem,
        compiler_params=params,
        name="spread",
    )(*in_hbm([samples, kernel, offsets.transpose(1, 0, 2), owners.reshape(1, blocks), tile_ids.reshape(1, blocks)]))

    along = grid_cols // Z_CHIPS
    deep_at = lax.div(lax.axis_index("gy").astype(jnp.int32), jnp.int32(along))

    def send(value, moves_z, wide):
        moves = [(a * along + y, b * along + (y + wide) % along) for a, b in moves_z for y in range(along)]
        return lax.ppermute(value, "gy", moves)

    places = jnp.stack((deep_at, lax.axis_index("gx").astype(jnp.int32), lax.axis_index("gy").astype(jnp.int32)))
    matrices, phases = (jnp.asarray(table) for table in depth_tables(planes))
    column = jnp.asarray(column_tables())
    half = NX // 2
    smem = pl.BlockSpec(memory_space=pltpu.SMEM)
    acc_shape = (half // PARTS * STRIDE, LANES)

    def in_vmem(arrays):
        return [pltpu.with_memory_space_constraint(array, pltpu.VMEM) for array in arrays]

    def add_tiles(sources, acc, columns=()):
        conditions = [None if len(holders) == Z_CHIPS else tuple(holders) for holders, _ in sources]
        kept = [jax.ShapeDtypeStruct(acc_shape, F32) if acc else pltpu.VMEM(acc_shape, F32)] * PARTS
        inputs = len(sources) + 3 + len(columns)
        *acc, token = pl.pallas_call(
            functools.partial(tiles_kernel, conditions, not acc, bool(columns)),
            out_shape=kept + [jax.ShapeDtypeStruct((TILE, LANES), F32)],
            in_specs=[smem] + [vmem] * len(sources) + [pl.BlockSpec(memory_space=pl.ANY)] * 2 + [vmem] * (len(columns) + len(acc)),
            out_specs=[vmem] * (PARTS + 1),
            input_output_aliases={inputs + part: part for part in range(PARTS)} if acc else {},
            scratch_shapes=[
                pltpu.SMEM((len(sources), TILE, LANES), F32),
                pltpu.VMEM(matrices.shape[1:], BF16),
                pltpu.VMEM(phases.shape[1:], F32),
                pltpu.SemaphoreType.DMA((len(sources) + 2,)),
            ],
            compiler_params=params,
            cost_estimate=pl.CostEstimate(flops=0, bytes_accessed=len(sources) << 23, transcendentals=0),
            name="tiles",
        )(places, *[array for _, array in sources], *in_hbm([matrices, phases, *columns]), *in_vmem(acc))
        return acc, token

    def after(value, token):
        return lax.optimization_barrier((value, token))[0]

    def across(value, holders):
        return [(holders, send(value, [(z, z) for z in holders], wide)) for wide in range(1, along)]

    every = range(Z_CHIPS)
    passed = {1: tiles, -1: tiles}
    arrived, token, acc = [(every, tiles)], None, []
    for steps in range(1, Z_CHIPS + 1):
        partners = []
        if steps == 1:
            partners += across(tiles, every)
        else:
            partners += [held for holders, array in arrived[:2] for held in across(after(array, token), holders)]
        moved = []
        if steps < Z_CHIPS:
            for way in (1, -1):
                moves = [(z, z + way) for z in every if 0 <= z + way < Z_CHIPS and 0 <= z - way * (steps - 1) < Z_CHIPS]
                value = passed[way] if token is None else after(passed[way], token)
                passed[way] = send(value, moves, 0)
                moved.append(([to for _, to in moves], passed[way]))
        acc, token = add_tiles(arrived, acc)
        arrived = moved + partners
    acc, _ = add_tiles(arrived, acc, [column])

    row_table = jnp.asarray(row_tables())
    part_shape = (3, 2 * planes_padded, LANES)

    def rows_for(relative, first, count, addends, after):
        def body(*refs):
            operands = 2 + PARTS + len(addends)
            rows_kernel(
                relative, first, count, chunks, grid_rows, len(addends), planes_padded, *refs[:operands], refs[-1]
            )

        return pl.pallas_call(
            body,
            in_specs=[smem] + [vmem] * (1 + PARTS + len(addends)) + [pl.BlockSpec(memory_space=pl.ANY)] * len(after),
            out_specs=vmem,
            out_shape=jax.ShapeDtypeStruct((count * slots,) + part_shape, F32),
            compiler_params=params,
            cost_estimate=pl.CostEstimate(flops=1, bytes_accessed=1, transcendentals=0),
            name="rows",
        )(places, *in_vmem(acc), row_table, *addends, *after)

    def swap(value, bit):
        return lax.ppermute(value, "gx", [(index, index ^ bit) for index in range(grid_rows)])

    last = []

    def rows_next(relative, first, count, addends):
        part = rows_for(relative, first, count, addends, last)
        last[:] = [part]
        return part

    def arrivals(relative, top):
        arrived = []
        bit = 1
        while bit <= top:
            arrived.append(swap(rows_next(relative | bit, 0, chunks, arrivals(relative | bit, bit // 2)), bit))
            bit *= 2
        return arrived

    top = grid_rows // 2
    far = arrivals(top, top // 2)
    near, crossed = [], []
    for chunk in range(chunks):
        if top == 2:
            near.append([(swap(rows_next(1, chunk, 1, []), 1), 0)])
        elif chunk == 0:
            arrived = arrivals(0, top // 2)
            near += [[(array, place) for array in arrived] for place in range(chunks)]
        crossed.append(swap(rows_next(top, chunk, 1, far), top))
    kept = rows_next(0, 0, chunks, [])
    parts = [[(kept, chunk), *near[chunk], (crossed[chunk], 0)] for chunk in range(chunks)]

    image = None
    for chunk in range(chunks):

        def finish(*refs, chunk=chunk):
            finish_kernel(chunk, planes_padded, len(parts[chunk]), refs)

        earlier = [] if image is None else [image]
        image = pl.pallas_call(
            finish,
            grid=(1,),
            out_shape=jax.ShapeDtypeStruct((2, planes, per_device, NX // 2), F32),
            in_specs=[
                pl.BlockSpec((slots,) + part_shape, lambda step, place=place: (place, 0, 0, 0))
                for _, place in parts[chunk]
            ]
            + [
                pl.BlockSpec((4 * LANES, NX // 2), lambda step: (0, 0)),
                pl.BlockSpec((1, NX // 2), lambda step: (0, 0)),
                pl.BlockSpec((1, per_device), lambda step: (0, 0)),
                pl.BlockSpec(memory_space=pltpu.SMEM),
            ]
            + [pl.BlockSpec(memory_space=pl.ANY)] * len(earlier),
            out_specs=pl.BlockSpec((2, planes, CHUNK, NX // 2), lambda step, chunk=chunk: (0, 0, chunk, 0)),
            input_output_aliases={len(parts[chunk]) + 4: 0} if earlier else {},
            compiler_params=params,
            name="finish",
        )(
            *[array for array, _ in parts[chunk]],
            jnp.asarray(order_tables()),
            deapod_first[None, :],
            deapod_second[None, :],
            deapod_third,
            *earlier,
        )
    return image


def solution(mesh):
    in_specs = (
        P(("gx", "gy"), None, None),
        P(("gx", "gy"), None, None, None),
        P(("gx", "gy"), None, None),
        P(("gx", "gy"), None),
        P(("gx", "gy")),
        P(),
        P("gx"),
        P("gy"),
    )
    out_specs = P(None, "gy", "gx", None)
    return jax.shard_map(
        on_device, mesh=mesh, in_specs=in_specs, out_specs=out_specs, check_vma=False
    )
```

```python
import functools
import math

import jax
import jax.numpy as jnp
import ml_dtypes
import numpy as np
from jax import lax
from jax.experimental import pallas as pl
from jax.experimental.pallas import tpu as pltpu
from jax.sharding import PartitionSpec as P

NX = 384
NY = 384
NZ = 384
TILE = 8
LANES = 128
PLANES = 32
CHUNK = 24
Z_CHIPS = 4
PARTS = 4
CELLS = TILE // PARTS
STRIDE = NY + TILE
PHASES = 128
BF16 = jnp.bfloat16
F32 = jnp.float32
VMEM_LIMIT = 8 * 1024 * 1024


def halves(array):
    high = array.astype(ml_dtypes.bfloat16)
    low = (array - high.astype(np.float64)).astype(ml_dtypes.bfloat16)
    return high, low


def split(value):
    high = value.astype(BF16)
    return high, (value - high.astype(F32)).astype(BF16)


def waves(freq, position, length):
    steps = np.mod(freq[:, None] * position[None, :], length)
    phase = 2.0 * math.pi * steps / length
    return np.cos(phase), np.sin(phase)


def depth_tables(planes):
    matrices, phases = [], []
    lane_part = np.arange(LANES) // 64
    lane_odd = np.arange(LANES) // 32 % 2
    lane_plane = np.arange(LANES) % 32
    used = (lane_plane < planes).astype(np.float64)
    for index in range(NZ // 2 // planes):
        position = index * planes + lane_plane - NZ // 4
        cos, sin = waves(np.arange(TILE) - NZ // 2, position, NZ)
        cos, sin = cos * used / math.sqrt(NZ), sin * used / math.sqrt(NZ)
        real = np.where(lane_part == 0, cos, sin)
        imag = np.where(lane_part == 0, -sin, cos)
        high, low = halves(np.concatenate((real, imag)))
        matrices.append(np.concatenate((high, high, low)))
        cos, sin = waves(np.arange(NZ // TILE), position, NZ // TILE)
        sign = np.where(lane_odd == 1, -1.0, 1.0)[None, :]
        sin = sin * np.where(lane_part == 0, -1.0, 1.0)[None, :]
        phases.append(np.stack((np.concatenate((cos, cos * sign)), np.concatenate((sin, sin * sign)))))
    return np.stack(matrices), np.stack(phases).astype(np.float32)


def column_tables():
    third = NY // 3
    out = []
    for residue in range(3):
        cos, sin = waves(3 * np.arange(NY // 6) + residue - NY // 4, np.arange(third) - NY // 2, NY)
        high, low = halves(np.concatenate((cos, sin)) / math.sqrt(NY))
        out.append(np.block([[high, high], [low, np.zeros_like(low)]]))
    return np.stack(out)


def row_tables():
    half = NX // 2
    freq = np.arange(half).reshape(-1, PARTS, CELLS).transpose(1, 0, 2).reshape(-1) - half
    quarter = NX // 4
    out = []
    for parity in range(2):
        position = 2 * np.arange(quarter) + parity - NX // 4
        cos, sin = waves(freq, position, NX)
        table = np.zeros((half, 2 * LANES))
        lanes = (np.arange(quarter) + parity * quarter) % LANES
        table[:, lanes] = cos / math.sqrt(NX)
        table[:, LANES + lanes] = sin / math.sqrt(NX)
        out.append(np.stack(halves(table)))
    return np.stack(out)


def order_tables():
    first = np.zeros((LANES, NX // 2))
    second = np.zeros((LANES, NX // 2))
    quarter = NX // 4
    for m1 in range(NX // 2):
        place = m1 // 2 + m1 % 2 * quarter
        if place < LANES:
            first[place, m1] = 1.0
        else:
            second[place - LANES, m1] = 1.0
    return np.concatenate((first, first, second, second)).astype(ml_dtypes.bfloat16)


def divide(value, divisor, limit):
    for shift in range(8, 24):
        factor = (1 << shift) // divisor + 1
        tried = np.arange(limit, dtype=np.int64)
        if factor * limit < 1 << 31 and np.array_equal(tried * factor >> shift, tried // divisor):
            return lax.shift_right_logical(value * factor, shift)
    raise ValueError(divisor)


def spread_kernel(tile_rows, tile_cols, grid_cols, devices, samples_ref, kernel_ref, offsets_ref, owners_ref, ids_ref, out_ref):
    owner, tile_id = owners_ref[...], ids_ref[...]
    tile_depth = NZ // TILE
    tiles_device = tile_rows * tile_cols * tile_depth
    owner_row = divide(owner, grid_cols, devices)
    tile_row = divide(tile_id, tile_cols * tile_depth, tiles_device)
    tile_col = divide(tile_id, tile_depth, tiles_device)
    row = owner_row * tile_rows + tile_row
    col = (owner - owner_row * grid_cols) * tile_cols + tile_col - tile_row * tile_cols
    folds = NX // TILE // 2
    upper = (row >= folds).astype(jnp.int32)
    base = (row - upper * folds) * (CELLS * STRIDE // TILE) + col
    phase = tile_id - tile_col * tile_depth + upper * tile_depth
    codes = (base * PHASES + phase).astype(F32)

    blocks = samples_ref.shape[0]
    taps = kernel_ref.shape[2]
    cell = lax.broadcasted_iota(jnp.int32, (TILE, LANES), 0)
    left = lax.broadcasted_iota(jnp.int32, (2 * TILE, LANES), 1) < LANES // 2

    def weights(block):
        placed = []
        for dim in range(3):
            shifted = cell - offsets_ref[dim, pl.ds(block, 1), :]
            value = jnp.zeros((TILE, LANES), F32)
            for tap in range(taps):
                value = jnp.where(shifted == tap, kernel_ref[block, dim, pl.ds(tap, 1), :], value)
            placed.append(value)
        plane = jnp.concatenate([placed[0][i : i + 1] * placed[1] for i in range(TILE)], axis=0)
        depth = jnp.concatenate([samples_ref[block, pl.ds(c, 1), :] * placed[2] for c in range(2)], axis=0)
        return depth, plane

    def pair_body(pair, carry):
        depth_a, plane_a = weights(2 * pair)
        depth_b, plane_b = weights(2 * pair + 1)
        depth_high, depth_low = split(jnp.concatenate((depth_a, depth_b), axis=0))
        plane_high, plane_low = split(jnp.concatenate((plane_a, plane_b), axis=0))
        piece = lax.dot_general(
            jnp.concatenate((depth_high, depth_low, depth_high), axis=1),
            jnp.concatenate((plane_high, plane_high, plane_low), axis=1),
            (((1,), (1,)), ((), ())),
            preferred_element_type=F32,
        )
        out_ref[pair] = jnp.where(left, piece[: 2 * TILE], piece[2 * TILE :])
        return carry

    lax.fori_loop(0, blocks // 2, pair_body, 0, unroll=16)
    out_ref[blocks // 2] = jnp.broadcast_to(codes, (2 * TILE, LANES))


def tiles_kernel(conditions, first, last, *refs):
    arrays = len(conditions)
    places_ref = refs[0]
    source_refs = refs[1 : 1 + arrays]
    depth_tables_ref, phase_tables_ref = refs[1 + arrays : 3 + arrays]
    acc_refs = refs[-7 - PARTS : -7]
    token_ref, codes_ref, depth_ref, phases_ref, even_ref, odd_ref, arrived = refs[-7:]
    token_ref[...] = jnp.zeros_like(token_ref)
    stride = STRIDE
    pairs = source_refs[0].shape[0] - 1
    batch = 8
    batches = pairs // batch
    assert batches % 2 == 0

    def copies(index):
        return pltpu.make_async_copy(
            source_refs[index].at[pairs, pl.ds(0, TILE)], codes_ref.at[index], arrived.at[index]
        )

    tables = [
        pltpu.make_async_copy(depth_tables_ref.at[places_ref[2]], depth_ref, arrived.at[arrays]),
        pltpu.make_async_copy(phase_tables_ref.at[places_ref[2]], phases_ref, arrived.at[arrays + 1]),
    ]
    for index in range(arrays):
        copies(index).start()
    for table in tables:
        table.start()

    if first:

        def clear(step, carry):
            at = pl.ds(pl.multiple_of(step * stride, stride), stride)
            for ref in acc_refs:
                ref[at, :] = jnp.zeros((stride, LANES), F32)
            return carry

        lax.fori_loop(0, NX // 2 // PARTS, clear, 0)

    for index in range(arrays):
        copies(index).wait()
    for table in tables:
        table.wait()

    def add_source(index):
        tiles_ref = source_refs[index]

        def spectrum(number, to_ref):
            tiles = jnp.concatenate([tiles_ref[number * batch + place] for place in range(batch)], axis=1)
            high, low = split(tiles)
            to_ref[...] = lax.dot_general(
                jnp.concatenate((high, low, high), axis=0),
                depth_ref[...],
                (((0,), (0,)), ((), ())),
                preferred_element_type=F32,
            )

        def accumulate(number, from_ref):
            for tile in range(2 * batch):
                code = codes_ref[index, 0, number * 2 * batch + tile].astype(jnp.int32)
                base = lax.shift_right_logical(code, 7)
                phase = jnp.bitwise_and(code, PHASES - 1)
                cos = phases_ref[0, pl.ds(phase, 1), :]
                sin = phases_ref[1, pl.ds(phase, 1), :]
                for i in range(TILE):
                    row = tile * TILE * TILE + i * TILE
                    value = from_ref[row : row + TILE, :]
                    value = value * cos + pltpu.roll(value, LANES // 2, 1) * sin
                    acc_ref = acc_refs[i // CELLS]
                    at = pl.ds(pl.multiple_of(base * TILE + i % CELLS * stride, TILE), TILE)
                    acc_ref[at, :] = acc_ref[at, :] + value

        spectrum(0, even_ref)

        def add_pair(step, carry):
            number = 2 * step
            spectrum(number + 1, odd_ref)
            accumulate(number, even_ref)
            spectrum(jnp.minimum(number + 2, batches - 2), even_ref)
            accumulate(number + 1, odd_ref)
            return carry

        lax.fori_loop(0, batches // 2, add_pair, 0, unroll=2)

    for index, condition in enumerate(conditions):
        if condition is None:
            add_source(index)
        else:
            holds = places_ref[0] == condition[0]
            for depth in condition[1:]:
                holds = jnp.logical_or(holds, places_ref[0] == depth)
            pl.when(holds)(functools.partial(add_source, index))

    if last:
        transform_columns(refs[3 + arrays], acc_refs)


def transform_columns(column_ref, acc_refs):
    third = NY // 3
    rows = column_ref.shape[1] // 4
    turn = jnp.where(lax.broadcasted_iota(jnp.int32, (1, LANES), 1) < LANES // 2, -1.0, 1.0)

    def columns(step, carry):
        start = pl.multiple_of(step * STRIDE, TILE)
        for pair in range(0, PARTS, 2):
            folded = ([], [], [])
            for ref in acc_refs[pair : pair + 2]:
                first, second, last = (ref[pl.ds(start + third * part, third), :] for part in range(3))
                both = second + last
                across = pltpu.roll(second - last, LANES // 2, 1) * (turn * math.sqrt(0.75))
                middle = first - 0.5 * both
                folded[0].append(first + both)
                folded[1].append(middle + across)
                folded[2].append(middle - across)
            for residue in range(3):
                high, low = split(jnp.concatenate(folded[residue], axis=1))
                product = jnp.dot(
                    column_ref[residue], jnp.concatenate((high, low), axis=0), preferred_element_type=F32
                )
                product = product[: 2 * rows] + product[2 * rows :]
                for side, ref in enumerate(acc_refs[pair : pair + 2]):
                    lanes = slice(side * LANES, (side + 1) * LANES)
                    ref[pl.ds(start + residue * rows, rows), :] = (
                        product[:rows, lanes] + pltpu.roll(product[rows:, lanes], LANES // 2, 1) * turn
                    )
        return carry

    lax.fori_loop(0, NX // 2 // PARTS, columns, 0, unroll=16)


def rows_kernel(relative, first, count, chunks, grid_rows, addends, planes_padded, places_ref, *refs):
    acc_refs, row_ref, addend_refs, out_ref = refs[:PARTS], refs[PARTS], refs[PARTS + 1 : -1], refs[-1]
    assert len(addend_refs) == addends
    rows = grid_rows * chunks * TILE
    device = jnp.bitwise_xor(places_ref[1], relative)
    lane = lax.broadcasted_iota(jnp.int32, (PLANES, LANES), 1)

    def block(step, carry):
        chunk, residue = step // 3, step % 3
        start = residue * rows + (device * chunks + first + chunk) * TILE
        turned = []
        for row in range(TILE):
            at = pl.ds(start + row, NX // 2 // PARTS, stride=STRIDE)
            turned.append(jnp.concatenate([ref[at, :] for ref in acc_refs], axis=0).T)
        parts = []
        for odd in range(2):
            at = odd * PLANES
            stacked = [value[part * 64 + at : part * 64 + at + PLANES] for value in turned for part in range(2)]
            high, low = split(jnp.concatenate(stacked, axis=0))
            size = high.shape[0]
            both = jnp.dot(jnp.concatenate((high, low), axis=0), row_ref[odd, 0], preferred_element_type=F32)
            product = both[:size] + both[size:] + jnp.dot(high, row_ref[odd, 1], preferred_element_type=F32)
            sides = []
            for row in range(TILE):
                real = product[2 * row * PLANES : (2 * row + 1) * PLANES]
                imag = product[(2 * row + 1) * PLANES : (2 * row + 2) * PLANES]
                sides.append((real[:, :LANES] - imag[:, LANES:], real[:, LANES:] + imag[:, :LANES]))
            parts.append(sides)
        for slot in range(TILE // 2):
            place = chunk * (CHUNK // 2) + 3 * slot + residue
            for part in range(2):
                even = [parts[0][slot + side * TILE // 2][part] for side in range(2)]
                odd = [parts[1][slot + side * TILE // 2][part] for side in range(2)]
                values = [jnp.where(lane < NX // 4, even[side], odd[side]) for side in range(2)]
                values.append(jnp.where(lane < LANES // 2, odd[0], pltpu.roll(odd[1], LANES // 2, 1)))
                for number, value in enumerate(values):
                    planes = pl.ds(part * planes_padded, planes_padded)
                    total = value[:planes_padded]
                    for ref in addend_refs:
                        shift = first * (CHUNK // 2) if ref.shape[0] > out_ref.shape[0] else 0
                        total = total + ref[shift + place, number, planes]
                    out_ref[place, number, planes] = total
        return carry

    lax.fori_loop(0, 3 * count, block, 0, unroll=3)


def finish_kernel(chunk, planes_padded, parts, refs):
    part_refs = refs[:parts]
    order_ref, first_ref, second_ref, third_ref = refs[parts : parts + 4]
    out_ref = refs[-1]
    planes = out_ref.shape[1]
    slots = part_refs[0].shape[0]
    stride = 6 * planes_padded
    flats = [ref.reshape(slots * stride, LANES) for ref in part_refs]
    order = order_ref[...]
    shape = (CHUNK, second_ref.shape[1])
    here = lax.broadcasted_iota(jnp.int32, shape, 1) == lax.broadcasted_iota(jnp.int32, shape, 0) + chunk * CHUNK
    second = jnp.sum(jnp.where(here, second_ref[...], 0.0), axis=1, keepdims=True)
    scale = second * first_ref[...]
    for part in range(2):
        for group in range(0, planes, TILE):
            members = range(group, min(group + TILE, planes))
            mains, rests = [], []
            for plane in members:
                values = []
                for number in range(3):
                    at = pl.ds((number * 2 + part) * planes_padded + plane, slots, stride=stride)
                    total = flats[0][at, :]
                    for flat in flats[1:]:
                        total = total + flat[at, :]
                    values.append(total)
                mains.append(jnp.concatenate(values[:2], axis=0))
                rests.append(jnp.concatenate((values[2], pltpu.roll(values[2], LANES // 2, 1)), axis=0))
            main = split(jnp.concatenate(mains, axis=0))
            rest = split(jnp.concatenate(rests, axis=0))
            ordered = jnp.dot(jnp.concatenate(main + rest, axis=1), order, preferred_element_type=F32)
            for index, plane in enumerate(members):
                out_ref[part, plane] = ordered[index * 2 * slots : (index + 1) * 2 * slots] * (scale * third_ref[plane])


def on_device(samples, kernel, offsets, owners, tile_ids, deapod_first, deapod_second, deapod_third):
    grid_rows = lax.axis_size("gx")
    grid_cols = lax.axis_size("gy")
    blocks = samples.shape[0]
    block_width = samples.shape[2]
    assert block_width == LANES and blocks == LANES
    tile_rows = NX // (TILE * grid_rows)
    tile_cols = NY // (TILE * grid_cols)
    planes = deapod_third.shape[0]
    per_device = deapod_second.shape[0]
    assert per_device % CHUNK == 0
    chunks = per_device // CHUNK
    slots = CHUNK // 2
    planes_padded = -(-planes // 8) * 8
    vmem = pl.BlockSpec(memory_space=pltpu.VMEM)
    params = pltpu.CompilerParams(vmem_limit_bytes=VMEM_LIMIT)

    def in_hbm(arrays):
        return [pltpu.with_memory_space_constraint(array, pltpu.HBM) for array in arrays]

    tiles = pl.pallas_call(
        functools.partial(spread_kernel, tile_rows, tile_cols, grid_cols, grid_rows * grid_cols),
        out_shape=pltpu.HBM((blocks // 2 + 1, 2 * TILE, LANES), F32),
        in_specs=[vmem] * 5,
        out_specs=vmem,
        compiler_params=params,
        name="spread",
    )(*in_hbm([samples, kernel, offsets.transpose(1, 0, 2), owners.reshape(1, blocks), tile_ids.reshape(1, blocks)]))

    along = grid_cols // Z_CHIPS
    deep_at = lax.div(lax.axis_index("gy").astype(jnp.int32), jnp.int32(along))

    def send(value, moves_z, wide):
        moves = [(a * along + y, b * along + (y + wide) % along) for a, b in moves_z for y in range(along)]
        return lax.ppermute(value, "gy", moves)

    places = jnp.stack((deep_at, lax.axis_index("gx").astype(jnp.int32), lax.axis_index("gy").astype(jnp.int32)))
    matrices, phases = (jnp.asarray(table) for table in depth_tables(planes))
    column = jnp.asarray(column_tables())
    half = NX // 2
    smem = pl.BlockSpec(memory_space=pltpu.SMEM)
    acc_shape = (half // PARTS * STRIDE, LANES)

    def in_vmem(arrays):
        return [pltpu.with_memory_space_constraint(array, pltpu.VMEM) for array in arrays]

    def add_tiles(sources, acc, columns=()):
        conditions = [None if len(holders) == Z_CHIPS else tuple(holders) for holders, _ in sources]
        spectra = pltpu.VMEM((16 * TILE * TILE, LANES), F32)
        kept = [jax.ShapeDtypeStruct(acc_shape, F32) if acc else pltpu.VMEM(acc_shape, F32)] * PARTS
        inputs = len(sources) + 3 + len(columns)
        *acc, token = pl.pallas_call(
            functools.partial(tiles_kernel, conditions, not acc, bool(columns)),
            out_shape=kept + [jax.ShapeDtypeStruct((TILE, LANES), F32)],
            in_specs=[smem] + [vmem] * len(sources) + [pl.BlockSpec(memory_space=pl.ANY)] * 2 + [vmem] * (len(columns) + len(acc)),
            out_specs=[vmem] * (PARTS + 1),
            input_output_aliases={inputs + part: part for part in range(PARTS)} if acc else {},
            scratch_shapes=[
                pltpu.SMEM((len(sources), TILE, LANES), F32),
                pltpu.VMEM(matrices.shape[1:], BF16),
                pltpu.VMEM(phases.shape[1:], F32),
                spectra,
                spectra,
                pltpu.SemaphoreType.DMA((len(sources) + 2,)),
            ],
            compiler_params=params,
            cost_estimate=pl.CostEstimate(flops=0, bytes_accessed=len(sources) << 23, transcendentals=0),
            name="tiles",
        )(places, *[array for _, array in sources], *in_hbm([matrices, phases, *columns]), *in_vmem(acc))
        return acc, token

    def after(value, token):
        return lax.optimization_barrier((value, token))[0]

    def across(value, holders):
        return [(holders, send(value, [(z, z) for z in holders], wide)) for wide in range(1, along)]

    every = range(Z_CHIPS)
    passed = {1: tiles, -1: tiles}
    arrived, waiting, token, acc = [(every, tiles)], [], None, []
    for steps in range(1, Z_CHIPS + 1):
        ready, waiting = (waiting, []) if steps == Z_CHIPS else (waiting[:-1], waiting[-1:])
        partners = []
        for holders, array in arrived:
            partners += across(array if token is None else after(array, token), holders)
        moved = []
        if steps < Z_CHIPS:
            for way in (1, -1):
                moves = [(z, z + way) for z in every if 0 <= z + way < Z_CHIPS and 0 <= z - way * (steps - 1) < Z_CHIPS]
                value = passed[way] if token is None else after(passed[way], token)
                passed[way] = send(value, moves, 0)
                moved.append(([to for _, to in moves], passed[way]))
        acc, token = add_tiles(arrived + [pair for pairs in ready for pair in pairs], acc)
        arrived = moved
        waiting.append(partners)
    acc, _ = add_tiles(waiting[-1], acc, [column])

    row_table = jnp.asarray(row_tables())
    part_shape = (3, 2 * planes_padded, LANES)

    def rows_for(relative, first, count, addends, after):
        def body(*refs):
            operands = 2 + PARTS + len(addends)
            rows_kernel(
                relative, first, count, chunks, grid_rows, len(addends), planes_padded, *refs[:operands], refs[-1]
            )

        return pl.pallas_call(
            body,
            in_specs=[smem] + [vmem] * (1 + PARTS + len(addends)) + [pl.BlockSpec(memory_space=pl.ANY)] * len(after),
            out_specs=vmem,
            out_shape=jax.ShapeDtypeStruct((count * slots,) + part_shape, F32),
            compiler_params=params,
            cost_estimate=pl.CostEstimate(flops=1, bytes_accessed=1, transcendentals=0),
            name="rows",
        )(places, *in_vmem(acc), row_table, *addends, *after)

    def swap(value, bit):
        return lax.ppermute(value, "gx", [(index, index ^ bit) for index in range(grid_rows)])

    last = []

    def rows_next(relative, first, count, addends):
        part = rows_for(relative, first, count, addends, last)
        last[:] = [part]
        return part

    def arrivals(relative, top):
        arrived = []
        bit = 1
        while bit <= top:
            arrived.append(swap(rows_next(relative | bit, 0, chunks, arrivals(relative | bit, bit // 2)), bit))
            bit *= 2
        return arrived

    top = grid_rows // 2
    far = arrivals(top, top // 2)
    near, crossed = [], []
    for chunk in range(chunks):
        if top == 2:
            near.append([(swap(rows_next(1, chunk, 1, []), 1), 0)])
        elif chunk == 0:
            arrived = arrivals(0, top // 2)
            near += [[(array, place) for array in arrived] for place in range(chunks)]
        crossed.append(swap(rows_next(top, chunk, 1, far), top))
    kept = rows_next(0, 0, chunks, [])
    parts = [[(kept, chunk), *near[chunk], (crossed[chunk], 0)] for chunk in range(chunks)]

    image = None
    for chunk in range(chunks):

        def finish(*refs, chunk=chunk):
            finish_kernel(chunk, planes_padded, len(parts[chunk]), refs)

        earlier = [] if image is None else [image]
        image = pl.pallas_call(
            finish,
            grid=(1,),
            out_shape=jax.ShapeDtypeStruct((2, planes, per_device, NX // 2), F32),
            in_specs=[
                pl.BlockSpec((slots,) + part_shape, lambda step, place=place: (place, 0, 0, 0))
                for _, place in parts[chunk]
            ]
            + [
                pl.BlockSpec((4 * LANES, NX // 2), lambda step: (0, 0)),
                pl.BlockSpec((1, NX // 2), lambda step: (0, 0)),
                pl.BlockSpec((1, per_device), lambda step: (0, 0)),
                pl.BlockSpec(memory_space=pltpu.SMEM),
            ]
            + [pl.BlockSpec(memory_space=pl.ANY)] * len(earlier),
            out_specs=pl.BlockSpec((2, planes, CHUNK, NX // 2), lambda step, chunk=chunk: (0, 0, chunk, 0)),
            input_output_aliases={len(parts[chunk]) + 4: 0} if earlier else {},
            compiler_params=params,
            name="finish",
        )(
            *[array for array, _ in parts[chunk]],
            jnp.asarray(order_tables()),
            deapod_first[None, :],
            deapod_second[None, :],
            deapod_third,
            *earlier,
        )
    return image


def solution(mesh):
    in_specs = (
        P(("gx", "gy"), None, None),
        P(("gx", "gy"), None, None, None),
        P(("gx", "gy"), None, None),
        P(("gx", "gy"), None),
        P(("gx", "gy")),
        P(),
        P("gx"),
        P("gy"),
    )
    out_specs = P(None, "gy", "gx", None)
    return jax.shard_map(
        on_device, mesh=mesh, in_specs=in_specs, out_specs=out_specs, check_vma=False
    )
```

```python
import functools
import math

import jax
import jax.numpy as jnp
import ml_dtypes
import numpy as np
from jax import lax
from jax.experimental import pallas as pl
from jax.experimental.pallas import tpu as pltpu
from jax.sharding import PartitionSpec as P

NX = 384
NY = 384
NZ = 384
TILE = 8
LANES = 128
PLANES = 32
CHUNK = 24
Z_CHIPS = 4
PARTS = 4
CELLS = TILE // PARTS
STRIDE = NY + TILE
PHASES = 128
BF16 = jnp.bfloat16
F32 = jnp.float32
VMEM_LIMIT = 8 * 1024 * 1024


def halves(array):
    high = array.astype(ml_dtypes.bfloat16)
    low = (array - high.astype(np.float64)).astype(ml_dtypes.bfloat16)
    return high, low


def split(value):
    high = value.astype(BF16)
    return high, (value - high.astype(F32)).astype(BF16)


def waves(freq, position, length):
    steps = np.mod(freq[:, None] * position[None, :], length)
    phase = 2.0 * math.pi * steps / length
    return np.cos(phase), np.sin(phase)


def depth_tables(planes):
    matrices, phases = [], []
    lane_part = np.arange(LANES) // 64
    lane_odd = np.arange(LANES) // 32 % 2
    lane_plane = np.arange(LANES) % 32
    used = (lane_plane < planes).astype(np.float64)
    for index in range(NZ // 2 // planes):
        position = index * planes + lane_plane - NZ // 4
        cos, sin = waves(np.arange(TILE) - NZ // 2, position, NZ)
        cos, sin = cos * used / math.sqrt(NZ), sin * used / math.sqrt(NZ)
        real = np.where(lane_part == 0, cos, sin)
        imag = np.where(lane_part == 0, -sin, cos)
        high, low = halves(np.concatenate((real, imag)))
        matrices.append(np.concatenate((high, high, low)))
        cos, sin = waves(np.arange(NZ // TILE), position, NZ // TILE)
        sign = np.where(lane_odd == 1, -1.0, 1.0)[None, :]
        sin = sin * np.where(lane_part == 0, -1.0, 1.0)[None, :]
        phases.append(np.stack((np.concatenate((cos, cos * sign)), np.concatenate((sin, sin * sign)))))
    return np.stack(matrices), np.stack(phases).astype(np.float32)


def column_tables():
    third = NY // 3
    out = []
    for residue in range(3):
        cos, sin = waves(3 * np.arange(NY // 6) + residue - NY // 4, np.arange(third) - NY // 2, NY)
        high, low = halves(np.concatenate((cos, sin)) / math.sqrt(NY))
        out.append(np.block([[high, high], [low, np.zeros_like(low)]]))
    return np.stack(out)


def row_tables():
    half = NX // 2
    freq = np.arange(half).reshape(-1, PARTS, CELLS).transpose(1, 0, 2).reshape(-1) - half
    quarter = NX // 4
    out = []
    for parity in range(2):
        position = 2 * np.arange(quarter) + parity - NX // 4
        cos, sin = waves(freq, position, NX)
        table = np.zeros((half, 2 * LANES))
        lanes = (np.arange(quarter) + parity * quarter) % LANES
        table[:, lanes] = cos / math.sqrt(NX)
        table[:, LANES + lanes] = sin / math.sqrt(NX)
        out.append(np.stack(halves(table)))
    return np.stack(out)


def order_tables():
    first = np.zeros((LANES, NX // 2))
    second = np.zeros((LANES, NX // 2))
    quarter = NX // 4
    for m1 in range(NX // 2):
        place = m1 // 2 + m1 % 2 * quarter
        if place < LANES:
            first[place, m1] = 1.0
        else:
            second[place - LANES, m1] = 1.0
    return np.concatenate((first, first, second, second)).astype(ml_dtypes.bfloat16)


def divide(value, divisor, limit):
    for shift in range(8, 24):
        factor = (1 << shift) // divisor + 1
        tried = np.arange(limit, dtype=np.int64)
        if factor * limit < 1 << 31 and np.array_equal(tried * factor >> shift, tried // divisor):
            return lax.shift_right_logical(value * factor, shift)
    raise ValueError(divisor)


def spread_kernel(tile_rows, tile_cols, grid_cols, devices, samples_ref, kernel_ref, offsets_ref, owners_ref, ids_ref, out_ref):
    owner, tile_id = owners_ref[...], ids_ref[...]
    tile_depth = NZ // TILE
    tiles_device = tile_rows * tile_cols * tile_depth
    owner_row = divide(owner, grid_cols, devices)
    tile_row = divide(tile_id, tile_cols * tile_depth, tiles_device)
    tile_col = divide(tile_id, tile_depth, tiles_device)
    row = owner_row * tile_rows + tile_row
    col = (owner - owner_row * grid_cols) * tile_cols + tile_col - tile_row * tile_cols
    folds = NX // TILE // 2
    upper = (row >= folds).astype(jnp.int32)
    base = (row - upper * folds) * (CELLS * STRIDE // TILE) + col
    phase = tile_id - tile_col * tile_depth + upper * tile_depth
    codes = (base * PHASES + phase).astype(F32)

    blocks = samples_ref.shape[0]
    taps = kernel_ref.shape[2]
    cell = lax.broadcasted_iota(jnp.int32, (TILE, LANES), 0)
    left = lax.broadcasted_iota(jnp.int32, (2 * TILE, LANES), 1) < LANES // 2

    def weights(block):
        placed = []
        for dim in range(3):
            shifted = cell - offsets_ref[dim, pl.ds(block, 1), :]
            value = jnp.zeros((TILE, LANES), F32)
            for tap in range(taps):
                value = jnp.where(shifted == tap, kernel_ref[block, dim, pl.ds(tap, 1), :], value)
            placed.append(value)
        plane = jnp.concatenate([placed[0][i : i + 1] * placed[1] for i in range(TILE)], axis=0)
        depth = jnp.concatenate([samples_ref[block, pl.ds(c, 1), :] * placed[2] for c in range(2)], axis=0)
        return depth, plane

    def pair_body(pair, carry):
        depth_a, plane_a = weights(2 * pair)
        depth_b, plane_b = weights(2 * pair + 1)
        depth_high, depth_low = split(jnp.concatenate((depth_a, depth_b), axis=0))
        plane_high, plane_low = split(jnp.concatenate((plane_a, plane_b), axis=0))
        piece = lax.dot_general(
            jnp.concatenate((depth_high, depth_low, depth_high), axis=1),
            jnp.concatenate((plane_high, plane_high, plane_low), axis=1),
            (((1,), (1,)), ((), ())),
            preferred_element_type=F32,
        )
        out_ref[pair] = jnp.where(left, piece[: 2 * TILE], piece[2 * TILE :])
        return carry

    lax.fori_loop(0, blocks // 2, pair_body, 0, unroll=16)
    out_ref[blocks // 2] = jnp.broadcast_to(codes, (2 * TILE, LANES))


def tiles_kernel(conditions, first, last, *refs):
    arrays = len(conditions)
    places_ref = refs[0]
    source_refs = refs[1 : 1 + arrays]
    depth_tables_ref, phase_tables_ref = refs[1 + arrays : 3 + arrays]
    acc_refs = refs[-7 - PARTS : -7]
    token_ref, codes_ref, depth_ref, phases_ref, even_ref, odd_ref, arrived = refs[-7:]
    token_ref[...] = jnp.zeros_like(token_ref)
    stride = STRIDE
    pairs = source_refs[0].shape[0] - 1
    batch = 8
    batches = pairs // batch
    assert batches % 2 == 0

    def copies(index):
        return pltpu.make_async_copy(
            source_refs[index].at[pairs, pl.ds(0, TILE)], codes_ref.at[index], arrived.at[index]
        )

    tables = [
        pltpu.make_async_copy(depth_tables_ref.at[places_ref[2]], depth_ref, arrived.at[arrays]),
        pltpu.make_async_copy(phase_tables_ref.at[places_ref[2]], phases_ref, arrived.at[arrays + 1]),
    ]
    for index in range(arrays):
        copies(index).start()
    for table in tables:
        table.start()

    if first:

        def clear(step, carry):
            at = pl.ds(pl.multiple_of(step * stride, stride), stride)
            for ref in acc_refs:
                ref[at, :] = jnp.zeros((stride, LANES), F32)
            return carry

        lax.fori_loop(0, NX // 2 // PARTS, clear, 0)

    for index in range(arrays):
        copies(index).wait()
    for table in tables:
        table.wait()

    def add_source(index):
        tiles_ref = source_refs[index]

        def spectrum(number, to_ref):
            tiles = jnp.concatenate([tiles_ref[number * batch + place] for place in range(batch)], axis=1)
            high, low = split(tiles)
            to_ref[...] = lax.dot_general(
                jnp.concatenate((high, low, high), axis=0),
                depth_ref[...],
                (((0,), (0,)), ((), ())),
                preferred_element_type=F32,
            )

        def accumulate(number, from_ref):
            for tile in range(2 * batch):
                code = codes_ref[index, 0, number * 2 * batch + tile].astype(jnp.int32)
                base = lax.shift_right_logical(code, 7)
                phase = jnp.bitwise_and(code, PHASES - 1)
                cos = phases_ref[0, pl.ds(phase, 1), :]
                sin = phases_ref[1, pl.ds(phase, 1), :]
                for i in range(TILE):
                    row = tile * TILE * TILE + i * TILE
                    value = from_ref[row : row + TILE, :]
                    value = value * cos + pltpu.roll(value, LANES // 2, 1) * sin
                    acc_ref = acc_refs[i // CELLS]
                    at = pl.ds(pl.multiple_of(base * TILE + i % CELLS * stride, TILE), TILE)
                    acc_ref[at, :] = acc_ref[at, :] + value

        spectrum(0, even_ref)

        def add_pair(step, carry):
            number = 2 * step
            spectrum(number + 1, odd_ref)
            accumulate(number, even_ref)
            spectrum(jnp.minimum(number + 2, batches - 2), even_ref)
            accumulate(number + 1, odd_ref)
            return carry

        lax.fori_loop(0, batches // 2, add_pair, 0, unroll=2)

    for index, condition in enumerate(conditions):
        if condition is None:
            add_source(index)
        else:
            holds = places_ref[0] == condition[0]
            for depth in condition[1:]:
                holds = jnp.logical_or(holds, places_ref[0] == depth)
            pl.when(holds)(functools.partial(add_source, index))

    if last:
        transform_columns(refs[3 + arrays], acc_refs)


def transform_columns(column_ref, acc_refs):
    third = NY // 3
    rows = column_ref.shape[1] // 4
    turn = jnp.where(lax.broadcasted_iota(jnp.int32, (1, LANES), 1) < LANES // 2, -1.0, 1.0)

    def columns(step, carry):
        start = pl.multiple_of(step * STRIDE, TILE)
        for pair in range(0, PARTS, 2):
            folded = ([], [], [])
            for ref in acc_refs[pair : pair + 2]:
                first, second, last = (ref[pl.ds(start + third * part, third), :] for part in range(3))
                both = second + last
                across = pltpu.roll(second - last, LANES // 2, 1) * (turn * math.sqrt(0.75))
                middle = first - 0.5 * both
                folded[0].append(first + both)
                folded[1].append(middle + across)
                folded[2].append(middle - across)
            for residue in range(3):
                high, low = split(jnp.concatenate(folded[residue], axis=1))
                product = jnp.dot(
                    column_ref[residue], jnp.concatenate((high, low), axis=0), preferred_element_type=F32
                )
                product = product[: 2 * rows] + product[2 * rows :]
                for side, ref in enumerate(acc_refs[pair : pair + 2]):
                    lanes = slice(side * LANES, (side + 1) * LANES)
                    ref[pl.ds(start + residue * rows, rows), :] = (
                        product[:rows, lanes] + pltpu.roll(product[rows:, lanes], LANES // 2, 1) * turn
                    )
        return carry

    lax.fori_loop(0, NX // 2 // PARTS, columns, 0, unroll=16)


def rows_kernel(relative, first, count, chunks, grid_rows, addends, planes_padded, places_ref, *refs):
    acc_refs, row_ref, addend_refs, out_ref = refs[:PARTS], refs[PARTS], refs[PARTS + 1 : -1], refs[-1]
    assert len(addend_refs) == addends
    rows = grid_rows * chunks * TILE
    device = jnp.bitwise_xor(places_ref[1], relative)
    lane = lax.broadcasted_iota(jnp.int32, (PLANES, LANES), 1)

    def block(step, carry):
        chunk, residue = step // 3, step % 3
        start = residue * rows + (device * chunks + first + chunk) * TILE
        turned = []
        for row in range(TILE):
            at = pl.ds(start + row, NX // 2 // PARTS, stride=STRIDE)
            turned.append(jnp.concatenate([ref[at, :] for ref in acc_refs], axis=0).T)
        parts = []
        for odd in range(2):
            at = odd * PLANES
            stacked = [value[part * 64 + at : part * 64 + at + PLANES] for value in turned for part in range(2)]
            high, low = split(jnp.concatenate(stacked, axis=0))
            size = high.shape[0]
            both = jnp.dot(jnp.concatenate((high, low), axis=0), row_ref[odd, 0], preferred_element_type=F32)
            product = both[:size] + both[size:] + jnp.dot(high, row_ref[odd, 1], preferred_element_type=F32)
            sides = []
            for row in range(TILE):
                real = product[2 * row * PLANES : (2 * row + 1) * PLANES]
                imag = product[(2 * row + 1) * PLANES : (2 * row + 2) * PLANES]
                sides.append((real[:, :LANES] - imag[:, LANES:], real[:, LANES:] + imag[:, :LANES]))
            parts.append(sides)
        for slot in range(TILE // 2):
            place = chunk * (CHUNK // 2) + 3 * slot + residue
            for part in range(2):
                even = [parts[0][slot + side * TILE // 2][part] for side in range(2)]
                odd = [parts[1][slot + side * TILE // 2][part] for side in range(2)]
                values = [jnp.where(lane < NX // 4, even[side], odd[side]) for side in range(2)]
                values.append(jnp.where(lane < LANES // 2, odd[0], pltpu.roll(odd[1], LANES // 2, 1)))
                for number, value in enumerate(values):
                    planes = pl.ds(part * planes_padded, planes_padded)
                    total = value[:planes_padded]
                    for ref in addend_refs:
                        shift = first * (CHUNK // 2) if ref.shape[0] > out_ref.shape[0] else 0
                        total = total + ref[shift + place, number, planes]
                    out_ref[place, number, planes] = total
        return carry

    lax.fori_loop(0, 3 * count, block, 0, unroll=3)


def finish_kernel(chunk, planes_padded, parts, refs):
    part_refs = refs[:parts]
    order_ref, first_ref, second_ref, third_ref = refs[parts : parts + 4]
    out_ref = refs[-1]
    planes = out_ref.shape[1]
    slots = part_refs[0].shape[0]
    stride = 6 * planes_padded
    flats = [ref.reshape(slots * stride, LANES) for ref in part_refs]
    order = order_ref[...]
    shape = (CHUNK, second_ref.shape[1])
    here = lax.broadcasted_iota(jnp.int32, shape, 1) == lax.broadcasted_iota(jnp.int32, shape, 0) + chunk * CHUNK
    second = jnp.sum(jnp.where(here, second_ref[...], 0.0), axis=1, keepdims=True)
    scale = second * first_ref[...]
    for part in range(2):
        for group in range(0, planes, TILE):
            members = range(group, min(group + TILE, planes))
            mains, rests = [], []
            for plane in members:
                values = []
                for number in range(3):
                    at = pl.ds((number * 2 + part) * planes_padded + plane, slots, stride=stride)
                    total = flats[0][at, :]
                    for flat in flats[1:]:
                        total = total + flat[at, :]
                    values.append(total)
                mains.append(jnp.concatenate(values[:2], axis=0))
                rests.append(jnp.concatenate((values[2], pltpu.roll(values[2], LANES // 2, 1)), axis=0))
            main = split(jnp.concatenate(mains, axis=0))
            rest = split(jnp.concatenate(rests, axis=0))
            ordered = jnp.dot(jnp.concatenate(main + rest, axis=1), order, preferred_element_type=F32)
            for index, plane in enumerate(members):
                out_ref[part, plane] = ordered[index * 2 * slots : (index + 1) * 2 * slots] * (scale * third_ref[plane])


def on_device(samples, kernel, offsets, owners, tile_ids, deapod_first, deapod_second, deapod_third):
    grid_rows = lax.axis_size("gx")
    grid_cols = lax.axis_size("gy")
    blocks = samples.shape[0]
    block_width = samples.shape[2]
    assert block_width == LANES and blocks == LANES
    tile_rows = NX // (TILE * grid_rows)
    tile_cols = NY // (TILE * grid_cols)
    planes = deapod_third.shape[0]
    per_device = deapod_second.shape[0]
    assert per_device % CHUNK == 0
    chunks = per_device // CHUNK
    slots = CHUNK // 2
    planes_padded = -(-planes // 8) * 8
    vmem = pl.BlockSpec(memory_space=pltpu.VMEM)
    params = pltpu.CompilerParams(vmem_limit_bytes=VMEM_LIMIT)

    def in_hbm(arrays):
        return [pltpu.with_memory_space_constraint(array, pltpu.HBM) for array in arrays]

    tiles = pl.pallas_call(
        functools.partial(spread_kernel, tile_rows, tile_cols, grid_cols, grid_rows * grid_cols),
        out_shape=pltpu.HBM((blocks // 2 + 1, 2 * TILE, LANES), F32),
        in_specs=[vmem] * 5,
        out_specs=vmem,
        compiler_params=params,
        name="spread",
    )(*in_hbm([samples, kernel, offsets.transpose(1, 0, 2), owners.reshape(1, blocks), tile_ids.reshape(1, blocks)]))

    along = grid_cols // Z_CHIPS
    deep_at = lax.div(lax.axis_index("gy").astype(jnp.int32), jnp.int32(along))

    def send(value, moves_z, wide):
        moves = [(a * along + y, b * along + (y + wide) % along) for a, b in moves_z for y in range(along)]
        return lax.ppermute(value, "gy", moves)

    places = jnp.stack((deep_at, lax.axis_index("gx").astype(jnp.int32), lax.axis_index("gy").astype(jnp.int32)))
    matrices, phases = (jnp.asarray(table) for table in depth_tables(planes))
    column = jnp.asarray(column_tables())
    half = NX // 2
    smem = pl.BlockSpec(memory_space=pltpu.SMEM)
    acc_shape = (half // PARTS * STRIDE, LANES)

    def in_vmem(arrays):
        return [pltpu.with_memory_space_constraint(array, pltpu.VMEM) for array in arrays]

    def add_tiles(sources, acc, columns=()):
        conditions = [None if len(holders) == Z_CHIPS else tuple(holders) for holders, _ in sources]
        spectra = pltpu.VMEM((16 * TILE * TILE, LANES), F32)
        kept = [jax.ShapeDtypeStruct(acc_shape, F32) if acc else pltpu.VMEM(acc_shape, F32)] * PARTS
        inputs = len(sources) + 3 + len(columns)
        *acc, token = pl.pallas_call(
            functools.partial(tiles_kernel, conditions, not acc, bool(columns)),
            out_shape=kept + [jax.ShapeDtypeStruct((TILE, LANES), F32)],
            in_specs=[smem] + [vmem] * len(sources) + [pl.BlockSpec(memory_space=pl.ANY)] * 2 + [vmem] * (len(columns) + len(acc)),
            out_specs=[vmem] * (PARTS + 1),
            input_output_aliases={inputs + part: part for part in range(PARTS)} if acc else {},
            scratch_shapes=[
                pltpu.SMEM((len(sources), TILE, LANES), F32),
                pltpu.VMEM(matrices.shape[1:], BF16),
                pltpu.VMEM(phases.shape[1:], F32),
                spectra,
                spectra,
                pltpu.SemaphoreType.DMA((len(sources) + 2,)),
            ],
            compiler_params=params,
            cost_estimate=pl.CostEstimate(flops=0, bytes_accessed=len(sources) << 23, transcendentals=0),
            name="tiles",
        )(places, *[array for _, array in sources], *in_hbm([matrices, phases, *columns]), *in_vmem(acc))
        return acc, token

    def after(value, token):
        return lax.optimization_barrier((value, token))[0]

    def across(value, holders):
        return [(holders, send(value, [(z, z) for z in holders], wide)) for wide in range(1, along)]

    every = range(Z_CHIPS)
    passed = {1: tiles, -1: tiles}
    arrived, token, acc = [(every, tiles)], None, []
    for steps in range(1, Z_CHIPS + 1):
        partners = []
        if steps == 1:
            partners += across(tiles, every)
        else:
            partners += [held for holders, array in arrived[:2] for held in across(after(array, token), holders)]
        moved = []
        if steps < Z_CHIPS:
            for way in (1, -1):
                moves = [(z, z + way) for z in every if 0 <= z + way < Z_CHIPS and 0 <= z - way * (steps - 1) < Z_CHIPS]
                value = passed[way] if token is None else after(passed[way], token)
                passed[way] = send(value, moves, 0)
                moved.append(([to for _, to in moves], passed[way]))
        acc, token = add_tiles(arrived, acc)
        arrived = moved + partners
    acc, _ = add_tiles(arrived, acc, [column])

    row_table = jnp.asarray(row_tables())
    part_shape = (3, 2 * planes_padded, LANES)

    def rows_for(relative, first, count, addends, after):
        def body(*refs):
            operands = 2 + PARTS + len(addends)
            rows_kernel(
                relative, first, count, chunks, grid_rows, len(addends), planes_padded, *refs[:operands], refs[-1]
            )

        return pl.pallas_call(
            body,
            in_specs=[smem] + [vmem] * (1 + PARTS + len(addends)) + [pl.BlockSpec(memory_space=pl.ANY)] * len(after),
            out_specs=vmem,
            out_shape=jax.ShapeDtypeStruct((count * slots,) + part_shape, F32),
            compiler_params=params,
            cost_estimate=pl.CostEstimate(flops=1, bytes_accessed=1, transcendentals=0),
            name="rows",
        )(places, *in_vmem(acc), row_table, *addends, *after)

    def swap(value, bit):
        return lax.ppermute(value, "gx", [(index, index ^ bit) for index in range(grid_rows)])

    last = []

    def rows_next(relative, first, count, addends):
        part = rows_for(relative, first, count, addends, last)
        last[:] = [part]
        return part

    def arrivals(relative, top):
        arrived = []
        bit = 1
        while bit <= top:
            arrived.append(swap(rows_next(relative | bit, 0, chunks, arrivals(relative | bit, bit // 2)), bit))
            bit *= 2
        return arrived

    top = grid_rows // 2
    far = arrivals(top, top // 2)
    near, crossed = [], []
    for chunk in range(chunks):
        if top == 2:
            near.append([(swap(rows_next(1, chunk, 1, []), 1), 0)])
        elif chunk == 0:
            arrived = arrivals(0, top // 2)
            near += [[(array, place) for array in arrived] for place in range(chunks)]
        crossed.append(swap(rows_next(top, chunk, 1, far), top))
    kept = rows_next(0, 0, chunks, [])
    parts = [[(kept, chunk), *near[chunk], (crossed[chunk], 0)] for chunk in range(chunks)]

    image = None
    for chunk in range(chunks):

        def finish(*refs, chunk=chunk):
            finish_kernel(chunk, planes_padded, len(parts[chunk]), refs)

        earlier = [] if image is None else [image]
        image = pl.pallas_call(
            finish,
            grid=(1,),
            out_shape=jax.ShapeDtypeStruct((2, planes, per_device, NX // 2), F32),
            in_specs=[
                pl.BlockSpec((slots,) + part_shape, lambda step, place=place: (place, 0, 0, 0))
                for _, place in parts[chunk]
            ]
            + [
                pl.BlockSpec((4 * LANES, NX // 2), lambda step: (0, 0)),
                pl.BlockSpec((1, NX // 2), lambda step: (0, 0)),
                pl.BlockSpec((1, per_device), lambda step: (0, 0)),
                pl.BlockSpec(memory_space=pltpu.SMEM),
            ]
            + [pl.BlockSpec(memory_space=pl.ANY)] * len(earlier),
            out_specs=pl.BlockSpec((2, planes, CHUNK, NX // 2), lambda step, chunk=chunk: (0, 0, chunk, 0)),
            input_output_aliases={len(parts[chunk]) + 4: 0} if earlier else {},
            compiler_params=params,
            name="finish",
        )(
            *[array for array, _ in parts[chunk]],
            jnp.asarray(order_tables()),
            deapod_first[None, :],
            deapod_second[None, :],
            deapod_third,
            *earlier,
        )
    return image


def solution(mesh):
    in_specs = (
        P(("gx", "gy"), None, None),
        P(("gx", "gy"), None, None, None),
        P(("gx", "gy"), None, None),
        P(("gx", "gy"), None),
        P(("gx", "gy")),
        P(),
        P("gx"),
        P("gy"),
    )
    out_specs = P(None, "gy", "gx", None)
    return jax.shard_map(
        on_device, mesh=mesh, in_specs=in_specs, out_specs=out_specs, check_vma=False
    )
```
